32 devices in a mesh: fsdp: 8 (over y, x, core), dp: 4 (over z).
Axes of the slice: x: 2, y: 2, z: 4, core: 2. Of those that a mesh axis runs over, the one named last changes fastest.
Arguments:
- inputs: bfloat16 [32768, 768], P(('fsdp', 'dp')), may hold values from -6 to 6
- time_of_row: float32 [32768], P(('fsdp', 'dp')), may hold values from 0 to 1
- coords: float32 [3, 32768], P(None, ('fsdp', 'dp')), may hold values from -8 to 8
- segment_ids: int32 [32768], P(('fsdp', 'dp')), may hold values from 0 to 2047, never falling along the last dimension, each value on 1 to 48 neighbouring positions
- cotangent: bfloat16 [32768, 768], P(('fsdp', 'dp')), may hold values from -6 to 6
- time_weight: bfloat16 [768], P('fsdp'), may hold values from -5 to 5
- ln1_gain: bfloat16 [768], P('fsdp'), may hold values from 0.5 to 1.5
- ln1_bias: bfloat16 [768], P('fsdp'), may hold values from -1.5 to 1.5
- w_qkv: bfloat16 [768, 2304], P('fsdp'), may hold values from -0.21875 to 0.21875
- q_bias: bfloat16 [768], P('fsdp'), may hold values from -2.5 to 2.5
- v_bias: bfloat16 [768], P('fsdp'), may hold values from -1.5 to 1.5
- w_out: bfloat16 [768, 768], P('fsdp'), may hold values from -0.875 to 0.875
- out_bias: bfloat16 [768], P('fsdp'), may hold values from -1.5 to 1.5
- kernel_mean: bfloat16 [128], P('fsdp'), may hold values from 0 to 8
- kernel_width: bfloat16 [128], P('fsdp'), may hold values from 0.5 to 3
- kernel_map: bfloat16 [128, 32], P('fsdp'), may hold values from -2 to 2
- ln2_gain: bfloat16 [768], P('fsdp'), may hold values from 0.5 to 1.5
- ln2_bias: bfloat16 [768], P('fsdp'), may hold values from -1.5 to 1.5
- w_up: bfloat16 [768, 3072], P('fsdp'), may hold values from -0.21875 to 0.21875
- up_bias: bfloat16 [3072], P('fsdp'), may hold values from -1.5 to 1.5
- w_down: bfloat16 [3072, 768], P('fsdp'), may hold values from -0.109375 to 0.109375
- down_bias: bfloat16 [768], P('fsdp'), may hold values from -1.5 to 1.5
Outputs:
- output: bfloat16 [32768, 768], P(('fsdp', 'dp'))
- grad_inputs: bfloat16 [32768, 768], P(('fsdp', 'dp'))
- grad_time_weight: float32 [768], P('fsdp')
- grad_ln1_gain: float32 [768], P('fsdp')
- grad_ln1_bias: float32 [768], P('fsdp')
- grad_w_qkv: float32 [768, 2304], P('fsdp')
- grad_q_bias: float32 [768], P('fsdp')
- grad_v_bias: float32 [768], P('fsdp')
- grad_w_out: float32 [768, 768], P('fsdp')
- grad_out_bias: float32 [768], P('fsdp')
- grad_kernel_mean: float32 [128], P('fsdp')
- grad_kernel_width: float32 [128], P('fsdp')
- grad_kernel_map: float32 [128, 32], P('fsdp')
- grad_ln2_gain: float32 [768], P('fsdp')
- grad_ln2_bias: float32 [768], P('fsdp')
- grad_w_up: float32 [768, 3072], P('fsdp')
- grad_up_bias: float32 [3072], P('fsdp')
- grad_w_down: float32 [3072, 768], P('fsdp')
- grad_down_bias: float32 [768], P('fsdp')
The draws below stay inside these ranges and needn't reach their ends.
Inputs may be any that keep to these rules, and one draw needn't show every extreme that they name: segment_ids never falls along the rows; each id covers 1 to 48 consecutive rows and some id exactly 48.
All inputs are finite; a program needn't handle non-finite values.
Results may differ from the reference program's by a relative error of at most 0.017.
Values may be sent and summed in bfloat16 or wider, within the bound.
No kernel may reach another device: no remote copies, remote signals or barrier semaphores. Data moves between devices by JAX's collectives and lax.ppermute only.
A program may use at most 192 MiB of HBM per device.

```python
import math
import jax
import jax.numpy as jnp
import numpy as np
from jax import lax

D = 768
HEADS = 32
HEAD_DIM = 24
FF = 3072
KERNELS = 128
SET = 256
ROWS = 32768


def raised(values, stream_key, source, target, blocks, factor):
    def block_of(position):
        return (jnp.arange(values.shape[position]) // (values.shape[position] // blocks)).reshape((-1,) + (1,) * (values.ndim - 1 - position))

    near = jax.random.permutation(stream_key, blocks)[block_of(target)]
    other_side = (block_of(target) + blocks // 2) % blocks
    return jnp.where((block_of(source) == near) | (block_of(source) == other_side), factor * values, values)


def level_of(rng, extent, cuts, low, high):
    factor_of, own = 1.0, jax.random.fold_in(rng, 6)
    for dim, parts in cuts:
        steps = jnp.exp(jax.random.uniform(jax.random.fold_in(own, dim), (parts,), jnp.float32, low / len(cuts), high / len(cuts)))
        factor_of = factor_of * jnp.repeat(steps, extent[dim] // parts).reshape([-1 if axis == dim else 1 for axis in range(len(extent))])
    return factor_of


def profile(count, total, bound, slope):
    portions = [(1 << 20) // math.isqrt(standing ** slope) + 1 for standing in range(2, count + 1)]
    rest, holding = total - bound - (count - 1), [1] * (count - 1)
    while rest > 0:
        movable = [i for i in range(count - 1) if holding[i] < bound]
        mass, remaining = sum([portions[i] for i in movable]), rest
        for i in movable:
            extra = min(bound - holding[i], max(1, remaining * portions[i] // mass), rest)
            holding[i] = holding[i] + extra
            rest = rest - extra
    return np.array([bound] + holding)


def ragged_sizes(own_key, amount, total, reach, skew):
    if amount == 2:
        one = jax.random.randint(own_key, (), max(1, total - reach), min(reach, total - 1) + 1)
        return jnp.stack([one, total - one])
    tallies = jnp.asarray(profile(amount, total, reach, skew), jnp.int32)
    pairs = (amount - 1) // 2
    donor, taker = tallies[1:1 + 2 * pairs:2], tallies[2:2 + 2 * pairs:2]
    slack = jnp.minimum(donor - 1, reach - taker)
    passed = jax.random.randint(jax.random.fold_in(own_key, 1), (pairs,), 0, 1 << 20) % (slack + 1)
    tallies = tallies.at[1:1 + 2 * pairs:2].set(donor - passed).at[2:2 + 2 * pairs:2].set(taker + passed)
    return tallies[jax.random.permutation(jax.random.fold_in(own_key, 2), amount)]


def gaussian(stream_key, dims, spread, bound, cuts=(), kind=jnp.bfloat16):
    values = jax.random.normal(stream_key, dims, jnp.float32) * spread
    if len(cuts) > 0:
        values = level_of(stream_key, dims, cuts, -0.22, 0.18) * values
    return jnp.clip(values, min=-bound, max=bound).astype(kind)


def noise_with(rng, extent, width, limit, cuts, heavy, kind=jnp.bfloat16):
    values = width * jax.random.normal(rng, extent, jnp.float32)
    if cuts:
        values = values * level_of(rng, extent, cuts, -0.22, 0.18)
    return jnp.clip(raised(values, jax.random.fold_in(rng, 3), *heavy), -limit, limit).astype(kind)


def setup_inputs(seed: int = 0) -> dict:
    key_list = jax.random.split(jax.random.key(seed), 23)
    inputs = noise_with(key_list[0], (ROWS, D), 1.0, 6.0, ((0, 32),), (0, 1, 32, 2.75))
    time_of_row = jnp.clip(1.0 * jax.random.uniform(key_list[1], (ROWS,), jnp.float32) ** level_of(key_list[1], (ROWS,), ((0, 32),), -0.2, 0.2), 0.0, 1.0)
    coords = gaussian(key_list[2], (3, ROWS), 1.5, 8.0, ((1, 32),), jnp.float32)
    segment_ids = jnp.searchsorted(jnp.cumsum(ragged_sizes(key_list[3], ROWS // 16, ROWS, 48, 1)), jnp.arange(ROWS), side="right").astype(jnp.int32)
    cotangent = noise_with(key_list[4], (ROWS, D), 1.0, 6.0, ((0, 32),), (0, 1, 32, 2.75))
    time_weight = gaussian(key_list[5], (D,), 1.0, 5.0, ((0, 8),))
    ln1_gain = jnp.clip(1.0 + 0.1 * jax.random.normal(key_list[6], (D,), jnp.float32), 0.5, 1.5).astype(jnp.bfloat16)
    ln1_bias = gaussian(key_list[7], (D,), 0.3, 1.5, ((0, 8),))
    w_qkv = gaussian(key_list[8], (D, 3 * D), D ** -0.5, 0.21875, ((0, 8),))
    q_bias = gaussian(key_list[9], (D,), 0.5, 2.5, ((0, 8),))
    v_bias = gaussian(key_list[10], (D,), 0.3, 1.5, ((0, 8),))
    w_out = gaussian(key_list[11], (D, D), (D // 16) ** -0.5, 0.875, ((0, 8),))
    out_bias = gaussian(key_list[12], (D,), 0.3, 1.5, ((0, 8),))
    kernel_mean = jnp.clip(8.0 * jax.random.uniform(key_list[13], (KERNELS,), jnp.float32) ** level_of(key_list[13], (KERNELS,), ((0, 8),), -0.2, 0.2), 0.0, 8.0).astype(jnp.bfloat16)
    kernel_width = jnp.clip(jnp.exp(math.log(3.0) - 1.7917595 * jax.random.uniform(key_list[14], (KERNELS,), jnp.float32) ** level_of(key_list[14], (KERNELS,), ((0, 8),), -0.2, 0.2)), 0.5, 3.0).astype(jnp.bfloat16)
    kernel_map = gaussian(key_list[15], (KERNELS, HEADS), (KERNELS // 16) ** -0.5, 2.0, ((0, 8),))
    ln2_gain = jnp.clip(1.0 + 0.1 * jax.random.normal(key_list[16], (D,), jnp.float32), 0.5, 1.5).astype(jnp.bfloat16)
    ln2_bias = gaussian(key_list[17], (D,), 0.3, 1.5, ((0, 8),))
    w_up = gaussian(key_list[18], (D, FF), D ** -0.5, 0.21875, ((0, 8),))
    up_bias = gaussian(key_list[19], (FF,), 0.3, 1.5, ((0, 8),))
    w_down = gaussian(key_list[20], (FF, D), FF ** -0.5, 0.109375, ((0, 8),))
    down_bias = gaussian(key_list[21], (D,), 0.3, 1.5, ((0, 8),))
    return {"inputs": inputs, "time_of_row": time_of_row, "coords": coords, "segment_ids": segment_ids, "cotangent": cotangent, "time_weight": time_weight, "ln1_gain": ln1_gain, "ln1_bias": ln1_bias, "w_qkv": w_qkv, "q_bias": q_bias, "v_bias": v_bias, "w_out": w_out, "out_bias": out_bias, "kernel_mean": kernel_mean, "kernel_width": kernel_width, "kernel_map": kernel_map, "ln2_gain": ln2_gain, "ln2_bias": ln2_bias, "w_up": w_up, "up_bias": up_bias, "w_down": w_down, "down_bias": down_bias}


HIGHEST = lax.Precision.HIGHEST
epsilon = 1e-05
root_tau = math.sqrt(2.0 * math.pi)

@jax.custom_vjp
def low(v):
    return lax.optimization_barrier(v.astype(jnp.bfloat16)).astype(jnp.float32)

@jax.custom_vjp
def low_back(v):
    return v

def low_keep(v):
    return (low(v), None)

def low_pass(kept, grad):
    return (grad,)

def back_keep(v):
    return (v, None)

def back_low(kept, grad):
    return (low(grad),)
low.defvjp(low_keep, low_pass)
low_back.defvjp(back_keep, back_low)

def layer_norm(values_in, gain_vec, shift_vec):
    average = lax.optimization_barrier(jnp.mean(values_in, axis=-1, keepdims=True))
    centred = values_in - average
    variance = lax.optimization_barrier(jnp.mean(centred * centred, axis=-1, keepdims=True))
    return centred * lax.rsqrt(variance + epsilon) * gain_vec + shift_vec

def kernel_terms(coords_group, kernel_mean, kernel_width):
    offsets = coords_group[:, :, :, None] - coords_group[:, :, None, :]
    radius = jnp.sqrt(lax.optimization_barrier(jnp.sum(offsets * offsets, axis=1)))
    standard = (radius[..., None] - kernel_mean) / kernel_width
    return jnp.exp(-0.5 * standard * standard) / (root_tau * kernel_width)

def group_attention(queries, keys_set, values, coords_group, segs_group, kernel_mean, kernel_width, kernel_map):
    features = low(kernel_terms(coords_group, kernel_mean, kernel_width))
    pair_bias = jnp.einsum('gijk,kh->ghij', features, kernel_map, precision=HIGHEST)
    scores = jnp.einsum('gihe,gjhe->ghij', queries, keys_set, precision=HIGHEST) + pair_bias
    scores = low_back(scores)
    joined = segs_group[:, :, None] == segs_group[:, None, :]
    scores = jnp.where(joined[:, None], scores, -1e+30)
    probs = jax.nn.softmax(scores, axis=-1)
    return jnp.einsum('ghij,gjhe->gihe', low(probs), values, precision=HIGHEST)

def layer_forward(weights, time_of_row, coords, segment_ids):
    inputs, time_weight, ln1_gain, ln1_bias, w_qkv, q_bias, v_bias, w_out, out_bias, kernel_mean, kernel_width, kernel_map, ln2_gain, ln2_bias, w_up, up_bias, w_down, down_bias = weights
    start = inputs + time_of_row[:, None] * time_weight
    normed = low(layer_norm(start, ln1_gain, ln1_bias))
    projected = jnp.dot(normed, w_qkv, precision=HIGHEST)
    queries = low(low_back(projected[:, :D] + q_bias) * HEAD_DIM ** (-0.5))
    keys_all = low(low_back(projected[:, D:2 * D]))
    values = low(low_back(projected[:, 2 * D:] + v_bias))
    sets_all = ROWS // SET
    per_group = math.gcd(sets_all, 4)
    group_count = sets_all // per_group

    def split_heads(array):
        return array.reshape(group_count, per_group, SET, HEADS, HEAD_DIM)
    coords_groups = jnp.transpose(coords.reshape(3, group_count, per_group, SET), (1, 2, 0, 3))
    segs_groups = segment_ids.reshape(group_count, per_group, SET)

    def one_group(pieces):
        return group_attention(pieces[0], pieces[1], pieces[2], pieces[3], pieces[4], kernel_mean, kernel_width, kernel_map)
    attended = lax.map(jax.checkpoint(one_group), (split_heads(queries), split_heads(keys_all), split_heads(values), coords_groups, segs_groups))
    attended = low(low_back(attended.reshape(ROWS, D)))
    attn_branch = low_back(jnp.dot(attended, w_out, precision=HIGHEST) + out_bias)
    middle = start + attn_branch
    normed2 = low(layer_norm(middle, ln2_gain, ln2_bias))
    pre_hidden = low_back(jnp.dot(normed2, w_up, precision=HIGHEST) + up_bias)
    hidden = low(jax.nn.gelu(pre_hidden, approximate=False))
    branch = low_back(jnp.dot(hidden, w_down, precision=HIGHEST) + down_bias)
    return middle + branch

def reference(inputs, time_of_row, coords, segment_ids, cotangent, time_weight, ln1_gain, ln1_bias, w_qkv, q_bias, v_bias, w_out, out_bias, kernel_mean, kernel_width, kernel_map, ln2_gain, ln2_bias, w_up, up_bias, w_down, down_bias):
    weights = tuple((array.astype(jnp.float32) for array in (inputs, time_weight, ln1_gain, ln1_bias, w_qkv, q_bias, v_bias, w_out, out_bias, kernel_mean, kernel_width, kernel_map, ln2_gain, ln2_bias, w_up, up_bias, w_down, down_bias)))

    def forward_all(*every):
        return layer_forward(every, time_of_row, coords, segment_ids)
    result, pullback = jax.vjp(forward_all, *weights)
    grads = pullback(cotangent.astype(jnp.float32))
    return (result.astype(jnp.bfloat16), grads[0].astype(jnp.bfloat16), grads[1], grads[2], grads[3], grads[4], grads[5], grads[6], grads[7], grads[8], grads[9], grads[10], grads[11], grads[12], grads[13], grads[14], grads[15], grads[16], grads[17])
```

```python
import functools
import math

import jax
import jax.numpy as jnp
from jax import lax
from jax.experimental import pallas as pl
from jax.experimental.pallas import tpu as pltpu
from jax.sharding import PartitionSpec as P

SET = 256


epsilon = 1e-05


def layer_norm(values_in, gain_vec, shift_vec):
    average = jnp.mean(values_in, axis=-1, keepdims=True)
    centred = values_in - average
    variance = jnp.mean(centred * centred, axis=-1, keepdims=True)
    return centred * lax.rsqrt(variance + epsilon) * gain_vec + shift_vec


def contract_rows(left, right):
    return lax.dot_general(
        left, right, (((0,), (0,)), ((), ())), preferred_element_type=jnp.float32
    )


def times_transpose(left, right):
    return lax.dot_general(
        left, right, (((1,), (1,)), ((), ())), preferred_element_type=jnp.float32
    )


CH = 32
WIN = 128
GROUPS = ((0, 0, 10), (128, 10, 16), (384, 16, 26), (512, 26, 32))
HW = 24
VM = 60 * 1024 * 1024
root_half_log2e = math.sqrt(0.5 * math.log2(math.e))
f32, bf16 = jnp.float32, jnp.bfloat16
NT = (((1,), (1,)), ((), ()))
TN = (((0,), (0,)), ((), ()))


def dot(a, b, dims=(((1,), (0,)), ((), ()))):
    return lax.dot_general(a, b, dims, preferred_element_type=f32)


def lane_mask(lane0, head, rows):
    lanes = lax.broadcasted_iota(jnp.int32, (rows, 256), 1) + lane0
    return (lanes >= head * HW) & (lanes < (head + 1) * HW)


def spread_heads(block, lane0, h0, h1):
    wide = block.astype(f32)
    zero = jnp.zeros_like(wide)
    return jnp.concatenate(
        [jnp.where(lane_mask(lane0, h, wide.shape[0]), wide, zero).astype(bf16) for h in range(h0, h1)], axis=0
    )


def pick_heads(full, lane0, h0, h1):
    n = h1 - h0
    full = full.reshape(n, CH, 256)
    out = jnp.zeros((CH, 256), f32)
    for j in range(n):
        out = jnp.where(lane_mask(lane0, h0 + j, CH), full[j], out)
    return out


def window_start(i, rows):
    return pl.multiple_of(jnp.clip(i * CH - 48, 0, rows - WIN), 16)


def radius_of(ac, aw):
    d = ac[:, 0:1] - aw[0:1, :]
    s = d * d
    for j in (1, 2):
        d = ac[:, j : j + 1] - aw[j : j + 1, :]
        s = s + d * d
    return jnp.sqrt(s)


def fwd_kernel(q_ref, k_ref, v_ref, aw_ref, ac_ref, kp_ref, bmat_ref, o_ref, p_ref, rho_scr, f_scr, b_scr):
    rows = k_ref.shape[0]
    w = window_start(pl.program_id(0), rows)
    ac, aw = ac_ref[...], aw_ref[0]
    rho_scr[...] = radius_of(ac, aw)
    joined = ac[:, 3:4] == aw[3:4, :]
    for p in range(2):
        for kt in range(8):
            ks = slice(16 * kt, 16 * kt + 16)
            A, B, C = kp_ref[0, ks, :], kp_ref[1, ks, :], kp_ref[2, ks, :]
            for r in range(8):
                for gg in range(2):
                    rr = rho_scr[pl.ds(16 * p + 8 * gg + r, 1), :]
                    y = rr * A - B
                    f = jnp.exp2(C - y * y)
                    f_scr[p, r * 128 + 16 * kt : r * 128 + 16 * kt + 16, gg * 128 : gg * 128 + 128] = f.astype(bf16)
        bias = dot(bmat_ref[...], f_scr[p])
        for gg in range(2):
            b_scr[:, 2 * p + gg] = bias[:, gg * 128 : gg * 128 + 128].reshape(32, 8, 128)
    kwin = k_ref[pl.ds(w, WIN), :]
    vwin = v_ref[pl.ds(w, WIN), :]
    acc = []
    for lane0, h0, h1 in GROUPS:
        n = h1 - h0
        sl = slice(lane0, lane0 + 256)
        qm = spread_heads(q_ref[:, sl], lane0, h0, h1)
        s = dot(qm, kwin[:, sl], NT).reshape(n, CH, WIN) + b_scr[h0:h1].reshape(n, CH, WIN)
        s = jnp.where(joined[None], s, -1e30)
        e = jnp.exp(s - jnp.max(s, axis=-1, keepdims=True))
        pr = (e * (1.0 / jnp.sum(e, axis=-1, keepdims=True))).reshape(n * CH, WIN).astype(bf16)
        p_ref[0, h0 * CH : h1 * CH, :] = pr
        acc.append(pick_heads(dot(pr, vwin[:, sl]), lane0, h0, h1))
    for half in range(2):
        a, b = acc[2 * half], acc[2 * half + 1]
        full = jnp.concatenate([a[:, :128], a[:, 128:] + b[:, :128], b[:, 128:]], axis=1)
        o_ref[:, 384 * half : 384 * half + 384] = full.astype(bf16)


def bwd_kernel(q_ref, do_ref, k_ref, v_ref, p_ref, gp_ref, ds_ref, dk_scr, dv_scr, *, scale):
    rows = k_ref.shape[0]
    i = pl.program_id(0)
    w = window_start(i, rows)
    width = 32 * HW

    @pl.when(i == 0)
    def _():
        dk_scr[...] = jnp.zeros_like(dk_scr)
        dv_scr[...] = jnp.zeros_like(dv_scr)

    kwin = k_ref[pl.ds(w, WIN), :]
    vwin = v_ref[pl.ds(w, WIN), :]
    acc = []
    for lane0, h0, h1 in GROUPS:
        n = h1 - h0
        sl = slice(lane0, lane0 + 256)
        qm = spread_heads(q_ref[:, sl], lane0, h0, h1)
        dom = spread_heads(do_ref[:, sl], lane0, h0, h1)
        p_low = p_ref[0, h0 * CH : h1 * CH, :]
        dp = dot(dom, vwin[:, sl], NT)
        pf = p_low.astype(f32)
        pd = pf * dp
        ds = pd - pf * jnp.sum(pd, axis=-1, keepdims=True)
        ds4 = ds.reshape(n, 4, 8, WIN)
        for g in range(4):
            ds_ref[0, g // 2, h0 * 8 : h1 * 8, (g % 2) * 128 : (g % 2) * 128 + 128] = (
                ds4[:, g].reshape(n * 8, WIN).astype(bf16)
            )
        ds_low = ds.astype(bf16)
        acc.append(pick_heads(dot(ds_low, kwin[:, sl]), lane0, h0, h1))
        dk_scr[pl.ds(w, WIN), sl] += dot(ds_low, qm, TN)
        dv_scr[pl.ds(w, WIN), sl] += dot(p_low, dom, TN)
    r0 = pl.multiple_of(i * CH, CH)
    for half in range(2):
        a, b = acc[2 * half], acc[2 * half + 1]
        full = jnp.concatenate([a[:, :128], a[:, 128:] + b[:, :128], b[:, 128:]], axis=1)
        gp_ref[pl.ds(r0, CH), 384 * half : 384 * half + 384] = (full * scale).astype(bf16)

    @pl.when(i == pl.num_programs(0) - 1)
    def _():
        gp_ref[:, width : 2 * width] = dk_scr[...].astype(bf16)
        gp_ref[:, 2 * width :] = dv_scr[...].astype(bf16)


def feat_kernel(ds_ref, aw_ref, ac_ref, kp_ref, amat_ref, m0_ref, acc_ref, rho_scr, f_scr, gf_scr):
    i = pl.program_id(0)

    @pl.when(i == 0)
    def _():
        m0_ref[...] = jnp.zeros_like(m0_ref)
        acc_ref[...] = jnp.zeros_like(acc_ref)

    rho_scr[...] = radius_of(ac_ref[...], aw_ref[0])
    for p in range(2):
        gf_scr[p] = dot(amat_ref[...], ds_ref[0, p])
    for p in range(2):
        for kt in range(8):
            ks = slice(16 * kt, 16 * kt + 16)
            A, B, C = kp_ref[0, ks, :], kp_ref[1, ks, :], kp_ref[2, ks, :]
            a1 = acc_ref[0, ks, :]
            a2 = acc_ref[1, ks, :]
            for r in range(8):
                for gg in range(2):
                    rr = rho_scr[pl.ds(16 * p + 8 * gg + r, 1), :]
                    at = (p, slice(r * 128 + 16 * kt, r * 128 + 16 * kt + 16), slice(gg * 128, gg * 128 + 128))
                    y = rr * A - B
                    f = jnp.exp2(C - y * y)
                    f_scr[at] = f.astype(bf16)
                    ty = gf_scr[at] * f * y
                    a1 = a1 + ty
                    a2 = a2 + ty * y
            acc_ref[0, ks, :] = a1
            acc_ref[1, ks, :] = a2
        m0_ref[...] += dot(f_scr[p], ds_ref[0, p], NT)


def full_spec(shape):
    return pl.BlockSpec(shape, lambda i: (0,) * len(shape))


def params(limit=VM):
    return pltpu.CompilerParams(vmem_limit_bytes=limit, dimension_semantics=("arbitrary",))


def attn_fwd(q, k, v, aw, ac, kp, bmat):
    rows, width = q.shape
    c = rows // CH
    return pl.pallas_call(
        fwd_kernel,
        grid=(c,),
        in_specs=[
            pl.BlockSpec((CH, width), lambda i: (i, 0)),
            full_spec(k.shape), full_spec(v.shape),
            pl.BlockSpec((1, 8, WIN), lambda i: (i, 0, 0)),
            pl.BlockSpec((CH, 4), lambda i: (i, 0)),
            full_spec(kp.shape), full_spec(bmat.shape),
        ],
        out_specs=[pl.BlockSpec((CH, width), lambda i: (i, 0)), pl.BlockSpec((1, 32 * CH, WIN), lambda i: (i, 0, 0))],
        out_shape=[jax.ShapeDtypeStruct((rows, width), bf16), jax.ShapeDtypeStruct((c, 32 * CH, WIN), bf16)],
        scratch_shapes=[pltpu.VMEM((CH, WIN), f32), pltpu.VMEM((2, 1024, 256), bf16), pltpu.VMEM((32, 4, 8, 128), f32)],
        compiler_params=params(),
        name="attn_fwd",
    )(q, k, v, aw, ac, kp, bmat)


def attn_bwd(q, do, k, v, p, scale):
    rows, width = q.shape
    c = rows // CH
    return pl.pallas_call(
        functools.partial(bwd_kernel, scale=scale),
        grid=(c,),
        in_specs=[
            pl.BlockSpec((CH, width), lambda i: (i, 0)),
            pl.BlockSpec((CH, width), lambda i: (i, 0)),
            full_spec(k.shape), full_spec(v.shape),
            pl.BlockSpec((1, 32 * CH, WIN), lambda i: (i, 0, 0)),
        ],
        out_specs=[full_spec((rows, 3 * width)), pl.BlockSpec((1, 2, 256, 256), lambda i: (i, 0, 0, 0))],
        out_shape=[jax.ShapeDtypeStruct((rows, 3 * width), bf16), jax.ShapeDtypeStruct((c, 2, 256, 256), bf16)],
        scratch_shapes=[pltpu.VMEM((rows, width), f32)] * 2,
        compiler_params=params(),
        name="attn_bwd",
    )(q, do, k, v, p)


def attn_feat(ds, aw, ac, kp, amat):
    c = ds.shape[0]
    return pl.pallas_call(
        feat_kernel,
        grid=(c,),
        in_specs=[
            pl.BlockSpec((1, 2, 256, 256), lambda i: (i, 0, 0, 0)),
            pl.BlockSpec((1, 8, WIN), lambda i: (i, 0, 0)),
            pl.BlockSpec((CH, 4), lambda i: (i, 0)),
            full_spec(kp.shape), full_spec(amat.shape),
        ],
        out_specs=[full_spec((1024, 256)), full_spec((2, 128, 128))],
        out_shape=[jax.ShapeDtypeStruct((1024, 256), f32), jax.ShapeDtypeStruct((2, 128, 128), f32)],
        scratch_shapes=[pltpu.VMEM((CH, WIN), f32), pltpu.VMEM((2, 1024, 256), bf16), pltpu.VMEM((2, 1024, 256), f32)],
        compiler_params=params(),
        name="attn_feat",
    )(ds, aw, ac, kp, amat)


def aux_of(coords, segment_ids):
    rows = coords.shape[1]
    place = jnp.arange(rows, dtype=jnp.int32) // SET
    key = (segment_ids * (rows // SET) + place).astype(f32)
    packed = jnp.concatenate([coords, key[None], jnp.zeros((4, rows), f32)], axis=0)
    starts = [min(max(CH * i - 48, 0), rows - WIN) for i in range(rows // CH)]
    aw = jnp.stack([packed[:, s : s + WIN] for s in starts])
    ac = packed[:4].T
    return aw, ac


def kernel_consts(mean, width, kmap):
    mean, width = mean.astype(f32), width.astype(f32)
    a = root_half_log2e / width
    b = mean * a
    c = -jnp.log2(math.sqrt(2 * math.pi) * width)
    kp = jnp.broadcast_to(jnp.stack([a, b, c])[:, :, None], (3, mean.shape[0], 128))
    eye = jnp.eye(8, dtype=bf16)
    heads = kmap.shape[1]
    amat = (eye[:, None, None, :] * kmap[None, :, :, None]).reshape(8 * kmap.shape[0], heads * 8)
    return kp, amat


def feat_finish(m0, acc, width, kmap):
    n, heads = kmap.shape
    m = m0.reshape(8, n, heads, 8)
    g_map = jnp.sum(m * jnp.eye(8, dtype=f32)[:, None, None, :], axis=(0, 3))
    width = width.astype(f32)
    s = jnp.sum(acc, axis=-1)
    a0 = jnp.sum(g_map * kmap.astype(f32), axis=1)
    g_mean = s[0] / (root_half_log2e * width)
    g_width = (s[1] / (root_half_log2e * root_half_log2e) - a0) / width
    return g_map, g_mean, g_width


def on_device(
    inputs,
    time_of_row,
    coords,
    segment_ids,
    cotangent,
    time_weight,
    ln1_gain,
    ln1_bias,
    w_qkv,
    q_bias,
    v_bias,
    w_out,
    out_bias,
    kernel_mean,
    kernel_width,
    kernel_map,
    ln2_gain,
    ln2_bias,
    w_up,
    up_bias,
    w_down,
    down_bias,
):
    attn_full = (
        lax.all_gather(time_weight, "fsdp", axis=0, tiled=True),
        lax.all_gather(ln1_gain, "fsdp", axis=0, tiled=True),
        lax.all_gather(ln1_bias, "fsdp", axis=0, tiled=True),
        lax.all_gather(w_qkv, "fsdp", axis=0, tiled=True),
        lax.all_gather(q_bias, "fsdp", axis=0, tiled=True),
        lax.all_gather(v_bias, "fsdp", axis=0, tiled=True),
        lax.all_gather(w_out, "fsdp", axis=0, tiled=True),
        lax.all_gather(out_bias, "fsdp", axis=0, tiled=True),
        lax.all_gather(kernel_mean, "fsdp", axis=0, tiled=True),
        lax.all_gather(kernel_width, "fsdp", axis=0, tiled=True),
        lax.all_gather(kernel_map, "fsdp", axis=0, tiled=True),
    )
    (
        time_full,
        gain_first,
        shift_first,
        qkv_full,
        qbias_full,
        vbias_full,
        wout_full,
        obias_full,
        mean_full,
        width_full,
        map_full,
    ) = attn_full
    rows_here = inputs.shape[0]
    width_model = inputs.shape[1]
    head_count = map_full.shape[1]
    head_width = width_model // head_count
    query_scale = head_width ** (-0.5)

    start = inputs.astype(jnp.float32) + time_of_row[:, None] * time_full.astype(jnp.float32)
    normed_low = layer_norm(
        start, gain_first.astype(jnp.float32), shift_first.astype(jnp.float32)
    ).astype(jnp.bfloat16)
    projected = jnp.dot(normed_low, qkv_full, preferred_element_type=jnp.float32)
    queries = ((projected[:, :width_model] + qbias_full.astype(jnp.float32)) * query_scale).astype(
        jnp.bfloat16
    )
    keys_low = projected[:, width_model : 2 * width_model].astype(jnp.bfloat16)
    values_low = (projected[:, 2 * width_model :] + vbias_full.astype(jnp.float32)).astype(
        jnp.bfloat16
    )
    aux_win, aux_col = aux_of(coords, segment_ids)
    consts, spread_map = kernel_consts(mean_full, width_full, map_full)
    attended, probs = attn_fwd(
        queries, keys_low, values_low, aux_win, aux_col, consts, spread_map.T
    )
    middle = (
        start
        + jnp.dot(attended, wout_full, preferred_element_type=jnp.float32)
        + obias_full.astype(jnp.float32)
    )
    ffn_full = (
        lax.all_gather(ln2_gain, "fsdp", axis=0, tiled=True),
        lax.all_gather(ln2_bias, "fsdp", axis=0, tiled=True),
        lax.all_gather(w_up, "fsdp", axis=0, tiled=True),
        lax.all_gather(up_bias, "fsdp", axis=0, tiled=True),
        lax.all_gather(w_down, "fsdp", axis=0, tiled=True),
        lax.all_gather(down_bias, "fsdp", axis=0, tiled=True),
    )
    gain_second, shift_second, up_full, upbias_full, down_full, dbias_full = ffn_full
    normed2_low = layer_norm(
        middle, gain_second.astype(jnp.float32), shift_second.astype(jnp.float32)
    ).astype(jnp.bfloat16)
    pre_hidden = jnp.dot(
        normed2_low, up_full, preferred_element_type=jnp.float32
    ) + upbias_full.astype(jnp.float32)
    hidden_low = jax.nn.gelu(pre_hidden, approximate=False).astype(jnp.bfloat16)
    result = (
        middle
        + jnp.dot(hidden_low, down_full, preferred_element_type=jnp.float32)
        + dbias_full.astype(jnp.float32)
    )
    output = result.astype(jnp.bfloat16)
    ffn_back = (
        lax.all_gather(ln2_gain, "fsdp", axis=0, tiled=True),
        lax.all_gather(ln2_bias, "fsdp", axis=0, tiled=True),
        lax.all_gather(w_up, "fsdp", axis=0, tiled=True),
        lax.all_gather(up_bias, "fsdp", axis=0, tiled=True),
        lax.all_gather(w_down, "fsdp", axis=0, tiled=True),
        lax.all_gather(down_bias, "fsdp", axis=0, tiled=True),
    )
    grad_output = cotangent.astype(jnp.float32)
    grad_w_down = contract_rows(hidden_low, cotangent)
    grad_down_bias = jnp.sum(grad_output, axis=0)
    grad_hidden = times_transpose(cotangent, ffn_back[4])
    unused_gelu, gelu_pull = jax.vjp(functools.partial(jax.nn.gelu, approximate=False), pre_hidden)
    grad_pre = gelu_pull(grad_hidden)[0].astype(jnp.bfloat16)
    grad_w_up = contract_rows(normed2_low, grad_pre)
    grad_up_bias = jnp.sum(grad_pre.astype(jnp.float32), axis=0)
    grad_normed2 = times_transpose(grad_pre, ffn_back[2])
    unused_second, second_pull = jax.vjp(
        layer_norm, middle, ffn_back[0].astype(jnp.float32), ffn_back[1].astype(jnp.float32)
    )
    grad_middle_part, grad_ln2_gain, grad_ln2_bias = second_pull(grad_normed2)
    grad_middle = grad_output + grad_middle_part
    attn_back = (
        lax.all_gather(time_weight, "fsdp", axis=0, tiled=True),
        lax.all_gather(ln1_gain, "fsdp", axis=0, tiled=True),
        lax.all_gather(ln1_bias, "fsdp", axis=0, tiled=True),
        lax.all_gather(w_qkv, "fsdp", axis=0, tiled=True),
        lax.all_gather(q_bias, "fsdp", axis=0, tiled=True),
        lax.all_gather(v_bias, "fsdp", axis=0, tiled=True),
        lax.all_gather(w_out, "fsdp", axis=0, tiled=True),
        lax.all_gather(out_bias, "fsdp", axis=0, tiled=True),
        lax.all_gather(kernel_mean, "fsdp", axis=0, tiled=True),
        lax.all_gather(kernel_width, "fsdp", axis=0, tiled=True),
        lax.all_gather(kernel_map, "fsdp", axis=0, tiled=True),
    )
    grad_attn = grad_middle.astype(jnp.bfloat16)
    grad_w_out = contract_rows(attended, grad_attn)
    grad_out_bias = jnp.sum(grad_attn.astype(jnp.float32), axis=0)
    grad_attended = times_transpose(grad_attn, attn_back[6]).astype(jnp.bfloat16)
    grad_projected, grad_scores = attn_bwd(
        queries, grad_attended, keys_low, values_low, probs, query_scale
    )
    map_parts, feature_parts = attn_feat(grad_scores, aux_win, aux_col, consts, spread_map)
    grad_kernel_map, grad_kernel_mean, grad_kernel_width = feat_finish(
        map_parts, feature_parts, width_full, map_full
    )
    grad_pre_query = grad_projected[:, :width_model]
    grad_values = grad_projected[:, 2 * width_model :]
    grad_w_qkv = contract_rows(normed_low, grad_projected)
    grad_q_bias = jnp.sum(grad_pre_query.astype(jnp.float32), axis=0)
    grad_v_bias = jnp.sum(grad_values.astype(jnp.float32), axis=0)
    grad_normed = times_transpose(grad_projected, attn_back[3])
    unused_first, first_pull = jax.vjp(
        layer_norm, start, attn_back[1].astype(jnp.float32), attn_back[2].astype(jnp.float32)
    )
    grad_start_part, grad_ln1_gain, grad_ln1_bias = first_pull(grad_normed)
    grad_start = grad_middle + grad_start_part
    grad_time_weight = jnp.sum(time_of_row[:, None] * grad_start, axis=0)
    grad_inputs = grad_start.astype(jnp.bfloat16)
    owned = (
        lax.psum_scatter(grad_time_weight, "fsdp", scatter_dimension=0, tiled=True),
        lax.psum_scatter(grad_ln1_gain, "fsdp", scatter_dimension=0, tiled=True),
        lax.psum_scatter(grad_ln1_bias, "fsdp", scatter_dimension=0, tiled=True),
        lax.psum_scatter(grad_w_qkv, "fsdp", scatter_dimension=0, tiled=True),
        lax.psum_scatter(grad_q_bias, "fsdp", scatter_dimension=0, tiled=True),
        lax.psum_scatter(grad_v_bias, "fsdp", scatter_dimension=0, tiled=True),
        lax.psum_scatter(grad_w_out, "fsdp", scatter_dimension=0, tiled=True),
        lax.psum_scatter(grad_out_bias, "fsdp", scatter_dimension=0, tiled=True),
        lax.psum_scatter(grad_kernel_mean, "fsdp", scatter_dimension=0, tiled=True),
        lax.psum_scatter(grad_kernel_width, "fsdp", scatter_dimension=0, tiled=True),
        lax.psum_scatter(grad_kernel_map, "fsdp", scatter_dimension=0, tiled=True),
        lax.psum_scatter(grad_ln2_gain, "fsdp", scatter_dimension=0, tiled=True),
        lax.psum_scatter(grad_ln2_bias, "fsdp", scatter_dimension=0, tiled=True),
        lax.psum_scatter(grad_w_up, "fsdp", scatter_dimension=0, tiled=True),
        lax.psum_scatter(grad_up_bias, "fsdp", scatter_dimension=0, tiled=True),
        lax.psum_scatter(grad_w_down, "fsdp", scatter_dimension=0, tiled=True),
        lax.psum_scatter(grad_down_bias, "fsdp", scatter_dimension=0, tiled=True),
    )
    owned = (
        lax.psum(owned[0].astype(jnp.bfloat16), "dp").astype(jnp.float32),
        lax.psum(owned[1].astype(jnp.bfloat16), "dp").astype(jnp.float32),
        lax.psum(owned[2].astype(jnp.bfloat16), "dp").astype(jnp.float32),
        lax.psum(owned[3].astype(jnp.bfloat16), "dp").astype(jnp.float32),
        lax.psum(owned[4].astype(jnp.bfloat16), "dp").astype(jnp.float32),
        lax.psum(owned[5].astype(jnp.bfloat16), "dp").astype(jnp.float32),
        lax.psum(owned[6].astype(jnp.bfloat16), "dp").astype(jnp.float32),
        lax.psum(owned[7].astype(jnp.bfloat16), "dp").astype(jnp.float32),
        lax.psum(owned[8].astype(jnp.bfloat16), "dp").astype(jnp.float32),
        lax.psum(owned[9].astype(jnp.bfloat16), "dp").astype(jnp.float32),
        lax.psum(owned[10].astype(jnp.bfloat16), "dp").astype(jnp.float32),
        lax.psum(owned[11].astype(jnp.bfloat16), "dp").astype(jnp.float32),
        lax.psum(owned[12].astype(jnp.bfloat16), "dp").astype(jnp.float32),
        lax.psum(owned[13].astype(jnp.bfloat16), "dp").astype(jnp.float32),
        lax.psum(owned[14].astype(jnp.bfloat16), "dp").astype(jnp.float32),
        lax.psum(owned[15].astype(jnp.bfloat16), "dp").astype(jnp.float32),
        lax.psum(owned[16].astype(jnp.bfloat16), "dp").astype(jnp.float32),
    )
    return (
        output,
        grad_inputs,
        owned[0],
        owned[1],
        owned[2],
        owned[3],
        owned[4],
        owned[5],
        owned[6],
        owned[7],
        owned[8],
        owned[9],
        owned[10],
        owned[11],
        owned[12],
        owned[13],
        owned[14],
        owned[15],
        owned[16],
    )


def solution(mesh):
    placed = (
        P(("fsdp", "dp"), None),
        P(("fsdp", "dp")),
        P(None, ("fsdp", "dp")),
        P(("fsdp", "dp")),
        P(("fsdp", "dp"), None),
        P("fsdp"),
        P("fsdp"),
        P("fsdp"),
        P("fsdp", None),
        P("fsdp"),
        P("fsdp"),
        P("fsdp", None),
        P("fsdp"),
        P("fsdp"),
        P("fsdp"),
        P("fsdp", None),
        P("fsdp"),
        P("fsdp"),
        P("fsdp", None),
        P("fsdp"),
        P("fsdp", None),
        P("fsdp"),
    )
    return jax.shard_map(
        on_device,
        mesh=mesh,
        in_specs=placed,
        out_specs=(
            P(("fsdp", "dp"), None),
            P(("fsdp", "dp"), None),
            P("fsdp"),
            P("fsdp"),
            P("fsdp"),
            P("fsdp", None),
            P("fsdp"),
            P("fsdp"),
            P("fsdp", None),
            P("fsdp"),
            P("fsdp"),
            P("fsdp"),
            P("fsdp", None),
            P("fsdp"),
            P("fsdp"),
            P("fsdp", None),
            P("fsdp"),
            P("fsdp", None),
            P("fsdp"),
        ),
        check_vma=False,
    )
```

```python
import functools, math
import jax, jax.numpy as jnp
from jax import lax
from jax.experimental import pallas as pl
from jax.experimental.pallas import tpu as pltpu
from jax.sharding import PartitionSpec as P

SET = 256
CH = 32
WIN = 128
GROUPS = ((0, 0, 10), (128, 10, 16), (384, 16, 26), (512, 26, 32))
HW = 24
VM = 60 * 1024 * 1024
root_half_log2e = math.sqrt(0.5 * math.log2(math.e))
f32, bf16 = jnp.float32, jnp.bfloat16
NT = (((1,), (1,)), ((), ()))
TN = (((0,), (0,)), ((), ()))


def dot(a, b, dims=(((1,), (0,)), ((), ()))):
    return lax.dot_general(a, b, dims, preferred_element_type=f32)


def lane_mask(lane0, head, rows):
    lanes = lax.broadcasted_iota(jnp.int32, (rows, 256), 1) + lane0
    return (lanes >= head * HW) & (lanes < (head + 1) * HW)


def spread_heads(block, lane0, h0, h1):
    wide = block.astype(f32)
    zero = jnp.zeros_like(wide)
    return jnp.concatenate(
        [jnp.where(lane_mask(lane0, h, wide.shape[0]), wide, zero).astype(bf16) for h in range(h0, h1)], axis=0
    )


def pick_heads(full, lane0, h0, h1):
    n = h1 - h0
    full = full.reshape(n, CH, 256)
    out = jnp.zeros((CH, 256), f32)
    for j in range(n):
        out = jnp.where(lane_mask(lane0, h0 + j, CH), full[j], out)
    return out


def window_start(i, rows):
    return pl.multiple_of(jnp.clip(i * CH - 48, 0, rows - WIN), 16)


def radius_of(ac, aw):
    d = ac[:, 0:1] - aw[0:1, :]
    s = d * d
    for j in (1, 2):
        d = ac[:, j : j + 1] - aw[j : j + 1, :]
        s = s + d * d
    return jnp.sqrt(s)


def bias_kernel(aw_ref, ac_ref, kp_ref, bmat_ref, b_ref, rho_scr, f_scr):
    ac, aw = ac_ref[...], aw_ref[0]
    rho_scr[...] = radius_of(ac, aw)
    joined = ac[:, 3:4] == aw[3:4, :]
    for p in range(2):
        for kt in range(8):
            ks = slice(16 * kt, 16 * kt + 16)
            A, B, C = kp_ref[0, ks, :], kp_ref[1, ks, :], kp_ref[2, ks, :]
            for r in range(8):
                for gg in range(2):
                    rr = rho_scr[pl.ds(16 * p + 8 * gg + r, 1), :]
                    y = rr * A - B
                    f = jnp.exp2(C - y * y)
                    f_scr[p, r * 128 + 16 * kt : r * 128 + 16 * kt + 16, gg * 128 : gg * 128 + 128] = f.astype(bf16)
    for p in range(2):
        bias = dot(bmat_ref[...], f_scr[p])
        for gg in range(2):
            g = 2 * p + gg
            part = bias[:, gg * 128 : gg * 128 + 128].reshape(32, 8, WIN)
            b_ref[0, :, 8 * g : 8 * g + 8, :] = jnp.where(joined[8 * g : 8 * g + 8][None], part, -1e30)


def fwd_kernel(q_ref, k_ref, v_ref, b_ref, o_ref, p_ref):
    rows = k_ref.shape[0]
    w = window_start(pl.program_id(0), rows)
    kwin = k_ref[pl.ds(w, WIN), :]
    vwin = v_ref[pl.ds(w, WIN), :]
    acc = []
    for lane0, h0, h1 in GROUPS:
        n = h1 - h0
        sl = slice(lane0, lane0 + 256)
        qm = spread_heads(q_ref[:, sl], lane0, h0, h1)
        s = dot(qm, kwin[:, sl], NT).reshape(n, CH, WIN) + b_ref[0, h0:h1]
        e = jnp.exp(s - jnp.max(s, axis=-1, keepdims=True))
        pr = (e * (1.0 / jnp.sum(e, axis=-1, keepdims=True))).reshape(n * CH, WIN).astype(bf16)
        p_ref[0, h0 * CH : h1 * CH, :] = pr
        acc.append(pick_heads(dot(pr, vwin[:, sl]), lane0, h0, h1))
    store_lanes(o_ref, slice(None), acc, 1.0)


def store_lanes(ref, rows, acc, scale):
    for half in range(2):
        a, b = acc[2 * half], acc[2 * half + 1]
        full = jnp.concatenate([a[:, :128], a[:, 128:] + b[:, :128], b[:, 128:]], axis=1)
        if scale != 1.0:
            full = full * scale
        ref[rows, 384 * half : 384 * half + 384] = full.astype(bf16)


def bwd_kernel(q_ref, do_ref, k_ref, v_ref, p_ref, gp_ref, ds_ref, dk_scr, dv_scr, *, scale):
    rows = k_ref.shape[0]
    i = pl.program_id(0)
    w = window_start(i, rows)
    width = 32 * HW

    @pl.when(i == 0)
    def _():
        dk_scr[...] = jnp.zeros_like(dk_scr)
        dv_scr[...] = jnp.zeros_like(dv_scr)

    kwin = k_ref[pl.ds(w, WIN), :]
    vwin = v_ref[pl.ds(w, WIN), :]
    acc = []
    for lane0, h0, h1 in GROUPS:
        n = h1 - h0
        sl = slice(lane0, lane0 + 256)
        qm = spread_heads(q_ref[:, sl], lane0, h0, h1)
        dom = spread_heads(do_ref[:, sl], lane0, h0, h1)
        p_low = p_ref[0, h0 * CH : h1 * CH, :]
        dp = dot(dom, vwin[:, sl], NT)
        pf = p_low.astype(f32)
        pd = pf * dp
        ds = pd - pf * jnp.sum(pd, axis=-1, keepdims=True)
        ds4 = ds.reshape(n, 4, 8, WIN)
        for g in range(4):
            ds_ref[0, g // 2, h0 * 8 : h1 * 8, (g % 2) * 128 : (g % 2) * 128 + 128] = (
                ds4[:, g].reshape(n * 8, WIN).astype(bf16)
            )
        ds_low = ds.astype(bf16)
        acc.append(pick_heads(dot(ds_low, kwin[:, sl]), lane0, h0, h1))
        dk_scr[pl.ds(w, WIN), sl] += dot(ds_low, qm, TN)
        dv_scr[pl.ds(w, WIN), sl] += dot(p_low, dom, TN)
    store_lanes(gp_ref, pl.ds(pl.multiple_of(i * CH, CH), CH), acc, scale)

    @pl.when(i == pl.num_programs(0) - 1)
    def _():
        gp_ref[:, width : 2 * width] = dk_scr[...].astype(bf16)
        gp_ref[:, 2 * width :] = dv_scr[...].astype(bf16)


def feat_kernel(n_before, ds_ref, aw_ref, ac_ref, kp_ref, amat_ref, *rest):
    before, (m0_ref, acc_ref, rho_scr, f_scr, gf_scr) = rest[:n_before], rest[n_before:]
    i = pl.program_id(0)

    @pl.when(i == 0)
    def _():
        m0_ref[...] = before[0][...] if before else jnp.zeros_like(m0_ref)
        acc_ref[...] = before[1][...] if before else jnp.zeros_like(acc_ref)

    rho_scr[...] = radius_of(ac_ref[...], aw_ref[0])
    for p in range(2):
        gf_scr[p] = dot(amat_ref[...], ds_ref[0, p])
    for p in range(2):
        for kt in range(8):
            ks = slice(16 * kt, 16 * kt + 16)
            A, B, C = kp_ref[0, ks, :], kp_ref[1, ks, :], kp_ref[2, ks, :]
            a1 = acc_ref[0, ks, :]
            a2 = acc_ref[1, ks, :]
            for r in range(8):
                for gg in range(2):
                    rr = rho_scr[pl.ds(16 * p + 8 * gg + r, 1), :]
                    at = (p, slice(r * 128 + 16 * kt, r * 128 + 16 * kt + 16), slice(gg * 128, gg * 128 + 128))
                    y = rr * A - B
                    f = jnp.exp2(C - y * y)
                    f_scr[at] = f.astype(bf16)
                    ty = gf_scr[at] * f * y
                    a1 = a1 + ty
                    a2 = a2 + ty * y
            acc_ref[0, ks, :] = a1
            acc_ref[1, ks, :] = a2
        m0_ref[...] += dot(f_scr[p], ds_ref[0, p], NT)


def cost(micros):
    return pl.CostEstimate(flops=int(micros * 1.1535e9), bytes_accessed=0, transcendentals=0)


def full_spec(shape):
    return pl.BlockSpec(shape, lambda i: (0,) * len(shape))


def params(limit=VM):
    return pltpu.CompilerParams(vmem_limit_bytes=limit, dimension_semantics=("arbitrary",))


PARTS = 4


def shifted(spec_shape, base):
    return pl.BlockSpec(spec_shape, lambda i: (i + base,) + (0,) * (len(spec_shape) - 1))


def half_spec(shape, part):
    return pl.BlockSpec(shape, lambda i: (part,) + (0,) * (len(shape) - 1))


def attn_bias(aw, ac, kp, bmat):
    c = aw.shape[0]
    return pl.pallas_call(
        bias_kernel,
        grid=(c,),
        in_specs=[shifted((1, 8, WIN), 0), shifted((CH, 4), 0), full_spec(kp.shape), full_spec(bmat.shape)],
        out_specs=shifted((1, 32, CH, WIN), 0),
        out_shape=jax.ShapeDtypeStruct((c, 32, CH, WIN), f32),
        scratch_shapes=[pltpu.VMEM((CH, WIN), f32), pltpu.VMEM((2, 1024, 256), bf16)],
        compiler_params=params(),
        cost_estimate=cost(30),
        name="attn_bias",
    )(aw, ac, kp, bmat)


def attn_fwd(part, q, k, v, bias, before):
    rows, width = q.shape
    c = rows // CH
    per = c // PARTS
    base = part * per
    kv = half_spec((rows // PARTS, width), part)
    n_in = 4
    return pl.pallas_call(
        functools.partial(skip_refs, fwd_kernel, n_in, len(before)),
        grid=(per,),
        in_specs=[shifted((CH, width), base), kv, kv, shifted((1, 32, CH, WIN), base)]
        + [pl.BlockSpec(memory_space=pl.ANY)] * len(before),
        out_specs=[shifted((CH, width), base), shifted((1, 32 * CH, WIN), base)],
        out_shape=[jax.ShapeDtypeStruct((rows, width), bf16), jax.ShapeDtypeStruct((c, 32 * CH, WIN), bf16)],
        input_output_aliases={n_in + t: t for t in range(len(before))},
        compiler_params=params(),
        cost_estimate=cost(28 // PARTS),
        name="attn_fwd",
    )(q, k, v, bias, *before)


def skip_refs(kernel, n_in, n_before, *refs):
    kernel(*refs[:n_in], *refs[n_in + n_before :])


def attn_bwd(part, q, do, k, v, p, scale, before):
    rows, width = q.shape
    c = rows // CH
    per = c // PARTS
    base = part * per
    kv = half_spec((rows // PARTS, width), part)
    n_in = 5
    return pl.pallas_call(
        functools.partial(skip_refs, functools.partial(bwd_kernel, scale=scale), n_in, len(before)),
        grid=(per,),
        in_specs=[
            shifted((CH, width), base), shifted((CH, width), base), kv, kv,
            shifted((1, 32 * CH, WIN), base),
        ] + [pl.BlockSpec(memory_space=pl.ANY)] * len(before),
        out_specs=[half_spec((rows // PARTS, 3 * width), part), shifted((1, 2, 256, 256), base)],
        out_shape=[jax.ShapeDtypeStruct((rows, 3 * width), bf16), jax.ShapeDtypeStruct((c, 2, 256, 256), bf16)],
        scratch_shapes=[pltpu.VMEM((rows // PARTS, width), f32)] * 2,
        input_output_aliases={n_in + t: t for t in range(len(before))},
        compiler_params=params(),
        cost_estimate=cost(56 // PARTS),
        name="attn_bwd",
    )(q, do, k, v, p, *before)


def attn_feat(part, ds, aw, ac, kp, amat, before):
    per = ds.shape[0] // PARTS
    base = part * per
    n_in = 5
    return pl.pallas_call(
        functools.partial(feat_kernel, len(before)),
        grid=(per,),
        in_specs=[
            shifted((1, 2, 256, 256), base), shifted((1, 8, WIN), base), shifted((CH, 4), base),
            full_spec(kp.shape), full_spec(amat.shape),
        ] + [full_spec(b.shape) for b in before],
        out_specs=[full_spec((1024, 256)), full_spec((2, 128, 128))],
        out_shape=[jax.ShapeDtypeStruct((1024, 256), f32), jax.ShapeDtypeStruct((2, 128, 128), f32)],
        scratch_shapes=[pltpu.VMEM((CH, WIN), f32), pltpu.VMEM((2, 1024, 256), bf16), pltpu.VMEM((2, 1024, 256), f32)],
        compiler_params=params(),
        cost_estimate=cost(42 // PARTS),
        name="attn_feat",
    )(ds, aw, ac, kp, amat, *before)


def aux_of(coords, segment_ids):
    rows = coords.shape[1]
    place = jnp.arange(rows, dtype=jnp.int32) // SET
    key = (segment_ids * (rows // SET) + place).astype(f32)
    packed = jnp.concatenate([coords, key[None], jnp.zeros((4, rows), f32)], axis=0)
    half = rows // PARTS
    starts = [b + min(max(i - 48, 0), half - WIN) for b in range(0, rows, half) for i in range(0, half, CH)]
    aw = jnp.stack([packed[:, s : s + WIN] for s in starts])
    ac = packed[:4].T
    return aw, ac


def kernel_consts(mean, width, kmap):
    mean, width = mean.astype(f32), width.astype(f32)
    a = root_half_log2e / width
    b = mean * a
    c = -jnp.log2(math.sqrt(2 * math.pi) * width)
    kp = jnp.broadcast_to(jnp.stack([a, b, c])[:, :, None], (3, mean.shape[0], 128))
    eye = jnp.eye(8, dtype=bf16)
    heads = kmap.shape[1]
    amat = (eye[:, None, None, :] * kmap[None, :, :, None]).reshape(8 * kmap.shape[0], heads * 8)
    return kp, amat


def feat_finish(m0, acc, width, kmap):
    n, heads = kmap.shape
    m = m0.reshape(8, n, heads, 8)
    g_map = jnp.sum(m * jnp.eye(8, dtype=f32)[:, None, None, :], axis=(0, 3))
    width = width.astype(f32)
    s = jnp.sum(acc, axis=-1)
    a0 = jnp.sum(g_map * kmap.astype(f32), axis=1)
    g_mean = s[0] / (root_half_log2e * width)
    g_width = (s[1] / (root_half_log2e * root_half_log2e) - a0) / width
    return g_map, g_mean, g_width


TILE = 256
epsilon = 1e-05


def ln_parts(v):
    mean = jnp.mean(v, axis=-1, keepdims=True)
    centred = v - mean
    rstd = lax.rsqrt(jnp.mean(centred * centred, axis=-1, keepdims=True) + epsilon)
    return centred * rstd, rstd


def ln_back(xhat, rstd, dn, gain):
    dg = dn * gain
    m1 = jnp.mean(dg, axis=-1, keepdims=True)
    m2 = jnp.mean(dg * xhat, axis=-1, keepdims=True)
    return rstd * (dg - m1 - xhat * m2)


def rows_sum(v):
    return jnp.sum(v, axis=0, keepdims=True)


def fetch(idx_ref, pieces, moves, sem, base=0):
    copies = []
    for m, piece in enumerate(pieces):
        for dest, first, column, rows, columns in moves:
            at = pl.multiple_of(idx_ref[m] * rows, 16)
            copies.append(
                pltpu.make_async_copy(
                    piece.at[pl.ds(first, rows), :],
                    dest.at[pl.ds(at, rows), pl.ds(column, columns)],
                    sem.at[base + len(copies)],
                )
            )
    return copies


def fetch_whole(arrays, dests, sem):
    return [pltpu.make_async_copy(a, d, sem.at[i]) for i, (a, d) in enumerate(zip(arrays, dests))]


def qkv_copies(idx_ref, pieces, w_scr, sem):
    if len(pieces) == 1:
        return fetch_whole(pieces, [w_scr], sem)
    r, columns = pieces[0].shape
    return fetch(idx_ref, pieces, [(w_scr, 0, 0, r, columns)], sem)


def ffn_copies(idx_ref, pieces, wo, up, down, sem):
    if len(pieces) == 3:
        return fetch_whole(pieces, [wo, up, down], sem)
    width = wo.shape[0]
    n = len(pieces) // 2
    r = width // n
    wide = up.shape[1] // width
    moves = [(wo, 0, 0, r, width)] + [(up, r + b * r, b * width, r, width) for b in range(wide)]
    copies = fetch(idx_ref, pieces[:n], moves, sem)
    return copies + fetch(idx_ref, pieces[n:], [(down, 0, 0, wide * r, width)], sem, len(copies))


def any_spec():
    return pl.BlockSpec(memory_space=pl.ANY)


def row_spec(width, tile=TILE):
    return pl.BlockSpec((tile, width), lambda i, *_: (i, 0))


def whole_spec(shape):
    return pl.BlockSpec(shape, lambda i, *_: (0,) * len(shape))


def qkv_kernel(n, scale, idx_ref, x_ref, t_ref, vec_ref, *rest):
    pieces, (normed_ref, q_ref, k_ref, v_ref, w_scr, sem) = rest[:n], rest[n:]
    width = x_ref.shape[1]

    @pl.when(pl.program_id(0) == 0)
    def _():
        for c in qkv_copies(idx_ref, pieces, w_scr, sem):
            c.start()

    start = x_ref[...].astype(f32) + t_ref[...] * vec_ref[0:1, :]
    normed = (ln_parts(start)[0] * vec_ref[1:2, :] + vec_ref[2:3, :]).astype(bf16)
    normed_ref[...] = normed

    @pl.when(pl.program_id(0) == 0)
    def _():
        for c in qkv_copies(idx_ref, pieces, w_scr, sem):
            c.wait()

    q_ref[...] = ((dot(normed, w_scr[:, :width]) + vec_ref[3:4, :]) * scale).astype(bf16)
    k_ref[...] = dot(normed, w_scr[:, width : 2 * width]).astype(bf16)
    v_ref[...] = (dot(normed, w_scr[:, 2 * width :]) + vec_ref[4:5, :]).astype(bf16)


def qkv_forward(idx, x, t, vecs, pieces, scale):
    rows, width = x.shape
    n = len(pieces)
    out = jax.ShapeDtypeStruct((rows, width), bf16)
    return pl.pallas_call(
        functools.partial(qkv_kernel, n, scale),
        grid_spec=pltpu.PrefetchScalarGridSpec(
            num_scalar_prefetch=1,
            grid=(rows // TILE,),
            in_specs=[row_spec(width), row_spec(1), whole_spec(vecs.shape)] + [any_spec()] * n,
            out_specs=[row_spec(width)] * 4,
            scratch_shapes=[pltpu.VMEM((width, 3 * width), bf16), pltpu.SemaphoreType.DMA((n,))],
        ),
        out_shape=[out] * 4,
        compiler_params=params(),
        cost_estimate=cost(10),
        name="qkv_forward",
    )(idx, x, t, vecs, *pieces)


def gelu_parts(x):
    a = jnp.abs(x)
    t = 1.0 / (1.0 + (0.3275911 * math.sqrt(0.5)) * a)
    e = jnp.exp(-0.5 * x * x)
    poly = t * (0.254829592 + t * (-0.284496736 + t * (1.421413741 + t * (-1.453152027 + t * 1.061405429))))
    tail = 0.5 * poly * e
    cdf = jnp.where(x >= 0, 1.0 - tail, tail)
    return x * cdf, cdf + x * e * (1.0 / math.sqrt(2.0 * math.pi))


def split_cores(value, core, owners):
    rows, c = value.shape
    pairs = value.reshape(owners // 2, 2, rows // owners, c)
    even, odd = pairs[:, 0], pairs[:, 1]
    return jnp.where(core == 0, even, odd), jnp.where(core == 0, odd, even)


def ffn_kernel(n, split, steps, idx_ref, x_ref, t_ref, att_ref, cot_ref, vec_ref, upb_ref, *rest):
    pieces = rest[:n]
    (out_ref, ga_ref, gvec_ref, gupb_ref, gm_hbm, keep_hbm, send_hbm,
     wo, up, down, mid, n2, n2t, acc, gn2, hid, gp, stage_up, stage_down, stage_out, sem, out_sem) = rest[n:]
    j = pl.program_id(0)
    rows, width = x_ref.shape
    fc = hid.shape[1]
    tiles = rows // TILE
    core = lax.rem(idx_ref[0], 2)
    r = width // split if split else 0

    def up_copies(step):
        if not split:
            return [pltpu.make_async_copy(stage_up, keep_hbm.at[step], out_sem.at[0])]
        at = pl.ds(pl.multiple_of(step * r, r), r)
        return [
            pltpu.make_async_copy(stage_up.at[s], dest.at[:, at, :], out_sem.at[s])
            for s, dest in enumerate((keep_hbm, send_hbm))
        ]

    def down_copies(step):
        if not split:
            return [pltpu.make_async_copy(stage_down, send_hbm.at[pl.ds(step * fc, fc), :], out_sem.at[2])]
        pairs = fc // (2 * steps * r)
        at = pl.ds(steps * r, steps * r)
        return [
            pltpu.make_async_copy(stage_down.at[s], dest.at[pl.ds(step * pairs, pairs), at, :], out_sem.at[2 + s])
            for s, dest in enumerate((keep_hbm, send_hbm))
        ]

    def out_copies():
        if not split:
            return [pltpu.make_async_copy(stage_out, keep_hbm.at[steps], out_sem.at[4])]
        at = pl.ds(2 * steps * r, r)
        return [
            pltpu.make_async_copy(stage_out.at[s], dest.at[:, at, :], out_sem.at[4 + s])
            for s, dest in enumerate((keep_hbm, send_hbm))
        ]

    def put(stage, value, owners):
        if not split:
            stage[...] = value.astype(bf16)
            return
        keep, send = split_cores(value, core, owners)
        stage[0] = keep.astype(bf16)
        stage[1] = send.astype(bf16)

    @pl.when(j == 0)
    def _():
        copies = ffn_copies(idx_ref, pieces, wo, up, down, sem)
        for c in copies:
            c.start()
        for c in copies:
            c.wait()
        for i in range(tiles):
            rs = pl.ds(i * TILE, TILE)
            start = x_ref[rs, :].astype(f32) + t_ref[rs, :] * vec_ref[0:1, :]
            middle = start + dot(att_ref[rs, :], wo[...]) + vec_ref[1:2, :]
            mid[rs, :] = middle
            normed = (ln_parts(middle)[0] * vec_ref[2:3, :] + vec_ref[3:4, :]).astype(bf16)
            n2[rs, :] = normed
            n2t[:, i * TILE : (i + 1) * TILE] = normed.T

    f0 = pl.multiple_of(j * fc, fc)
    up_c = up[:, pl.ds(f0, fc)]
    down_c = down[pl.ds(f0, fc), :]
    upb = upb_ref[...]
    gb = jnp.zeros((1, fc), f32)
    for i in range(tiles):
        rs = pl.ds(i * TILE, TILE)
        pre = dot(n2[rs, :], up_c) + upb
        gh = dot(cot_ref[rs, :], down_c, NT)
        h, slope = gelu_parts(pre)
        h = h.astype(bf16)
        g = (gh * slope).astype(bf16)
        hid[rs, :] = h
        gp[rs, :] = g
        gb = gb + rows_sum(g.astype(f32))
        o = dot(h, down_c)
        b = dot(g, up_c, NT)

        @pl.when(j == 0)
        def _():
            acc[rs, :] = o
            gn2[rs, :] = b

        @pl.when(j > 0)
        def _():
            acc[rs, :] += o
            gn2[rs, :] += b

    gupb_ref[...] = gb

    @pl.when(j > 0)
    def _():
        for c in up_copies(j - 1) + down_copies(j - 1):
            c.wait()

    put(stage_down, dot(hid[...], cot_ref[...], TN), 2 * (fc // (2 * steps * r)) if split else 0)
    for c in down_copies(j):
        c.start()
    put(stage_up, dot(n2t[...], gp[...]), split)
    for c in up_copies(j):
        c.start()

    @pl.when(j == steps - 1)
    def _():
        sums = [jnp.zeros((1, width), f32)] * 4
        for i in range(tiles):
            rs = pl.ds(i * TILE, TILE)
            middle = mid[rs, :]
            out_ref[rs, :] = (middle + acc[rs, :] + vec_ref[4:5, :]).astype(bf16)
            xhat, rstd = ln_parts(middle)
            dn = gn2[rs, :]
            cot = cot_ref[rs, :].astype(f32)
            gm = cot + ln_back(xhat, rstd, dn, vec_ref[2:3, :])
            mid[rs, :] = gm
            ga = gm.astype(bf16)
            hid[rs, :] = ga
            ga_ref[rs, :] = dot(ga, wo[...], NT).astype(bf16)
            sums = [s + rows_sum(v) for s, v in zip(sums, (dn * xhat, dn, cot, ga.astype(f32)))]
        gvec_ref[...] = jnp.concatenate(sums + [jnp.zeros((4, width), f32)], axis=0)
        mid_copy = pltpu.make_async_copy(mid, gm_hbm, out_sem.at[6])
        mid_copy.start()
        put(stage_out, dot(att_ref[...], hid[...], TN), split)
        last = out_copies()
        for c in last:
            c.start()
        for c in last + up_copies(j) + down_copies(j):
            c.wait()
        mid_copy.wait()


def ffn_both(idx, x, t, att, cot, vecs, upb, pieces, ff, split):
    rows, width = x.shape
    n = len(pieces)
    fc = width
    steps = ff // fc
    sd = jax.ShapeDtypeStruct
    V = pltpu.VMEM
    if split:
        half = split // 2
        r = width // split
        grads = [sd((half, (2 * steps + 1) * r, width), bf16)] * 2
        stages = [V((2, half, r, width), bf16), V((2, fc // (2 * steps * r), steps * r, width), bf16), V((2, half, r, width), bf16)]
    else:
        grads = [sd((steps + 1, width, width), bf16), sd((ff, width), bf16)]
        stages = [V((width, width), bf16)] * 3
    return pl.pallas_call(
        functools.partial(ffn_kernel, n, split, steps),
        grid_spec=pltpu.PrefetchScalarGridSpec(
            num_scalar_prefetch=1,
            grid=(steps,),
            in_specs=[whole_spec((rows, width)), whole_spec((rows, 1)), whole_spec((rows, width)), whole_spec((rows, width)),
                      whole_spec(vecs.shape), pl.BlockSpec((1, fc), lambda j, *_: (0, j))] + [any_spec()] * n,
            out_specs=[whole_spec((rows, width)), whole_spec((rows, width)), whole_spec((8, width)),
                       pl.BlockSpec((1, fc), lambda j, *_: (0, j)), any_spec(), any_spec(), any_spec()],
            scratch_shapes=[V((width, width), bf16), V((width, ff), bf16), V((ff, width), bf16),
                            V((rows, width), f32), V((rows, width), bf16), V((width, rows), bf16),
                            V((rows, width), f32), V((rows, width), f32),
                            V((rows, fc), bf16), V((rows, fc), bf16), *stages,
                            pltpu.SemaphoreType.DMA((6 * n,)), pltpu.SemaphoreType.DMA((7,))],
        ),
        out_shape=[sd((rows, width), bf16), sd((rows, width), bf16), sd((8, width), f32), sd((1, ff), f32),
                   sd((rows, width), f32), *grads],
        compiler_params=params(),
        cost_estimate=cost(60),
        name="ffn_both",
    )(idx, x, t, att, cot, vecs, upb, *pieces)


def gqkv_kernel(split, idx_ref, normed_ref, gp_ref, *rest):
    outs, nt = rest[:-1], rest[-1]

    @pl.when(pl.program_id(0) == 0)
    def _():
        nt[...] = normed_ref[...].T

    grad = dot(nt[...], gp_ref[...])
    if split:
        keep, send = split_cores(grad, lax.rem(idx_ref[0], 2), split)
        outs[0][...] = keep.astype(bf16)
        outs[1][...] = send.astype(bf16)
    else:
        outs[0][0] = grad.astype(bf16)


def qkv_weight_grad(idx, normed, gp, split):
    rows, width = normed.shape
    sd = jax.ShapeDtypeStruct
    if split:
        half, r = split // 2, width // split
        out_specs = [pl.BlockSpec((half, r, width), lambda j, *_: (0, j, 0))] * 2
        out_shape = [sd((half, 3 * r, width), bf16)] * 2
    else:
        out_specs = [pl.BlockSpec((1, width, width), lambda j, *_: (j, 0, 0))]
        out_shape = [sd((3, width, width), bf16)]
    return pl.pallas_call(
        functools.partial(gqkv_kernel, split),
        grid_spec=pltpu.PrefetchScalarGridSpec(
            num_scalar_prefetch=1,
            grid=(3,),
            in_specs=[whole_spec((rows, width)), pl.BlockSpec((rows, width), lambda j, *_: (0, j))],
            out_specs=out_specs,
            scratch_shapes=[pltpu.VMEM((width, rows), bf16)],
        ),
        out_shape=out_shape,
        compiler_params=params(),
        cost_estimate=cost(8),
        name="qkv_weight_grad",
    )(idx, normed, gp)


def first_kernel(n, idx_ref, x_ref, t_ref, gm_ref, gp_ref, vec_ref, *rest):
    pieces, (gi_ref, gvec_ref, w_scr, sem) = rest[:n], rest[n:]
    i = pl.program_id(0)
    width = x_ref.shape[1]

    @pl.when(i == 0)
    def _():
        for c in qkv_copies(idx_ref, pieces, w_scr, sem):
            c.start()
        gvec_ref[...] = jnp.zeros_like(gvec_ref)
        for c in qkv_copies(idx_ref, pieces, w_scr, sem):
            c.wait()

    t = t_ref[...]
    dn = dot(gp_ref[...], w_scr[...], NT)
    start = x_ref[...].astype(f32) + t * vec_ref[0:1, :]
    xhat, rstd = ln_parts(start)
    gs = gm_ref[...] + ln_back(xhat, rstd, dn, vec_ref[1:2, :])
    gi_ref[...] = gs.astype(bf16)
    parts = [t * gs, dn * xhat, dn, gp_ref[:, :width].astype(f32), gp_ref[:, 2 * width :].astype(f32)]
    gvec_ref[...] += jnp.concatenate([rows_sum(v) for v in parts] + [jnp.zeros((3, width), f32)], axis=0)


def first_backward(idx, x, t, gm, gp, vecs, pieces):
    rows, width = x.shape
    n = len(pieces)
    sd = jax.ShapeDtypeStruct
    return pl.pallas_call(
        functools.partial(first_kernel, n),
        grid_spec=pltpu.PrefetchScalarGridSpec(
            num_scalar_prefetch=1,
            grid=(rows // TILE,),
            in_specs=[row_spec(width), row_spec(1), row_spec(width), row_spec(3 * width), whole_spec(vecs.shape)] + [any_spec()] * n,
            out_specs=[row_spec(width), whole_spec((8, width))],
            scratch_shapes=[pltpu.VMEM((width, 3 * width), bf16), pltpu.SemaphoreType.DMA((n,))],
        ),
        out_shape=[sd((rows, width), bf16), sd((8, width), f32)],
        compiler_params=params(),
        cost_estimate=cost(11),
        name="first_backward",
    )(idx, x, t, gm, gp, vecs, *pieces)


SHARDS = 8


def swap(value, axis, size, bit_mask):
    return lax.ppermute(value, axis, [(i, i ^ bit_mask) for i in range(size)])


def near(value):
    return swap(value, "fsdp", SHARDS, 1)


def along_x(value):
    return swap(value, "fsdp", SHARDS, 2)


def along_y(value):
    return swap(value, "fsdp", SHARDS, 4)


def with_near(far):
    pieces = []
    for piece in far:
        pieces += [piece, near(piece)]
    return pieces


def in_order(pieces, order):
    stacked = jnp.stack(pieces).astype(f32)
    hit = (jnp.arange(len(pieces))[:, None] == order[None, :]).astype(f32)
    return jnp.sum(hit.reshape(hit.shape + (1,) * (stacked.ndim - 1)) * stacked[None], axis=1)


def blocks_of(weight, width):
    r = weight.shape[0]
    return jnp.transpose(weight.reshape(r, -1, width), (1, 0, 2)).reshape(-1, width)


def far_first(kept, came, spot):
    place = spot // 2
    cut = kept.shape[1] // 32 * 16

    def total(mask, rows):
        pick = lambda v: lax.dynamic_index_in_dim(v, place ^ mask, 0, keepdims=False)[rows].astype(f32)
        return (pick(kept) + pick(came)).astype(kept.dtype)

    top, low = slice(None, cut), slice(cut, None)
    stay = (total(0, top), total(2, top), total(0, low), total(1, low))
    go_x = jnp.stack([total(1, top), total(3, top)])
    go_y = jnp.stack([total(2, low), total(3, low)])
    return stay, go_x, go_y


def add_low(a, b):
    return (a.astype(f32) + b.astype(f32)).astype(a.dtype)


def far_second(stay, from_x, from_y):
    own_top, y_top, own_low, x_low = stay
    return (add_low(own_top, from_x[0]), add_low(own_low, from_y[0])), add_low(y_top, from_x[1]), add_low(x_low, from_y[1])


def far_third(own, from_y, from_x):
    return jnp.concatenate([add_low(own[0], from_y), add_low(own[1], from_x)])


def halves(owned, spot):
    parts = owned.reshape(2, owned.shape[0] // 2, owned.shape[1])
    side = spot % 2
    return (
        lax.dynamic_index_in_dim(parts, side, 0, keepdims=False),
        lax.dynamic_index_in_dim(parts, 1 - side, 0, keepdims=False),
    )


def rows_first(kept, sent, size):
    return add_low(kept, swap(sent, "dp", size, 1))


def rows_middle(half, size):
    step = 2
    while step < size:
        half = add_low(half, swap(half, "dp", size, step))
        step *= 2
    return half


def rows_last(half, size, spot):
    other = swap(half, "dp", size, 1)
    even = spot % 2 == 0
    return jnp.concatenate([jnp.where(even, half, other), jnp.where(even, other, half)]).astype(f32)


def on_device(
    sizes,
    inputs,
    time_of_row,
    coords,
    segment_ids,
    cotangent,
    time_weight,
    ln1_gain,
    ln1_bias,
    w_qkv,
    q_bias,
    v_bias,
    w_out,
    out_bias,
    kernel_mean,
    kernel_width,
    kernel_map,
    ln2_gain,
    ln2_bias,
    w_up,
    up_bias,
    w_down,
    down_bias,
):
    n, planes = sizes
    direct = n == SHARDS
    split = n if direct else 0
    barrier = lax.optimization_barrier
    spot = lax.axis_index("fsdp")
    level = lax.axis_index("dp")
    order = (spot ^ jnp.arange(n)).astype(jnp.int32)
    width = inputs.shape[1]
    r = w_qkv.shape[0]
    heads = kernel_map.shape[1]
    own_kernels = kernel_map.shape[0]
    kernels = own_kernels * n
    wide = up_bias.shape[0] // r
    ff = n * wide * r
    scale = (width // heads) ** (-0.5)
    times = time_of_row[:, None]

    flat = jnp.concatenate([kernel_map.reshape(-1), kernel_mean, kernel_width])
    kernel_rows = -(-flat.shape[0] // r)
    flat = jnp.pad(flat, (0, kernel_rows * r - flat.shape[0])).reshape(kernel_rows, r)
    vectors = (time_weight, ln1_gain, ln1_bias, q_bias, v_bias, out_bias, ln2_gain, ln2_bias, down_bias)
    small = jnp.concatenate([jnp.stack(vectors), up_bias.reshape(wide, r), flat])
    if direct:
        small_all = [small] + [swap(small, "fsdp", n, m) for m in range(1, n)]
        qkv_far = [w_qkv] + [swap(w_qkv, "fsdp", n, 2 * m) for m in range(1, n // 2)]
        top = jnp.concatenate([w_out, blocks_of(w_up, width)])
        small_all = in_order(small_all, order)
    else:
        small_all = lax.all_gather(small, "fsdp", axis=0).astype(f32)
        qkv_p = (lax.all_gather(w_qkv, "fsdp", axis=0, tiled=True),)
        ffn_p = tuple(lax.all_gather(w, "fsdp", axis=0, tiled=True) for w in (w_out, w_up, w_down))
    vecs = jnp.transpose(small_all[:, :9], (1, 0, 2)).reshape(9, width)
    up_bias_all = small_all[:, 9 : 9 + wide].reshape(1, ff)
    tail = small_all[:, 9 + wide :].reshape(n, kernel_rows * r)
    map_size = own_kernels * heads
    map_all = tail[:, :map_size].reshape(kernels, heads).astype(bf16)
    mean_all = tail[:, map_size : map_size + own_kernels].reshape(kernels)
    width_all = tail[:, map_size + own_kernels : map_size + 2 * own_kernels].reshape(kernels)

    def rows_of(*picked):
        return jnp.concatenate([vecs[p : p + 1] for p in picked] + [jnp.zeros((8 - len(picked), width), f32)])

    aux_win, aux_col = aux_of(coords, segment_ids)
    consts, spread_map = kernel_consts(mean_all, width_all, map_all)
    bias = attn_bias(aux_win, aux_col, consts, spread_map.T)

    if direct:
        bias, qkv_far, top, bottom = barrier((bias, qkv_far, top, w_down))
        top_x, top_y, low_x, low_y = along_x(top), along_y(top), along_x(bottom), along_y(bottom)
        qkv_p = tuple(with_near(qkv_far))
    normed, queries, keys, values = qkv_forward(order, inputs, times, rows_of(0, 1, 2, 3, 4), qkv_p, scale)
    done = attn_fwd(0, queries, keys, values, bias, ())
    done = attn_fwd(1, queries, keys, values, bias, done)
    if direct:
        done, top_x, top_y, low_x, low_y = barrier((done, top_x, top_y, low_x, low_y))
        top_d, low_d = along_y(top_x), along_x(low_y)
    done = attn_fwd(2, queries, keys, values, bias, done)
    if direct:
        done, top_d, low_d = barrier((done, top_d, low_d))
        ffn_p = tuple(with_near((top, top_x, top_y, top_d)) + with_near((bottom, low_x, low_y, low_d)))
    attended, probs = attn_fwd(3, queries, keys, values, bias, done)

    output, grad_attended, ffn_vecs, grad_up_bias, grad_middle, ffn_keep, ffn_send = ffn_both(
        order, inputs, times, attended, cotangent, rows_of(0, 5, 6, 7, 8), up_bias_all, ffn_p, ff, split
    )

    def backward(part, before):
        return attn_bwd(part, queries, grad_attended, keys, values, probs, scale, before)

    def feat(part, before):
        return attn_feat(part, grad_scores, aux_win, aux_col, consts, spread_map, before)

    def by_owner(array, blocks):
        return array.reshape(blocks, n, -1, width)

    def scattered(array, blocks):
        owned = lax.psum_scatter(by_owner(array, blocks), "fsdp", scatter_dimension=1)
        return owned.reshape(-1, width)

    if direct:
        ffn_came = near(ffn_send)
        done = backward(0, ())
        stay, go_x, go_y = far_first(ffn_keep, ffn_came, spot)
        done, stay, go_x, go_y = barrier((done, stay, go_x, go_y))
        from_x, from_y = along_x(go_x), along_y(go_y)
        done = backward(2, backward(1, done))
        own, go_y, go_x = far_second(stay, from_x, from_y)
        done, own, go_y, go_x = barrier((done, own, go_y, go_x))
        from_y, from_x = along_y(go_y), along_x(go_x)
        grad_projected, grad_scores = backward(3, done)
        ffn_z = halves(far_third(own, from_y, from_x), level)
        grad_projected, ffn_z = barrier((grad_projected, ffn_z))
        ffn_z = rows_first(*ffn_z, planes)
        qkv_keep, qkv_send = qkv_weight_grad(order, normed, grad_projected, split)
        stay, go_x, go_y = far_first(qkv_keep, near(qkv_send), spot)
        grad_projected, stay, go_x, go_y = barrier((grad_projected, stay, go_x, go_y))
        from_x, from_y = along_x(go_x), along_y(go_y)
    else:
        done = backward(2, backward(1, backward(0, ())))
        grad_projected, grad_scores = backward(3, done)
        ffn_owned = jnp.concatenate([scattered(ffn_keep[:wide], wide), scattered(ffn_send, 1), scattered(ffn_keep[wide:], 1)])
        ffn_z = rows_first(*halves(ffn_owned, level), planes)
        qkv_owned = scattered(qkv_weight_grad(order, normed, grad_projected, split)[0], 3)
    grad_inputs, first_vecs = first_backward(
        order, inputs, times, grad_middle, grad_projected, rows_of(0, 1), qkv_p
    )
    if direct:
        own, go_y, go_x = far_second(stay, from_x, from_y)
        grad_scores, first_vecs, ffn_z, own, go_y, go_x = barrier((grad_scores, first_vecs, ffn_z, own, go_y, go_x))
        from_y, from_x = along_y(go_y), along_x(go_x)
    ffn_z = rows_middle(ffn_z, planes)
    sums = feat(0, ())
    if direct:
        qkv_owned = far_third(own, from_y, from_x)
    sums, qkv_z = barrier((sums, halves(qkv_owned, level)))
    qkv_z = rows_first(*qkv_z, planes)
    sums = feat(1, sums)
    sums, ffn_z, qkv_z = barrier((sums, ffn_z, qkv_z))
    ffn_owned = rows_last(ffn_z, planes, level)
    qkv_z = rows_middle(qkv_z, planes)
    sums = feat(2, sums)
    sums, qkv_z, ffn_owned = barrier((sums, qkv_z, ffn_owned))
    qkv_owned = rows_last(qkv_z, planes, level)
    grad_map, grad_mean, grad_width = feat_finish(*feat(3, sums), width_all, map_all)

    grad_rows = [first_vecs[:5], ffn_vecs[3:4], ffn_vecs[:3]]
    flat = jnp.concatenate(
        [grad_map.reshape(n, map_size), grad_mean.reshape(n, own_kernels), grad_width.reshape(n, own_kernels)], axis=1
    )
    flat = jnp.pad(flat, ((0, 0), (0, kernel_rows * r - flat.shape[1]))).reshape(n, kernel_rows, r)
    vector_rows = jnp.transpose(jnp.concatenate(grad_rows).reshape(9, n, r), (1, 0, 2))
    packed = jnp.concatenate([vector_rows, grad_up_bias.reshape(n, wide, r), flat], axis=1)
    if direct:
        total = lax.dynamic_index_in_dim(packed, spot, 0, keepdims=False)
        for m in range(1, n):
            total = total + swap(lax.dynamic_index_in_dim(packed, spot ^ m, 0, keepdims=False), "fsdp", n, m)
    else:
        total = lax.psum_scatter(packed, "fsdp", scatter_dimension=0)
    step = 1
    while step < planes:
        total = total + swap(total, "dp", planes, step)
        step *= 2
    tail = total[9 + wide :].reshape(-1)
    up_rows = wide * r
    grad_up, grad_down, grad_out = ffn_owned[:up_rows], ffn_owned[up_rows : 2 * up_rows], ffn_owned[2 * up_rows :]

    def columns(array):
        return jnp.transpose(array.reshape(-1, r, width), (1, 0, 2)).reshape(r, -1)

    return (
        output,
        grad_inputs,
        total[0],
        total[1],
        total[2],
        columns(qkv_owned),
        total[3],
        total[4],
        grad_out,
        total[5],
        tail[map_size : map_size + own_kernels],
        tail[map_size + own_kernels : map_size + 2 * own_kernels],
        tail[:map_size].reshape(own_kernels, heads),
        total[6],
        total[7],
        columns(grad_up),
        total[9 : 9 + wide].reshape(up_rows),
        grad_down,
        total[8],
    )


def solution(mesh):
    rows, split, whole = P(("fsdp", "dp"), None), P("fsdp"), P("fsdp", None)
    placed = (
        rows,
        P(("fsdp", "dp")),
        P(None, ("fsdp", "dp")),
        P(("fsdp", "dp")),
        rows,
        split,
        split,
        split,
        whole,
        split,
        split,
        whole,
        split,
        split,
        split,
        whole,
        split,
        split,
        whole,
        split,
        whole,
        split,
    )
    out_placed = (
        rows,
        rows,
        split,
        split,
        split,
        whole,
        split,
        split,
        whole,
        split,
        split,
        split,
        whole,
        split,
        split,
        whole,
        split,
        whole,
        split,
    )
    return jax.shard_map(
        functools.partial(on_device, (mesh.shape["fsdp"], mesh.shape["dp"])),
        mesh=mesh,
        in_specs=placed,
        out_specs=out_placed,
        check_vma=False,
    )
```

```python
import functools, math
import jax, jax.numpy as jnp
from jax import lax
from jax.experimental import pallas as pl
from jax.experimental.pallas import tpu as pltpu
from jax.sharding import PartitionSpec as P

SET = 256
CH = 32
STEP = 4
UNROLL = 4
PAIR = 4
FEAT_STEP = 2
WIN = 128
GROUPS = ((0, 0), (128, 8), (384, 16), (512, 24))
HW = 24
VM = 60 * 1024 * 1024
f32, bf16 = jnp.float32, jnp.bfloat16
NT = (((1,), (1,)), ((), ()))
TN = (((0,), (0,)), ((), ()))


def dot(a, b, dims=(((1,), (0,)), ((), ()))):
    return lax.dot_general(a, b, dims, preferred_element_type=f32)


def spread_heads(block, lane0, h0):
    wide = block.astype(f32)
    lanes = lax.broadcasted_iota(jnp.int32, (8, 256), 1) + lane0
    masks = [(lanes >= h * HW) & (lanes < (h + 1) * HW) for h in range(h0, h0 + 8)]
    zero = jnp.zeros((8, 256), f32)
    parts = [jnp.where(m, wide[8 * g : 8 * g + 8], zero) for g in range(4) for m in masks]
    return jnp.concatenate(parts, axis=0).astype(bf16)


def own_rows(full, lane0, h0):
    lanes = lax.broadcasted_iota(jnp.int32, (8, 256), 1) + lane0
    groups = []
    for g in range(4):
        out = jnp.zeros((8, 256), f32)
        for h in range(8):
            m = (lanes >= (h0 + h) * HW) & (lanes < (h0 + h + 1) * HW)
            out = jnp.where(m, full[64 * g + 8 * h : 64 * g + 8 * h + 8], out)
        groups.append(out)
    return jnp.concatenate(groups, axis=0)


def window_start(i):
    per = SET // CH
    base = i // per * SET
    return pl.multiple_of(jnp.clip(i * CH - 48, base, base + SET - WIN), 16)


def radius_of(ac, aw):
    d = ac[:, 0:1] - aw[0:1, :]
    s = d * d
    for j in (1, 2):
        d = ac[:, j : j + 1] - aw[j : j + 1, :]
        s = s + d * d
    return jnp.sqrt(s)


def per_chunk(body, unroll):
    if STEP == unroll:
        for t in range(STEP):
            body(t)
        return

    @pl.loop(0, STEP // unroll)
    def _(s):
        for t in range(unroll):
            body(s * unroll + t)


def chunk_rows(t):
    return pl.ds(pl.multiple_of(t * CH, CH), CH)


def parts3(v):
    high = v.astype(bf16).astype(f32)
    rest = v - high
    middle = rest.astype(bf16).astype(f32)
    return high, middle, (rest - middle).astype(bf16).astype(f32)


def distance_rows(ac, aw):
    rho = radius_of(ac, aw)
    rho = jnp.concatenate([rho[8 * g : 8 * g + 8] for g in range(4)], axis=1)
    (sh, sm, sl), (h, m, l) = parts3(rho * rho), parts3(rho)
    one = jnp.ones_like(rho)
    slots = [sh, sh, sm, sm, sh, sl, h, h, m, m, h, l, one, one, one, jnp.zeros_like(rho)]
    return jnp.concatenate(slots, axis=0).astype(bf16)


def bias_kernel(aw_ref, ac_ref, gmat_ref, bmat_ref, b_ref, f_ref, t_scr):
    @pl.loop(0, STEP // PAIR)
    def _(s):
        chunks = [s * PAIR + u for u in range(PAIR)]
        ac = [ac_ref[chunk_rows(t), :] for t in chunks]
        aw = [aw_ref[t] for t in chunks]
        dist = [distance_rows(a, w) for a, w in zip(ac, aw)]
        e = [dot(gmat_ref[...], d) for d in dist]
        f = [jnp.exp2(v).astype(bf16) for v in e]
        bias = [dot(bmat_ref[...], v) for v in f]
        for u, t in enumerate(chunks):
            f_ref[t] = f[u]
            joined = ac[u][:, 3:4] == aw[u][3:4, :]
            for g in range(4):
                part = bias[u][:, 128 * g : 128 * g + 128].reshape(32, 8, WIN)
                part = jnp.where(joined[8 * g : 8 * g + 8][None], part, -1e30)
                for q in range(4):
                    t_scr[u, 256 * q + 64 * g : 256 * q + 64 * g + 64, :] = part[8 * q : 8 * q + 8].reshape(64, WIN)
        for u, t in enumerate(chunks):
            for n in range(8):
                b_ref[t, :, 128 * n : 128 * n + 128] = t_scr[u, 128 * n : 128 * n + 128, :].T


def fwd_kernel(q_ref, k_ref, v_ref, b_ref, o_ref, p_ref):
    def chunk(t):
        w = window_start(pl.program_id(0) * STEP + t)
        rt = chunk_rows(t)
        kwin = k_ref[pl.ds(w, WIN), :]
        vwin = v_ref[pl.ds(w, WIN), :]
        spans = [slice(lane0, lane0 + 256) for lane0, _ in GROUPS]
        wide = [spread_heads(q_ref[rt, sl], lane0, h0) for sl, (lane0, h0) in zip(spans, GROUPS)]
        s = [dot(kwin[:, sl], qm, NT) + b_ref[t, :, 256 * j : 256 * j + 256] for j, (sl, qm) in enumerate(zip(spans, wide))]
        e = [jnp.exp(v - jnp.max(v, axis=0, keepdims=True)) for v in s]
        pr = [(v * (1.0 / jnp.sum(v, axis=0, keepdims=True))).astype(bf16) for v in e]
        full = [dot(v, vwin[:, sl], TN) for sl, v in zip(spans, pr)]
        acc = [own_rows(v, *GROUPS[j]) for j, v in enumerate(full)]
        for j, v in enumerate(pr):
            p_ref[t, :, 256 * j : 256 * j + 256] = v
        store_lanes(o_ref, rt, acc)

    per_chunk(chunk, UNROLL)


def store_lanes(ref, rows, acc):
    for half in range(2):
        a, b = acc[2 * half], acc[2 * half + 1]
        full = jnp.concatenate([a[:, :128], a[:, 128:] + b[:, :128], b[:, 128:]], axis=1)
        ref[rows, 384 * half : 384 * half + 384] = full.astype(bf16)


def bwd_kernel(q_ref, do_ref, k_ref, v_ref, p_ref, gp_ref, ds_ref, dk_scr, dv_scr, *, scale):
    i = pl.program_id(0)
    width = 32 * HW

    @pl.when(i == 0)
    def _():
        dk_scr[...] = jnp.zeros_like(dk_scr)
        dv_scr[...] = jnp.zeros_like(dv_scr)

    def chunk(t):
        w = window_start(i * STEP + t)
        rt = chunk_rows(t)
        kwin = k_ref[pl.ds(w, WIN), :]
        vwin = v_ref[pl.ds(w, WIN), :]
        left = lax.broadcasted_iota(jnp.int32, (WIN, 128), 1) < 64
        spans = [slice(lane0, lane0 + 256) for lane0, _ in GROUPS]
        qm = [spread_heads(q_ref[rt, sl], lane0, h0) for sl, (lane0, h0) in zip(spans, GROUPS)]
        dom = [spread_heads(do_ref[rt, sl], lane0, h0) for sl, (lane0, h0) in zip(spans, GROUPS)]
        p_low = [p_ref[t, :, 256 * j : 256 * j + 256] for j in range(4)]
        dp = [dot(vwin[:, sl], v, NT) for sl, v in zip(spans, dom)]
        dv = [dot(a, b) for a, b in zip(p_low, dom)]
        pf = [v.astype(f32) for v in p_low]
        pd = [a * b for a, b in zip(pf, dp)]
        ds = [a - b * jnp.sum(a, axis=0, keepdims=True) for a, b in zip(pd, pf)]
        ds_low = [v.astype(bf16) for v in ds]
        full = [dot(v, kwin[:, sl], TN) for sl, v in zip(spans, ds_low)]
        dk = [dot(a, b) for a, b in zip(ds_low, qm)]
        acc = [own_rows(v, *GROUPS[j]) * scale for j, v in enumerate(full)]
        for j in (0, 2):
            for p in range(2):
                a, b = (ds[j + t][:, 128 * p : 128 * p + 128] for t in range(2))
                at = slice(64 * j, 64 * j + 128)
                ds_ref[t, 256 * p : 256 * p + WIN, at] = jnp.where(left, a, pltpu.roll(b, 64, 1)).astype(bf16)
                ds_ref[t, 256 * p + WIN : 256 * p + 256, at] = jnp.where(left, pltpu.roll(a, 64, 1), b).astype(bf16)
        for scr, parts in ((dk_scr, dk), (dv_scr, dv)):
            for half in range(2):
                a, b = parts[2 * half : 2 * half + 2]
                both = jnp.concatenate([a[:, :128], a[:, 128:] + b[:, :128], b[:, 128:]], axis=1)
                scr[pl.ds(w, WIN), 384 * half : 384 * half + 384] += both
        store_lanes(gp_ref, pl.ds(pl.multiple_of((i * STEP + t) * CH, CH), CH), acc)

    per_chunk(chunk, UNROLL)

    @pl.when(i == pl.num_programs(0) - 1)
    def _():
        gp_ref[:, width : 2 * width] = dk_scr[...].astype(bf16)
        gp_ref[:, 2 * width :] = dv_scr[...].astype(bf16)


def feat_kernel(n_before, last, ds_ref, f_ref, aw_ref, ac_ref, amat_ref, kcol_ref, *rest):
    before, (m0_ref, s_ref, *out_ref, rho_scr, gf_scr) = rest[:n_before], rest[n_before:]

    @pl.when(pl.program_id(0) == 0)
    def _():
        m0_ref[...] = before[0][...] if before else jnp.zeros_like(m0_ref)
        s_ref[...] = before[1][...] if before else jnp.zeros_like(s_ref)

    for u in range(FEAT_STEP):
        t = u
        rho = radius_of(ac_ref[chunk_rows(t), :], aw_ref[t])
        rho_scr[u] = jnp.concatenate([rho[8 * g : 8 * g + 8] for g in range(4)], axis=1)
    for u in range(FEAT_STEP):
        t = u
        for rb in range(4):
            span = slice(256 * rb, 256 * rb + 256)
            gf_scr[u, span, :] = dot(amat_ref[span, :], ds_ref[t], NT)
            m0_ref[span, :] += dot(f_ref[t, span, :], ds_ref[t])
            for kt in range(8):
                ks = slice(16 * kt, 16 * kt + 16)
                s1, s2 = s_ref[0, ks, :], s_ref[1, ks, :]
                for r in (2 * rb, 2 * rb + 1):
                    for g in range(4):
                        at = (u, slice(128 * r + 16 * kt, 128 * r + 16 * kt + 16), slice(128 * g, 128 * g + 128))
                        rr = rho_scr[u, r : r + 1, 128 * g : 128 * g + 128]
                        w = gf_scr[at] * f_ref[t, at[1], at[2]].astype(f32) * rr
                        s1 = s1 + w
                        s2 = s2 + w * rr
                s_ref[0, ks, :] = s1
                s_ref[1, ks, :] = s2

    if last:

        @pl.when(pl.program_id(0) == pl.num_programs(0) - 1)
        def _():
            out_ref[0][...] = kernel_grads(m0_ref, s_ref, kcol_ref[...])


def kernel_grads(m0_ref, s_ref, kcol):
    n = kcol.shape[0]
    lanes = lax.broadcasted_iota(jnp.int32, (n, 256), 1)
    m = jnp.zeros((n, 256), f32)
    for r in range(8):
        m = jnp.where(lanes % 8 == r, m0_ref[n * r : n * r + n, :], m)
    heads = lax.broadcasted_iota(jnp.int32, (256, 128), 0) // 8 == lax.broadcasted_iota(jnp.int32, (256, 128), 1)
    heads = heads.astype(f32).astype(bf16)
    g_map = sum(dot(v.astype(bf16), heads) for v in parts3(m))
    lanes = lanes[:, :128]
    s0 = jnp.sum(jnp.where(lanes < 32, g_map * kcol, 0.0), axis=-1, keepdims=True)
    s1 = jnp.sum(s_ref[0], axis=-1, keepdims=True)
    s2 = jnp.sum(s_ref[1], axis=-1, keepdims=True)
    mean, width = kcol[:, 32:33], kcol[:, 33:34]
    square = width * width
    g_mean = (s1 - mean * s0) / square
    g_width = ((s2 - 2.0 * mean * s1 + mean * mean * s0) / square - s0) / width
    return jnp.where(lanes == 32, g_mean, jnp.where(lanes == 33, g_width, g_map))


def cost(micros):
    return pl.CostEstimate(flops=int(micros * 1.1535e9), bytes_accessed=0, transcendentals=0)


def full_spec(shape):
    return pl.BlockSpec(shape, lambda i: (0,) * len(shape))


def params(limit=VM):
    return pltpu.CompilerParams(vmem_limit_bytes=limit, dimension_semantics=("arbitrary",))


BIAS_PARTS = 2
FWD_PARTS = 2
BWD_PARTS = 4
FEAT_PARTS = 4


def shifted(spec_shape, base):
    return pl.BlockSpec(spec_shape, lambda i: (i + base,) + (0,) * (len(spec_shape) - 1))


def half_spec(shape, part):
    return pl.BlockSpec(shape, lambda i: (part,) + (0,) * (len(shape) - 1))


def attn_bias(part, aw, ac, gmat, bmat, before):
    c = aw.shape[0]
    per = c // BIAS_PARTS // STEP
    base = part * per
    n_in = 4
    return pl.pallas_call(
        functools.partial(skip_refs, bias_kernel, n_in, len(before)),
        grid=(per,),
        in_specs=[
            shifted((STEP, 8, WIN), base), shifted((STEP * CH, 4), base), full_spec(gmat.shape), full_spec(bmat.shape),
        ] + [pl.BlockSpec(memory_space=pl.ANY)] * len(before),
        out_specs=[shifted((STEP, WIN, 1024), base), shifted((STEP, 1024, 4 * WIN), base)],
        out_shape=[jax.ShapeDtypeStruct((c, WIN, 1024), f32), jax.ShapeDtypeStruct((c, 1024, 4 * WIN), bf16)],
        scratch_shapes=[pltpu.VMEM((PAIR, 1024, WIN), f32)],
        input_output_aliases={n_in + t: t for t in range(len(before))},
        compiler_params=params(),
        cost_estimate=cost(24 // BIAS_PARTS),
        name="attn_bias",
    )(aw, ac, gmat, bmat, *before)


def attn_fwd(part, q, k, v, bias, before):
    rows, width = q.shape
    c = rows // CH
    per = c // FWD_PARTS // STEP
    base = part * per
    kv = half_spec((rows // FWD_PARTS, width), part)
    n_in = 4
    return pl.pallas_call(
        functools.partial(skip_refs, fwd_kernel, n_in, len(before)),
        grid=(per,),
        in_specs=[shifted((STEP * CH, width), base), kv, kv, shifted((STEP, WIN, 1024), base)]
        + [pl.BlockSpec(memory_space=pl.ANY)] * len(before),
        out_specs=[shifted((STEP * CH, width), base), shifted((STEP, WIN, 1024), base)],
        out_shape=[jax.ShapeDtypeStruct((rows, width), bf16), jax.ShapeDtypeStruct((c, WIN, 1024), bf16)],
        input_output_aliases={n_in + t: t for t in range(len(before))},
        compiler_params=params(),
        cost_estimate=cost(16 // FWD_PARTS),
        name="attn_fwd",
    )(q, k, v, bias, *before)


def skip_refs(kernel, n_in, n_before, *refs):
    kernel(*refs[:n_in], *refs[n_in + n_before :])


def attn_bwd(part, q, do, k, v, p, scale, before):
    rows, width = q.shape
    c = rows // CH
    per = c // BWD_PARTS // STEP
    base = part * per
    kv = half_spec((rows // BWD_PARTS, width), part)
    n_in = 5
    return pl.pallas_call(
        functools.partial(skip_refs, functools.partial(bwd_kernel, scale=scale), n_in, len(before)),
        grid=(per,),
        in_specs=[
            shifted((STEP * CH, width), base), shifted((STEP * CH, width), base), kv, kv,
            shifted((STEP, WIN, 1024), base),
        ] + [pl.BlockSpec(memory_space=pl.ANY)] * len(before),
        out_specs=[half_spec((rows // BWD_PARTS, 3 * width), part), shifted((STEP, 4 * WIN, 256), base)],
        out_shape=[jax.ShapeDtypeStruct((rows, 3 * width), bf16), jax.ShapeDtypeStruct((c, 4 * WIN, 256), bf16)],
        scratch_shapes=[pltpu.VMEM((rows // BWD_PARTS, width), f32)] * 2,
        input_output_aliases={n_in + t: t for t in range(len(before))},
        compiler_params=params(),
        cost_estimate=cost(24 // BWD_PARTS),
        name="attn_bwd",
    )(q, do, k, v, p, *before)


def attn_feat(part, ds, feats, aw, ac, amat, kcol, before):
    per = ds.shape[0] // FEAT_PARTS // FEAT_STEP
    base = part * per
    last = part == FEAT_PARTS - 1
    n = kcol.shape[0]
    shapes = [(1024, 256), (2, n, WIN)] + [(n, 128)] * last
    return pl.pallas_call(
        functools.partial(feat_kernel, len(before), last),
        grid=(per,),
        in_specs=[
            shifted((FEAT_STEP, 4 * WIN, 256), base), shifted((FEAT_STEP, 1024, 4 * WIN), base),
            shifted((FEAT_STEP, 8, WIN), base), shifted((FEAT_STEP * CH, 4), base),
            full_spec(amat.shape), full_spec(kcol.shape),
        ] + [full_spec(b.shape) for b in before],
        out_specs=[full_spec(s) for s in shapes],
        out_shape=[jax.ShapeDtypeStruct(s, f32) for s in shapes],
        scratch_shapes=[pltpu.VMEM((FEAT_STEP, 8, 4 * WIN), f32), pltpu.VMEM((FEAT_STEP, 1024, 4 * WIN), f32)],
        compiler_params=params(),
        cost_estimate=cost(32 // FEAT_PARTS),
        name="attn_feat",
    )(ds, feats, aw, ac, amat, kcol, *before)


def aux_of(coords, segment_ids):
    rows = coords.shape[1]
    place = jnp.arange(rows, dtype=jnp.int32) // SET
    key = (segment_ids * (rows // SET) + place).astype(f32)
    packed = jnp.concatenate([coords, key[None], jnp.zeros((4, rows), f32)], axis=0)
    half = SET
    starts = [b + min(max(i - 48, 0), half - WIN) for b in range(0, rows, half) for i in range(0, half, CH)]
    aw = jnp.stack([packed[:, s : s + WIN] for s in starts])
    ac = packed[:4].T
    return aw, ac


def split3(v):
    high = lax.reduce_precision(v, 8, 7)
    middle = lax.reduce_precision(v - high, 8, 7)
    return high, middle, lax.reduce_precision(v - high - middle, 8, 7)


def kernel_consts(mean, width, kmap):
    mean, width = mean.astype(f32), width.astype(f32)
    half = 0.5 * math.log2(math.e) / (width * width)
    ah, am, al = split3(-half)
    bh, bm, bl = split3(2.0 * half * mean)
    ch, cm, cl = split3(-half * mean * mean - jnp.log2(math.sqrt(2.0 * math.pi) * width))
    slots = jnp.stack([ah, am, ah, am, al, ah, bh, bm, bh, bm, bl, bh, ch, cm, cl, jnp.zeros_like(ah)], axis=1)
    eye = jnp.eye(8, dtype=f32)
    n, heads = kmap.shape
    gmat = (eye[:, None, None, :] * slots[None, :, :, None]).reshape(8 * n, 128).astype(bf16)
    amat = (eye[:, None, None, :] * kmap.astype(f32)[None, :, :, None]).reshape(8 * n, heads * 8).astype(bf16)
    kcol = jnp.concatenate([kmap.astype(f32), mean[:, None], width[:, None], jnp.zeros((n, 94), f32)], axis=1)
    return gmat, amat, kcol


TILE = 256
epsilon = 1e-05


def ln_parts(v):
    mean = jnp.mean(v, axis=-1, keepdims=True)
    centred = v - mean
    rstd = lax.rsqrt(jnp.mean(centred * centred, axis=-1, keepdims=True) + epsilon)
    return centred * rstd, rstd


def ln_back(xhat, rstd, dn, gain):
    dg = dn * gain
    m1 = jnp.mean(dg, axis=-1, keepdims=True)
    m2 = jnp.mean(dg * xhat, axis=-1, keepdims=True)
    return rstd * (dg - m1 - xhat * m2)


def rows_sum(v):
    return jnp.sum(v, axis=0, keepdims=True)


def fetch(idx_ref, pieces, moves, sem, base=0):
    copies = []
    for m, (piece, top) in enumerate(pieces):
        for dest, first, column, rows, columns in moves:
            at = pl.multiple_of(idx_ref[m] * rows, 16)
            copies.append(
                pltpu.make_async_copy(
                    piece.at[pl.ds(top + first, rows), :],
                    dest.at[pl.ds(at, rows), pl.ds(column, columns)],
                    sem.at[base + len(copies)],
                )
            )
    return copies


def fetch_whole(arrays, dests, sem):
    return [pltpu.make_async_copy(a, d, sem.at[i]) for i, (a, d) in enumerate(zip(arrays, dests))]


def qkv_copies(idx_ref, pieces, w_scr, sem):
    if len(pieces) == 1:
        return fetch_whole(pieces, [w_scr], sem)
    r, columns = pieces[0].shape
    return fetch(idx_ref, [(p, 0) for p in pieces], [(w_scr, 0, 0, r, columns)], sem)


def ffn_copies(idx_ref, pieces, wo, up, down, sem):
    if len(pieces) == 3:
        copies = fetch_whole(pieces, [wo, up, down], sem)
        return copies[:1], copies[1:]
    width = wo.shape[0]
    n = len(pieces) - 2
    r = width // n
    wide = up.shape[1] // width
    cut = (1 + wide) * r
    tops = [(p, 0) for p in pieces[:n]]
    lows = [(p, cut) for p in pieces[: n - 2]] + [(p, 0) for p in pieces[n:]]
    first = fetch(idx_ref, tops, [(wo, 0, 0, r, width)], sem)
    moves = [(up, r + b * r, b * width, r, width) for b in range(wide)]
    later = fetch(idx_ref, tops, moves, sem, len(first))
    return first, later + fetch(idx_ref, lows, [(down, 0, 0, wide * r, width)], sem, len(first) + len(later))


def any_spec():
    return pl.BlockSpec(memory_space=pl.ANY)


def row_spec(width, tile=TILE):
    return pl.BlockSpec((tile, width), lambda i, *_: (i, 0))


def whole_spec(shape):
    return pl.BlockSpec(shape, lambda i, *_: (0,) * len(shape))


def qkv_kernel(n, scale, idx_ref, x_ref, t_ref, vec_ref, *rest):
    pieces, (normed_ref, q_ref, k_ref, v_ref, w_scr, sem) = rest[:n], rest[n:]
    width = x_ref.shape[1]

    @pl.when(pl.program_id(0) == 0)
    def _():
        for c in qkv_copies(idx_ref, pieces, w_scr, sem):
            c.start()

    start = x_ref[...].astype(f32) + t_ref[...] * vec_ref[0:1, :]
    normed = (ln_parts(start)[0] * vec_ref[1:2, :] + vec_ref[2:3, :]).astype(bf16)
    normed_ref[...] = normed

    @pl.when(pl.program_id(0) == 0)
    def _():
        for c in qkv_copies(idx_ref, pieces, w_scr, sem):
            c.wait()

    q_ref[...] = ((dot(normed, w_scr[:, :width]) + vec_ref[3:4, :]) * scale).astype(bf16)
    k_ref[...] = dot(normed, w_scr[:, width : 2 * width]).astype(bf16)
    v_ref[...] = (dot(normed, w_scr[:, 2 * width :]) + vec_ref[4:5, :]).astype(bf16)


def qkv_forward(idx, x, t, vecs, pieces, scale):
    rows, width = x.shape
    n = len(pieces)
    out = jax.ShapeDtypeStruct((rows, width), bf16)
    return pl.pallas_call(
        functools.partial(qkv_kernel, n, scale),
        grid_spec=pltpu.PrefetchScalarGridSpec(
            num_scalar_prefetch=1,
            grid=(rows // TILE,),
            in_specs=[row_spec(width), row_spec(1), whole_spec(vecs.shape)] + [any_spec()] * n,
            out_specs=[row_spec(width)] * 4,
            scratch_shapes=[pltpu.VMEM((width, 3 * width), bf16), pltpu.SemaphoreType.DMA((n,))],
        ),
        out_shape=[out] * 4,
        compiler_params=params(),
        cost_estimate=cost(10),
        name="qkv_forward",
    )(idx, x, t, vecs, *pieces)


def gelu_parts(x):
    a = jnp.abs(x)
    t = 1.0 / (1.0 + (0.3275911 * math.sqrt(0.5)) * a)
    e = jnp.exp(-0.5 * x * x)
    poly = t * (0.254829592 + t * (-0.284496736 + t * (1.421413741 + t * (-1.453152027 + t * 1.061405429))))
    tail = 0.5 * poly * e
    cdf = jnp.where(x >= 0, 1.0 - tail, tail)
    return x * cdf, cdf + x * e * (1.0 / math.sqrt(2.0 * math.pi))


def split_cores(value, core, owners):
    rows, c = value.shape
    pairs = value.reshape(owners // 2, 2, rows // owners, c)
    even, odd = pairs[:, 0], pairs[:, 1]
    return jnp.where(core == 0, even, odd), jnp.where(core == 0, odd, even)


def ffn_kernel(n, split, steps, idx_ref, x_ref, t_ref, att_ref, cot_ref, vec_ref, upb_ref, *rest):
    pieces = rest[:n]
    (out_ref, ga_ref, gvec_ref, gupb_ref, gm_hbm, keep_hbm, send_hbm,
     wo, up, down, mid, n2, acc, gn2, hid, gp, stage_up, stage_down, sem, out_sem, gm_sem) = rest[n:]
    j = pl.program_id(0)
    rows, width = x_ref.shape
    fc = hid.shape[1]
    tiles = rows // TILE
    core = lax.rem(idx_ref[0], 2)
    r = width // split if split else 0

    def moves(step):
        slot = lax.rem(step, 2)
        if not split:
            return [
                pltpu.make_async_copy(stage_up.at[slot], keep_hbm.at[step], out_sem.at[slot, 0]),
                pltpu.make_async_copy(stage_down.at[slot], send_hbm.at[pl.ds(step * fc, fc), :], out_sem.at[slot, 2]),
            ]
        pairs = fc // (2 * steps * r)
        up_at = pl.ds(pl.multiple_of(step * r, r), r)
        down_at = pl.ds(steps * r, steps * r)
        copies = []
        for s, dest in enumerate((keep_hbm, send_hbm)):
            copies.append(pltpu.make_async_copy(stage_up.at[slot, s], dest.at[:, up_at, :], out_sem.at[slot, s]))
            copies.append(
                pltpu.make_async_copy(
                    stage_down.at[slot, s], dest.at[pl.ds(step * pairs, pairs), down_at, :], out_sem.at[slot, 2 + s]
                )
            )
        return copies

    def out_copies():
        if not split:
            return [pltpu.make_async_copy(stage_up.at[0], keep_hbm.at[steps], out_sem.at[0, 0])]
        at = pl.ds(2 * steps * r, r)
        return [
            pltpu.make_async_copy(stage_up.at[0, s], dest.at[:, at, :], out_sem.at[0, s])
            for s, dest in enumerate((keep_hbm, send_hbm))
        ]

    def put(stage, slot, value, owners):
        if not split:
            stage[slot] = value.astype(bf16)
            return
        keep, send = split_cores(value, core, owners)
        stage[slot, 0] = keep.astype(bf16)
        stage[slot, 1] = send.astype(bf16)

    @pl.when(j == 0)
    def _():
        first, later = ffn_copies(idx_ref, pieces, wo, up, down, sem)
        for c in first + later:
            c.start()
        for c in first:
            c.wait()
        for i in range(tiles):
            rs = pl.ds(i * TILE, TILE)
            start = x_ref[rs, :].astype(f32) + t_ref[rs, :] * vec_ref[0:1, :]
            middle = start + dot(att_ref[rs, :], wo[...]) + vec_ref[1:2, :]
            mid[rs, :] = middle
            acc[rs, :] = middle + vec_ref[4:5, :]
            gn2[rs, :] = jnp.zeros((TILE, width), f32)
            normed = (ln_parts(middle)[0] * vec_ref[2:3, :] + vec_ref[3:4, :]).astype(bf16)
            n2[rs, :] = normed
        for c in later:
            c.wait()

    @pl.when(j > 1)
    def _():
        for c in moves(j - 2):
            c.wait()

    f0 = pl.multiple_of(j * fc, fc)
    up_c = up[:, pl.ds(f0, fc)]
    down_c = down[pl.ds(f0, fc), :]
    upb = upb_ref[...]
    gb = jnp.zeros((1, fc), f32)
    ahead = []

    def enter(i):
        rs = pl.ds(i * TILE, TILE)
        ahead.append((dot(n2[rs, :], up_c), dot(cot_ref[rs, :], down_c, NT)))

    enter(0)
    for i in range(tiles):
        rs = pl.ds(i * TILE, TILE)
        if i + 1 < tiles:
            enter(i + 1)
        pre, gh = ahead[i]
        h, slope = gelu_parts(pre + upb)
        h = h.astype(bf16)
        g = (gh * slope).astype(bf16)
        hid[rs, :] = h
        gp[rs, :] = g
        gb = gb + rows_sum(g.astype(f32))
        acc[rs, :] += dot(h, down_c)
        gn2[rs, :] += dot(g, up_c, NT)
    gupb_ref[...] = gb
    slot = lax.rem(j, 2)
    put(stage_down, slot, dot(hid[...], cot_ref[...], TN), 2 * (fc // (2 * steps * r)) if split else 0)
    put(stage_up, slot, dot(n2[...], gp[...], TN), split)
    for c in moves(j):
        c.start()

    @pl.when(j == steps - 1)
    def _():
        sums = [jnp.zeros((1, width), f32)] * 4
        for i in range(tiles):
            rs = pl.ds(i * TILE, TILE)
            out_ref[rs, :] = acc[rs, :].astype(bf16)
            xhat, rstd = ln_parts(mid[rs, :])
            dn = gn2[rs, :]
            cot = cot_ref[rs, :].astype(f32)
            gm = cot + ln_back(xhat, rstd, dn, vec_ref[2:3, :])
            mid[rs, :] = gm
            ga = gm.astype(bf16)
            hid[rs, :] = ga
            ga_ref[rs, :] = dot(ga, wo[...], NT).astype(bf16)
            sums = [s + rows_sum(v) for s, v in zip(sums, (dn * xhat, dn, cot, ga.astype(f32)))]
        gvec_ref[...] = jnp.concatenate(sums + [jnp.zeros((4, width), f32)], axis=0)
        mid_copy = pltpu.make_async_copy(mid, gm_hbm, gm_sem)
        mid_copy.start()
        grad_out = dot(att_ref[...], hid[...], TN)
        for c in moves(j - 1) + moves(j):
            c.wait()
        put(stage_up, 0, grad_out, split)
        last = out_copies()
        for c in last:
            c.start()
        for c in last:
            c.wait()
        mid_copy.wait()


def ffn_both(idx, x, t, att, cot, vecs, upb, pieces, ff, split):
    rows, width = x.shape
    n = len(pieces)
    fc = width
    steps = ff // fc
    sd = jax.ShapeDtypeStruct
    V = pltpu.VMEM
    if split:
        half = split // 2
        r = width // split
        grads = [sd((half, (2 * steps + 1) * r, width), bf16)] * 2
        stages = [V((2, 2, half, r, width), bf16), V((2, 2, fc // (2 * steps * r), steps * r, width), bf16)]
    else:
        grads = [sd((steps + 1, width, width), bf16), sd((ff, width), bf16)]
        stages = [V((2, width, width), bf16)] * 2
    return pl.pallas_call(
        functools.partial(ffn_kernel, n, split, steps),
        grid_spec=pltpu.PrefetchScalarGridSpec(
            num_scalar_prefetch=1,
            grid=(steps,),
            in_specs=[whole_spec((rows, width)), whole_spec((rows, 1)), whole_spec((rows, width)), whole_spec((rows, width)),
                      whole_spec(vecs.shape), pl.BlockSpec((1, fc), lambda j, *_: (0, j))] + [any_spec()] * n,
            out_specs=[whole_spec((rows, width)), whole_spec((rows, width)), whole_spec((8, width)),
                       pl.BlockSpec((1, fc), lambda j, *_: (0, j)), any_spec(), any_spec(), any_spec()],
            scratch_shapes=[V((width, width), bf16), V((width, ff), bf16), V((ff, width), bf16),
                            V((rows, width), f32), V((rows, width), bf16),
                            V((rows, width), f32), V((rows, width), f32),
                            V((rows, fc), bf16), V((rows, fc), bf16), *stages,
                            pltpu.SemaphoreType.DMA((6 * n,)), pltpu.SemaphoreType.DMA((2, 4)), pltpu.SemaphoreType.DMA],
        ),
        out_shape=[sd((rows, width), bf16), sd((rows, width), bf16), sd((8, width), f32), sd((1, ff), f32),
                   sd((rows, width), f32), *grads],
        compiler_params=params(),
        cost_estimate=cost(60),
        name="ffn_both",
    )(idx, x, t, att, cot, vecs, upb, *pieces)


def gqkv_kernel(split, idx_ref, normed_ref, gp_ref, *rest):
    outs, nt = rest[:-1], rest[-1]

    @pl.when(pl.program_id(0) == 0)
    def _():
        nt[...] = normed_ref[...].T

    grad = dot(nt[...], gp_ref[...])
    if split:
        keep, send = split_cores(grad, lax.rem(idx_ref[0], 2), split)
        outs[0][...] = keep.astype(bf16)
        outs[1][...] = send.astype(bf16)
    else:
        outs[0][0] = grad.astype(bf16)


def qkv_weight_grad(idx, normed, gp, split):
    rows, width = normed.shape
    sd = jax.ShapeDtypeStruct
    if split:
        half, r = split // 2, width // split
        out_specs = [pl.BlockSpec((half, r, width), lambda j, *_: (0, j, 0))] * 2
        out_shape = [sd((half, 3 * r, width), bf16)] * 2
    else:
        out_specs = [pl.BlockSpec((1, width, width), lambda j, *_: (j, 0, 0))]
        out_shape = [sd((3, width, width), bf16)]
    return pl.pallas_call(
        functools.partial(gqkv_kernel, split),
        grid_spec=pltpu.PrefetchScalarGridSpec(
            num_scalar_prefetch=1,
            grid=(3,),
            in_specs=[whole_spec((rows, width)), pl.BlockSpec((rows, width), lambda j, *_: (0, j))],
            out_specs=out_specs,
            scratch_shapes=[pltpu.VMEM((width, rows), bf16)],
        ),
        out_shape=out_shape,
        compiler_params=params(),
        cost_estimate=cost(8),
        name="qkv_weight_grad",
    )(idx, normed, gp)


def first_kernel(n, idx_ref, x_ref, t_ref, gm_ref, gp_ref, vec_ref, *rest):
    pieces, (gi_ref, gvec_ref, w_scr, sem) = rest[:n], rest[n:]
    i = pl.program_id(0)
    width = x_ref.shape[1]

    @pl.when(i == 0)
    def _():
        for c in qkv_copies(idx_ref, pieces, w_scr, sem):
            c.start()
        gvec_ref[...] = jnp.zeros_like(gvec_ref)
        for c in qkv_copies(idx_ref, pieces, w_scr, sem):
            c.wait()

    t = t_ref[...]
    dn = dot(gp_ref[...], w_scr[...], NT)
    start = x_ref[...].astype(f32) + t * vec_ref[0:1, :]
    xhat, rstd = ln_parts(start)
    gs = gm_ref[...] + ln_back(xhat, rstd, dn, vec_ref[1:2, :])
    gi_ref[...] = gs.astype(bf16)
    parts = [t * gs, dn * xhat, dn, gp_ref[:, :width].astype(f32), gp_ref[:, 2 * width :].astype(f32)]
    gvec_ref[...] += jnp.concatenate([rows_sum(v) for v in parts] + [jnp.zeros((3, width), f32)], axis=0)


def first_backward(idx, x, t, gm, gp, vecs, pieces):
    rows, width = x.shape
    n = len(pieces)
    sd = jax.ShapeDtypeStruct
    return pl.pallas_call(
        functools.partial(first_kernel, n),
        grid_spec=pltpu.PrefetchScalarGridSpec(
            num_scalar_prefetch=1,
            grid=(rows // TILE,),
            in_specs=[row_spec(width), row_spec(1), row_spec(width), row_spec(3 * width), whole_spec(vecs.shape)] + [any_spec()] * n,
            out_specs=[row_spec(width), whole_spec((8, width))],
            scratch_shapes=[pltpu.VMEM((width, 3 * width), bf16), pltpu.SemaphoreType.DMA((n,))],
        ),
        out_shape=[sd((rows, width), bf16), sd((8, width), f32)],
        compiler_params=params(),
        cost_estimate=cost(11),
        name="first_backward",
    )(idx, x, t, gm, gp, vecs, *pieces)


SHARDS = 8


def swap(value, axis, size, bit_mask):
    return lax.ppermute(value, axis, [(i, i ^ bit_mask) for i in range(size)])


def near(value):
    return swap(value, "fsdp", SHARDS, 1)


def along_x(value):
    return swap(value, "fsdp", SHARDS, 2)


def along_y(value):
    return swap(value, "fsdp", SHARDS, 4)


def with_near(far):
    pieces = []
    for piece in far:
        pieces += [piece, near(piece)]
    return pieces


def in_order(pieces, order):
    stacked = pieces.astype(f32)
    hit = (jnp.arange(stacked.shape[0])[:, None] == order[None, :]).astype(f32)
    return jnp.sum(hit.reshape(hit.shape + (1,) * (stacked.ndim - 1)) * stacked[None], axis=1)


def blocks_of(weight, width):
    r = weight.shape[0]
    return jnp.transpose(weight.reshape(r, -1, width), (1, 0, 2)).reshape(-1, width)


def far_first(kept, came, spot):
    place = spot // 2
    cut = kept.shape[1] // 32 * 16

    def total(mask, rows):
        pick = lambda v: lax.dynamic_index_in_dim(v, place ^ mask, 0, keepdims=False)[rows].astype(f32)
        return (pick(kept) + pick(came)).astype(kept.dtype)

    top, low = slice(None, cut), slice(cut, None)
    stay = (total(0, top), total(2, top), total(0, low), total(1, low))
    go_x = jnp.stack([total(1, top), total(3, top)])
    go_y = jnp.stack([total(2, low), total(3, low)])
    return stay, go_x, go_y


def add_low(a, b):
    return (a.astype(f32) + b.astype(f32)).astype(a.dtype)


def far_second(stay, from_x, from_y):
    own_top, y_top, own_low, x_low = stay
    return (add_low(own_top, from_x[0]), add_low(own_low, from_y[0])), add_low(y_top, from_x[1]), add_low(x_low, from_y[1])


def far_third(own, from_y, from_x):
    return jnp.concatenate([add_low(own[0], from_y), add_low(own[1], from_x)])


def halves(owned, spot):
    parts = owned.reshape(2, owned.shape[0] // 2, owned.shape[1])
    side = spot % 2
    return (
        lax.dynamic_index_in_dim(parts, side, 0, keepdims=False),
        lax.dynamic_index_in_dim(parts, 1 - side, 0, keepdims=False),
    )


def rows_first(kept, sent, size):
    return add_low(kept, swap(sent, "dp", size, 1))


def rows_middle(half, size):
    step = 2
    while step < size:
        half = add_low(half, swap(half, "dp", size, step))
        step *= 2
    return half


def rows_last(half, size, spot):
    other = swap(half, "dp", size, 1)
    even = spot % 2 == 0
    return jnp.concatenate([jnp.where(even, half, other), jnp.where(even, other, half)]).astype(f32)


def sum_owned(packed, spot, size):
    if size != SHARDS:
        return lax.psum_scatter(packed, "fsdp", scatter_dimension=0)
    total = lax.dynamic_index_in_dim(packed, spot, 0, keepdims=False)
    for m in range(1, size):
        total = total + swap(lax.dynamic_index_in_dim(packed, spot ^ m, 0, keepdims=False), "fsdp", size, m)
    return total


def sum_planes(value, size):
    terms = [value] + [swap(value, "dp", size, m) for m in range(1, size)]
    while len(terms) > 1:
        terms = [a + b for a, b in zip(terms[::2], terms[1::2])]
    return terms[0]


def on_device(
    sizes,
    inputs,
    time_of_row,
    coords,
    segment_ids,
    cotangent,
    time_weight,
    ln1_gain,
    ln1_bias,
    w_qkv,
    q_bias,
    v_bias,
    w_out,
    out_bias,
    kernel_mean,
    kernel_width,
    kernel_map,
    ln2_gain,
    ln2_bias,
    w_up,
    up_bias,
    w_down,
    down_bias,
):
    n, planes = sizes
    direct = n == SHARDS
    split = n if direct else 0
    barrier = lax.optimization_barrier
    spot = lax.axis_index("fsdp")
    level = lax.axis_index("dp")
    order = (spot ^ jnp.arange(n)).astype(jnp.int32)
    width = inputs.shape[1]
    r = w_qkv.shape[0]
    heads = kernel_map.shape[1]
    own_kernels = kernel_map.shape[0]
    kernels = own_kernels * n
    wide = up_bias.shape[0] // r
    ff = n * wide * r
    scale = (width // heads) ** (-0.5)
    times = time_of_row[:, None]

    kernel_cols = jnp.concatenate([kernel_map, kernel_mean[:, None], kernel_width[:, None]], axis=1)
    vectors = (time_weight, ln1_gain, ln1_bias, q_bias, v_bias, out_bias, ln2_gain, ln2_bias, down_bias)
    vectors = jnp.concatenate([jnp.stack(vectors), up_bias.reshape(wide, r)])
    if direct:
        lanes = 128
        small = jnp.concatenate(
            [jnp.pad(v, ((0, 0), (0, lanes - v.shape[1]))) for v in (kernel_cols, vectors)]
        )
        pair = jnp.stack([small, near(small)])
        pair, w_first, w_second, coords, segment_ids, times = barrier(
            (pair, w_qkv, (w_out, w_up, w_down), coords, segment_ids, times)
        )
        small_far = [swap(pair, "fsdp", n, 2 * m) for m in range(1, n // 2)]
        qkv_far = [w_first] + [swap(w_first, "fsdp", n, 2 * m) for m in range(1, n // 2)]
        second = jnp.concatenate([w_second[0], blocks_of(w_second[1], width), w_second[2]])
        small_all = in_order(jnp.concatenate([pair] + small_far), order)
        kernel_cols, vectors = small_all[:, :own_kernels], small_all[:, own_kernels:, :r]
    else:
        kernel_cols = lax.all_gather(kernel_cols, "fsdp", axis=0).astype(f32)
        vectors = lax.all_gather(vectors, "fsdp", axis=0).astype(f32)
        qkv_p = (lax.all_gather(w_qkv, "fsdp", axis=0, tiled=True),)
        ffn_p = tuple(lax.all_gather(w, "fsdp", axis=0, tiled=True) for w in (w_out, w_up, w_down))
    kernel_cols = kernel_cols.reshape(kernels, -1)

    aux_win, aux_col = aux_of(coords, segment_ids)
    gmat, amat, kernel_columns = kernel_consts(
        kernel_cols[:, heads], kernel_cols[:, heads + 1], kernel_cols[:, :heads].astype(bf16)
    )
    bmat = amat.T
    done = attn_bias(0, aux_win, aux_col, gmat, bmat, ())
    if direct:
        done, second, qkv_far = barrier((done, second, qkv_far))
        qkv_p = tuple(with_near(qkv_far))
        from_x, from_y = along_x(second), along_y(second)
    bias, feats = attn_bias(1, aux_win, aux_col, gmat, bmat, done)
    vecs = jnp.transpose(vectors[:, :9], (1, 0, 2)).reshape(9, width)
    up_bias_all = vectors[:, 9:].reshape(1, ff)

    def rows_of(*picked):
        return jnp.concatenate([vecs[p : p + 1] for p in picked] + [jnp.zeros((8 - len(picked), width), f32)])

    first_rows, ffn_rows, back_rows = rows_of(0, 1, 2, 3, 4), rows_of(0, 5, 6, 7, 8), rows_of(0, 1)
    if direct:
        bias, qkv_p, ready = barrier((bias, qkv_p, (first_rows, ffn_rows, back_rows, up_bias_all, amat, kernel_columns)))
        first_rows, ffn_rows, back_rows, up_bias_all, amat, kernel_columns = ready
    normed, queries, keys, values = qkv_forward(order, inputs, times, first_rows, qkv_p, scale)
    if direct:
        cut = (1 + wide) * r
        queries, from_x, from_y = barrier((queries, from_x, from_y))
        top_d, low_d = along_y(from_x[:cut]), along_x(from_y[cut:])
        ffn_p = with_near((second, from_x, from_y))
    attended, probs = attn_fwd(1, queries, keys, values, bias, attn_fwd(0, queries, keys, values, bias, ()))
    if direct:
        attended, top_d, low_d, ffn_p = barrier((attended, top_d, low_d, ffn_p))
        ffn_p = tuple(ffn_p + with_near((top_d, low_d)))

    output, grad_attended, ffn_vecs, grad_up_bias, grad_middle, ffn_keep, ffn_send = ffn_both(
        order, inputs, times, attended, cotangent, ffn_rows, up_bias_all, ffn_p, ff, split
    )
    up_rows = wide * r

    def backward(part, before):
        return attn_bwd(part, queries, grad_attended, keys, values, probs, scale, before)

    def feat(part, before):
        return attn_feat(part, grad_scores, feats, aux_win, aux_col, amat, kernel_columns, before)

    def scattered(array, blocks):
        owned = lax.psum_scatter(array.reshape(blocks, n, -1, width), "fsdp", scatter_dimension=1)
        return owned.reshape(-1, width)

    if direct:
        ffn_came = near(ffn_send)
        done = backward(0, ())
        done, a = barrier((done, far_first(ffn_keep, ffn_came, spot)))
        a = (a[0], along_x(a[1]), along_y(a[2]))
        grad_projected, grad_scores = backward(3, backward(2, backward(1, done)))
        qkv_keep, qkv_send = qkv_weight_grad(order, normed, grad_projected, split)
        qkv_keep, qkv_send, a = barrier((qkv_keep, qkv_send, far_second(*a)))
        a = (a[0], along_y(a[1]), along_x(a[2]))
        c = far_first(qkv_keep, near(qkv_send), spot)
    else:
        grad_projected, grad_scores = backward(3, backward(2, backward(1, backward(0, ()))))
        a = jnp.concatenate([scattered(ffn_keep[:wide], wide), scattered(ffn_send, 1), scattered(ffn_keep[wide:], 1)])
        c = scattered(qkv_weight_grad(order, normed, grad_projected, split)[0], 3)
    grad_inputs, first_vecs = first_backward(
        order, inputs, times, grad_middle, grad_projected, back_rows, qkv_p
    )
    if direct:
        grad_scores, first_vecs, a, c = barrier((grad_scores, first_vecs, far_third(*a), c))
        c = (c[0], along_x(c[1]), along_y(c[2]))
    a = lax.psum(a, "dp")

    sums = feat(0, ())
    if direct:
        sums, c = barrier((sums, far_second(*c)))
        c = (c[0], along_y(c[1]), along_x(c[2]))
    sums = feat(1, sums)
    if direct:
        c = far_third(*c)
    sums, c = barrier((sums, halves(c, level)))
    c = rows_first(*c, planes)
    sums = feat(2, sums)
    sums, c = barrier((sums, c))
    c = rows_middle(c, planes)
    kernel_part = feat(3, sums)[2].reshape(n, own_kernels, -1)
    kernel_part, c = barrier((kernel_part, c))

    grad_rows = [first_vecs[:5], ffn_vecs[3:4], ffn_vecs[:3]]
    vector_rows = jnp.transpose(jnp.concatenate(grad_rows).reshape(9, n, r), (1, 0, 2))
    vector_rows = jnp.concatenate([vector_rows, grad_up_bias.reshape(n, wide, r)], axis=1)
    vector_rows = jnp.pad(vector_rows, ((0, 0), (0, 0), (0, kernel_part.shape[2] - r)))
    small, a = barrier((sum_owned(jnp.concatenate([kernel_part, vector_rows], axis=1), spot, n), a))
    small = sum_planes(small, planes)
    gaussians, vectors = small[:own_kernels], small[own_kernels:, :r]
    grad_qkv = rows_last(c, planes, level)
    grad_up, grad_down, grad_out = a[:up_rows], a[up_rows : 2 * up_rows], a[2 * up_rows :]

    def columns(array):
        return jnp.transpose(array.reshape(-1, r, width), (1, 0, 2)).reshape(r, -1)

    return (
        output,
        grad_inputs,
        vectors[0],
        vectors[1],
        vectors[2],
        columns(grad_qkv),
        vectors[3],
        vectors[4],
        grad_out.astype(f32),
        vectors[5],
        gaussians[:, heads],
        gaussians[:, heads + 1],
        gaussians[:, :heads],
        vectors[6],
        vectors[7],
        columns(grad_up).astype(f32),
        vectors[9:].reshape(up_rows),
        grad_down.astype(f32),
        vectors[8],
    )


def solution(mesh):
    rows, split, whole = P(("fsdp", "dp"), None), P("fsdp"), P("fsdp", None)
    placed = (
        rows,
        P(("fsdp", "dp")),
        P(None, ("fsdp", "dp")),
        P(("fsdp", "dp")),
        rows,
        split,
        split,
        split,
        whole,
        split,
        split,
        whole,
        split,
        split,
        split,
        whole,
        split,
        split,
        whole,
        split,
        whole,
        split,
    )
    out_placed = (
        rows,
        rows,
        split,
        split,
        split,
        whole,
        split,
        split,
        whole,
        split,
        split,
        split,
        whole,
        split,
        split,
        whole,
        split,
        whole,
        split,
    )
    return jax.shard_map(
        functools.partial(on_device, (mesh.shape["fsdp"], mesh.shape["dp"])),
        mesh=mesh,
        in_specs=placed,
        out_specs=out_placed,
        check_vma=False,
    )
```

```python
import functools, math
import jax, jax.numpy as jnp
from jax import lax
from jax.experimental import pallas as pl
from jax.experimental.pallas import tpu as pltpu
from jax.sharding import PartitionSpec as P

SET = 256
CH = 32
STEP = 4
UNROLL = 4
PAIR = 4
FEAT_STEP = 2
WIN = 128
GROUPS = ((0, 0), (128, 8), (384, 16), (512, 24))
HW = 24
VM = 60 * 1024 * 1024
f32, bf16 = jnp.float32, jnp.bfloat16
NT = (((1,), (1,)), ((), ()))
TN = (((0,), (0,)), ((), ()))


def dot(a, b, dims=(((1,), (0,)), ((), ()))):
    return lax.dot_general(a, b, dims, preferred_element_type=f32)


def spread_heads(block, lane0, h0):
    wide = block.astype(f32)
    lanes = lax.broadcasted_iota(jnp.int32, (8, 256), 1) + lane0
    masks = [(lanes >= h * HW) & (lanes < (h + 1) * HW) for h in range(h0, h0 + 8)]
    zero = jnp.zeros((8, 256), f32)
    parts = [jnp.where(m, wide[8 * g : 8 * g + 8], zero) for g in range(4) for m in masks]
    return jnp.concatenate(parts, axis=0).astype(bf16)


def own_rows(full, lane0, h0):
    lanes = lax.broadcasted_iota(jnp.int32, (8, 256), 1) + lane0
    groups = []
    for g in range(4):
        out = jnp.zeros((8, 256), f32)
        for h in range(8):
            m = (lanes >= (h0 + h) * HW) & (lanes < (h0 + h + 1) * HW)
            out = jnp.where(m, full[64 * g + 8 * h : 64 * g + 8 * h + 8], out)
        groups.append(out)
    return jnp.concatenate(groups, axis=0)


def window_start(i):
    per = SET // CH
    base = i // per * SET
    return pl.multiple_of(jnp.clip(i * CH - 48, base, base + SET - WIN), 16)


def radius_of(ac, aw):
    d = ac[:, 0:1] - aw[0:1, :]
    s = d * d
    for j in (1, 2):
        d = ac[:, j : j + 1] - aw[j : j + 1, :]
        s = s + d * d
    return jnp.sqrt(s)


def per_chunk(body, unroll):
    if STEP == unroll:
        for t in range(STEP):
            body(t)
        return

    @pl.loop(0, STEP // unroll)
    def _(s):
        for t in range(unroll):
            body(s * unroll + t)


def chunk_rows(t):
    return pl.ds(pl.multiple_of(t * CH, CH), CH)


def parts3(v):
    high = v.astype(bf16).astype(f32)
    rest = v - high
    middle = rest.astype(bf16).astype(f32)
    return high, middle, (rest - middle).astype(bf16).astype(f32)


def distance_rows(ac, aw):
    rho = radius_of(ac, aw)
    rho = jnp.concatenate([rho[8 * g : 8 * g + 8] for g in range(4)], axis=1)
    (sh, sm, sl), (h, m, l) = parts3(rho * rho), parts3(rho)
    one = jnp.ones_like(rho)
    slots = [sh, sh, sm, sm, sh, sl, h, h, m, m, h, l, one, one, one, jnp.zeros_like(rho)]
    return jnp.concatenate(slots, axis=0).astype(bf16)


def bias_kernel(aw_ref, ac_ref, gmat_ref, amat_ref, b_ref, f_ref, t_scr):
    @pl.loop(0, STEP // PAIR)
    def _(s):
        chunks = [s * PAIR + u for u in range(PAIR)]
        ac = [ac_ref[chunk_rows(t), :] for t in chunks]
        aw = [aw_ref[t] for t in chunks]
        dist = [distance_rows(a, w) for a, w in zip(ac, aw)]
        e = [dot(gmat_ref[...], d) for d in dist]
        f = [jnp.exp2(v).astype(bf16) for v in e]
        bias = [dot(amat_ref[...], v, TN) for v in f]
        for u, t in enumerate(chunks):
            f_ref[t] = f[u]
            joined = ac[u][:, 3:4] == aw[u][3:4, :]
            for g in range(4):
                part = bias[u][:, 128 * g : 128 * g + 128].reshape(32, 8, WIN)
                part = jnp.where(joined[8 * g : 8 * g + 8][None], part, -1e30)
                for q in range(4):
                    t_scr[u, 256 * q + 64 * g : 256 * q + 64 * g + 64, :] = part[8 * q : 8 * q + 8].reshape(64, WIN)
        for u, t in enumerate(chunks):
            for n in range(8):
                b_ref[t, :, 128 * n : 128 * n + 128] = t_scr[u, 128 * n : 128 * n + 128, :].T


def fwd_kernel(q_ref, k_ref, v_ref, b_ref, o_ref, p_ref):
    def chunk(t):
        w = window_start(pl.program_id(0) * STEP + t)
        rt = chunk_rows(t)
        kwin = k_ref[pl.ds(w, WIN), :]
        vwin = v_ref[pl.ds(w, WIN), :]
        spans = [slice(lane0, lane0 + 256) for lane0, _ in GROUPS]
        wide = [spread_heads(q_ref[rt, sl], lane0, h0) for sl, (lane0, h0) in zip(spans, GROUPS)]
        s = [dot(kwin[:, sl], qm, NT) + b_ref[t, :, 256 * j : 256 * j + 256] for j, (sl, qm) in enumerate(zip(spans, wide))]
        e = [jnp.exp(v - jnp.max(v, axis=0, keepdims=True)) for v in s]
        pr = [(v * (1.0 / jnp.sum(v, axis=0, keepdims=True))).astype(bf16) for v in e]
        full = [dot(v, vwin[:, sl], TN) for sl, v in zip(spans, pr)]
        acc = [own_rows(v, *GROUPS[j]) for j, v in enumerate(full)]
        for j, v in enumerate(pr):
            p_ref[t, :, 256 * j : 256 * j + 256] = v
        store_lanes(o_ref, rt, acc)

    per_chunk(chunk, UNROLL)


def store_lanes(ref, rows, acc):
    for half in range(2):
        a, b = acc[2 * half], acc[2 * half + 1]
        full = jnp.concatenate([a[:, :128], a[:, 128:] + b[:, :128], b[:, 128:]], axis=1)
        ref[rows, 384 * half : 384 * half + 384] = full.astype(bf16)


def bwd_kernel(q_ref, do_ref, k_ref, v_ref, p_ref, gp_ref, ds_ref, dk_scr, dv_scr, *, scale):
    i = pl.program_id(0)
    width = 32 * HW

    @pl.when(i == 0)
    def _():
        dk_scr[...] = jnp.zeros_like(dk_scr)
        dv_scr[...] = jnp.zeros_like(dv_scr)

    def chunk(t):
        w = window_start(i * STEP + t)
        rt = chunk_rows(t)
        kwin = k_ref[pl.ds(w, WIN), :]
        vwin = v_ref[pl.ds(w, WIN), :]
        left = lax.broadcasted_iota(jnp.int32, (WIN, 128), 1) < 64
        spans = [slice(lane0, lane0 + 256) for lane0, _ in GROUPS]
        qm = [spread_heads(q_ref[rt, sl], lane0, h0) for sl, (lane0, h0) in zip(spans, GROUPS)]
        dom = [spread_heads(do_ref[rt, sl], lane0, h0) for sl, (lane0, h0) in zip(spans, GROUPS)]
        p_low = [p_ref[t, :, 256 * j : 256 * j + 256] for j in range(4)]
        dp = [dot(vwin[:, sl], v, NT) for sl, v in zip(spans, dom)]
        dv = [dot(a, b) for a, b in zip(p_low, dom)]
        pf = [v.astype(f32) for v in p_low]
        pd = [a * b for a, b in zip(pf, dp)]
        ds = [a - b * jnp.sum(a, axis=0, keepdims=True) for a, b in zip(pd, pf)]
        ds_low = [v.astype(bf16) for v in ds]
        full = [dot(v, kwin[:, sl], TN) for sl, v in zip(spans, ds_low)]
        dk = [dot(a, b) for a, b in zip(ds_low, qm)]
        acc = [own_rows(v, *GROUPS[j]) * scale for j, v in enumerate(full)]
        for j in (0, 2):
            for p in range(2):
                a, b = (ds[j + t][:, 128 * p : 128 * p + 128] for t in range(2))
                at = slice(64 * j, 64 * j + 128)
                ds_ref[t, 256 * p : 256 * p + WIN, at] = jnp.where(left, a, pltpu.roll(b, 64, 1)).astype(bf16)
                ds_ref[t, 256 * p + WIN : 256 * p + 256, at] = jnp.where(left, pltpu.roll(a, 64, 1), b).astype(bf16)
        for scr, parts in ((dk_scr, dk), (dv_scr, dv)):
            for half in range(2):
                a, b = parts[2 * half : 2 * half + 2]
                both = jnp.concatenate([a[:, :128], a[:, 128:] + b[:, :128], b[:, 128:]], axis=1)
                scr[pl.ds(w, WIN), 384 * half : 384 * half + 384] += both
        store_lanes(gp_ref, pl.ds(pl.multiple_of((i * STEP + t) * CH, CH), CH), acc)

    per_chunk(chunk, UNROLL)

    @pl.when(i == pl.num_programs(0) - 1)
    def _():
        gp_ref[:, width : 2 * width] = dk_scr[...].astype(bf16)
        gp_ref[:, 2 * width :] = dv_scr[...].astype(bf16)


def feat_kernel(n_before, last, ds_ref, f_ref, aw_ref, ac_ref, amat_ref, kcol_ref, *rest):
    before, (m_ref, s_ref, *out_ref, rho_scr, gf_scr, m0_ref) = rest[:n_before], rest[n_before:]

    @pl.when(pl.program_id(0) == 0)
    def _():
        m0_ref[...] = jnp.zeros_like(m0_ref)
        s_ref[...] = before[1][...] if before else jnp.zeros_like(s_ref)

    for u in range(FEAT_STEP):
        t = u
        rho = radius_of(ac_ref[chunk_rows(t), :], aw_ref[t])
        rho_scr[u] = jnp.concatenate([rho[8 * g : 8 * g + 8] for g in range(4)], axis=1)
    for u in range(FEAT_STEP):
        t = u
        for rb in range(4):
            span = slice(256 * rb, 256 * rb + 256)
            gf_scr[u, span, :] = dot(amat_ref[span, :], ds_ref[t], NT)
            m0_ref[span, :] += dot(f_ref[t, span, :], ds_ref[t])
            for kt in range(8):
                ks = slice(16 * kt, 16 * kt + 16)
                s1, s2 = s_ref[0, ks, :], s_ref[1, ks, :]
                for r in (2 * rb, 2 * rb + 1):
                    for g in range(4):
                        at = (u, slice(128 * r + 16 * kt, 128 * r + 16 * kt + 16), slice(128 * g, 128 * g + 128))
                        rr = rho_scr[u, r : r + 1, 128 * g : 128 * g + 128]
                        w = gf_scr[at] * f_ref[t, at[1], at[2]].astype(f32) * rr
                        s1 = s1 + w
                        s2 = s2 + w * rr
                s_ref[0, ks, :] = s1
                s_ref[1, ks, :] = s2

    @pl.when(pl.program_id(0) == pl.num_programs(0) - 1)
    def _():
        n = kcol_ref.shape[0]
        lanes = lax.broadcasted_iota(jnp.int32, (n, 256), 1)
        m = jnp.zeros((n, 256), f32)
        for r in range(8):
            m = jnp.where(lanes % 8 == r, m0_ref[n * r : n * r + n, :], m)
        if before:
            m = m + before[0][...]
        m_ref[...] = m
        if last:
            out_ref[0][...] = kernel_grads(m, s_ref, kcol_ref[...])


def kernel_grads(m, s_ref, kcol):
    n = kcol.shape[0]
    heads = lax.broadcasted_iota(jnp.int32, (256, 128), 0) // 8 == lax.broadcasted_iota(jnp.int32, (256, 128), 1)
    heads = heads.astype(f32).astype(bf16)
    g_map = sum(dot(v.astype(bf16), heads) for v in parts3(m))
    lanes = lax.broadcasted_iota(jnp.int32, (n, 128), 1)
    s0 = jnp.sum(jnp.where(lanes < 32, g_map * kcol, 0.0), axis=-1, keepdims=True)
    s1 = jnp.sum(s_ref[0], axis=-1, keepdims=True)
    s2 = jnp.sum(s_ref[1], axis=-1, keepdims=True)
    mean, width = kcol[:, 32:33], kcol[:, 33:34]
    square = width * width
    g_mean = (s1 - mean * s0) / square
    g_width = ((s2 - 2.0 * mean * s1 + mean * mean * s0) / square - s0) / width
    return jnp.where(lanes == 32, g_mean, jnp.where(lanes == 33, g_width, g_map))


def cost(micros):
    return pl.CostEstimate(flops=int(micros * 1.1535e9), bytes_accessed=0, transcendentals=0)


def full_spec(shape):
    return pl.BlockSpec(shape, lambda i: (0,) * len(shape))


def params(limit=VM):
    return pltpu.CompilerParams(vmem_limit_bytes=limit, dimension_semantics=("arbitrary",))


BIAS_PARTS = 2
FWD_PARTS = 1
BWD_PARTS = 4
FEAT_PARTS = 4


def shifted(spec_shape, base):
    return pl.BlockSpec(spec_shape, lambda i: (i + base,) + (0,) * (len(spec_shape) - 1))


def half_spec(shape, part):
    return pl.BlockSpec(shape, lambda i: (part,) + (0,) * (len(shape) - 1))


def attn_bias(part, aw, ac, gmat, amat, before):
    c = aw.shape[0]
    per = c // BIAS_PARTS // STEP
    base = part * per
    n_in = 4
    return pl.pallas_call(
        functools.partial(skip_refs, bias_kernel, n_in, len(before)),
        grid=(per,),
        in_specs=[
            shifted((STEP, 8, WIN), base), shifted((STEP * CH, 4), base), full_spec(gmat.shape), full_spec(amat.shape),
        ] + [pl.BlockSpec(memory_space=pl.ANY)] * len(before),
        out_specs=[shifted((STEP, WIN, 1024), base), shifted((STEP, 1024, 4 * WIN), base)],
        out_shape=[jax.ShapeDtypeStruct((c, WIN, 1024), f32), jax.ShapeDtypeStruct((c, 1024, 4 * WIN), bf16)],
        scratch_shapes=[pltpu.VMEM((PAIR, 1024, WIN), f32)],
        input_output_aliases={n_in + t: t for t in range(len(before))},
        compiler_params=params(),
        cost_estimate=cost(4 // BIAS_PARTS),
        name="attn_bias",
    )(aw, ac, gmat, amat, *before)


def attn_fwd(part, q, k, v, bias, before):
    rows, width = q.shape
    c = rows // CH
    per = c // FWD_PARTS // STEP
    base = part * per
    kv = half_spec((rows // FWD_PARTS, width), part)
    n_in = 4
    return pl.pallas_call(
        functools.partial(skip_refs, fwd_kernel, n_in, len(before)),
        grid=(per,),
        in_specs=[shifted((STEP * CH, width), base), kv, kv, shifted((STEP, WIN, 1024), base)]
        + [pl.BlockSpec(memory_space=pl.ANY)] * len(before),
        out_specs=[shifted((STEP * CH, width), base), shifted((STEP, WIN, 1024), base)],
        out_shape=[jax.ShapeDtypeStruct((rows, width), bf16), jax.ShapeDtypeStruct((c, WIN, 1024), bf16)],
        input_output_aliases={n_in + t: t for t in range(len(before))},
        compiler_params=params(),
        cost_estimate=cost(16 // FWD_PARTS),
        name="attn_fwd",
    )(q, k, v, bias, *before)


def skip_refs(kernel, n_in, n_before, *refs):
    kernel(*refs[:n_in], *refs[n_in + n_before :])


def attn_bwd(part, q, do, k, v, p, scale, before):
    rows, width = q.shape
    c = rows // CH
    per = c // BWD_PARTS // STEP
    base = part * per
    kv = half_spec((rows // BWD_PARTS, width), part)
    n_in = 5
    return pl.pallas_call(
        functools.partial(skip_refs, functools.partial(bwd_kernel, scale=scale), n_in, len(before)),
        grid=(per,),
        in_specs=[
            shifted((STEP * CH, width), base), shifted((STEP * CH, width), base), kv, kv,
            shifted((STEP, WIN, 1024), base),
        ] + [pl.BlockSpec(memory_space=pl.ANY)] * len(before),
        out_specs=[half_spec((rows // BWD_PARTS, 3 * width), part), shifted((STEP, 4 * WIN, 256), base)],
        out_shape=[jax.ShapeDtypeStruct((rows, 3 * width), bf16), jax.ShapeDtypeStruct((c, 4 * WIN, 256), bf16)],
        scratch_shapes=[pltpu.VMEM((rows // BWD_PARTS, width), f32)] * 2,
        input_output_aliases={n_in + t: t for t in range(len(before))},
        compiler_params=params(),
        cost_estimate=cost(2),
        name="attn_bwd",
    )(q, do, k, v, p, *before)


def attn_feat(part, ds, feats, aw, ac, amat, kcol, before):
    per = ds.shape[0] // FEAT_PARTS // FEAT_STEP
    base = part * per
    last = part == FEAT_PARTS - 1
    n = kcol.shape[0]
    shapes = [(n, 256), (2, n, WIN)] + [(n, 128)] * last
    return pl.pallas_call(
        functools.partial(feat_kernel, len(before), last),
        grid=(per,),
        in_specs=[
            shifted((FEAT_STEP, 4 * WIN, 256), base), shifted((FEAT_STEP, 1024, 4 * WIN), base),
            shifted((FEAT_STEP, 8, WIN), base), shifted((FEAT_STEP * CH, 4), base),
            full_spec(amat.shape), full_spec(kcol.shape),
        ] + [full_spec(b.shape) for b in before],
        out_specs=[full_spec(s) for s in shapes],
        out_shape=[jax.ShapeDtypeStruct(s, f32) for s in shapes],
        scratch_shapes=[
            pltpu.VMEM((FEAT_STEP, 8, 4 * WIN), f32), pltpu.VMEM((FEAT_STEP, 1024, 4 * WIN), f32), pltpu.VMEM((1024, 256), f32),
        ],
        compiler_params=params(),
        cost_estimate=cost(1),
        name="attn_feat",
    )(ds, feats, aw, ac, amat, kcol, *before)


def aux_of(coords, segment_ids):
    rows = coords.shape[1]
    place = jnp.arange(rows, dtype=jnp.int32) // SET
    key = (segment_ids * (rows // SET) + place).astype(f32)
    packed = jnp.concatenate([coords, key[None], jnp.zeros((4, rows), f32)], axis=0)
    half = SET
    starts = [b + min(max(i - 48, 0), half - WIN) for b in range(0, rows, half) for i in range(0, half, CH)]
    aw = jnp.stack([packed[:, s : s + WIN] for s in starts])
    ac = packed[:4].T
    return aw, ac


def split3(v):
    high = lax.reduce_precision(v, 8, 7)
    middle = lax.reduce_precision(v - high, 8, 7)
    return high, middle, lax.reduce_precision(v - high - middle, 8, 7)


def kernel_consts(mean, width, kmap):
    mean, width = mean.astype(f32), width.astype(f32)
    half = 0.5 * math.log2(math.e) / (width * width)
    ah, am, al = split3(-half)
    bh, bm, bl = split3(2.0 * half * mean)
    ch, cm, cl = split3(-half * mean * mean - jnp.log2(math.sqrt(2.0 * math.pi) * width))
    slots = jnp.stack([ah, am, ah, am, al, ah, bh, bm, bh, bm, bl, bh, ch, cm, cl, jnp.zeros_like(ah)], axis=1)
    eye = jnp.eye(8, dtype=f32)
    n, heads = kmap.shape
    gmat = (eye[:, None, None, :] * slots[None, :, :, None]).reshape(8 * n, 128).astype(bf16)
    amat = (eye[:, None, None, :] * kmap.astype(f32)[None, :, :, None]).reshape(8 * n, heads * 8).astype(bf16)
    kcol = jnp.concatenate([kmap.astype(f32), mean[:, None], width[:, None], jnp.zeros((n, 94), f32)], axis=1)
    return gmat, amat, kcol


TILE = 256
BLOCK = 512
epsilon = 1e-05


def ln_parts(v):
    mean = jnp.mean(v, axis=-1, keepdims=True)
    centred = v - mean
    rstd = lax.rsqrt(jnp.mean(centred * centred, axis=-1, keepdims=True) + epsilon)
    return centred * rstd, rstd


def ln_back(xhat, rstd, dn, gain):
    dg = dn * gain
    m1 = jnp.mean(dg, axis=-1, keepdims=True)
    m2 = jnp.mean(dg * xhat, axis=-1, keepdims=True)
    return rstd * (dg - m1 - xhat * m2)


def rows_sum(v):
    return jnp.sum(v, axis=0, keepdims=True)


def fetch(idx_ref, pieces, moves, sem, base=0):
    copies = []
    for m, (piece, top) in enumerate(pieces):
        for dest, first, column, rows, columns in moves:
            at = pl.multiple_of(idx_ref[m] * rows, 16)
            copies.append(
                pltpu.make_async_copy(
                    piece.at[pl.ds(top + first, rows), :],
                    dest.at[pl.ds(at, rows), pl.ds(column, columns)],
                    sem.at[base + len(copies)],
                )
            )
    return copies


def fetch_whole(arrays, dests, sem):
    return [pltpu.make_async_copy(a, d, sem.at[i]) for i, (a, d) in enumerate(zip(arrays, dests))]


def qkv_copies(idx_ref, pieces, w_scr, sem):
    if len(pieces) == 1:
        return fetch_whole(pieces, [w_scr], sem)
    r, columns = pieces[0].shape
    return fetch(idx_ref, [(p, 0) for p in pieces], [(w_scr, 0, 0, r, columns)], sem)


def ffn_copies(idx_ref, pieces, wo, up, down, sem):
    if len(pieces) == 3:
        copies = fetch_whole(pieces, [wo, up, down], sem)
        return copies[:1], copies[1:]
    width = wo.shape[0]
    n = len(pieces) - 2
    r = width // n
    wide = up.shape[1] // width
    cut = (1 + wide) * r
    tops = [(p, 0) for p in pieces[:n]]
    lows = [(p, cut) for p in pieces[: n - 2]] + [(p, 0) for p in pieces[n:]]
    first = fetch(idx_ref, tops, [(wo, 0, 0, r, width)], sem)
    moves = [(up, r + b * r, b * width, r, width) for b in range(wide)]
    later = fetch(idx_ref, tops, moves, sem, len(first))
    return first, later + fetch(idx_ref, lows, [(down, 0, 0, wide * r, width)], sem, len(first) + len(later))


def any_spec():
    return pl.BlockSpec(memory_space=pl.ANY)


def row_spec(width, tile=TILE):
    return pl.BlockSpec((tile, width), lambda i, *_: (i, 0))


def whole_spec(shape):
    return pl.BlockSpec(shape, lambda i, *_: (0,) * len(shape))


def sub_tiles():
    return [pl.ds(i * TILE, TILE) for i in range(BLOCK // TILE)]


def qkv_kernel(n, scale, idx_ref, x_ref, t_ref, vec_ref, *rest):
    pieces, (normed_ref, q_ref, k_ref, v_ref, w_scr, sem) = rest[:n], rest[n:]
    width = x_ref.shape[1]

    @pl.when(pl.program_id(0) == 0)
    def _():
        for c in qkv_copies(idx_ref, pieces, w_scr, sem):
            c.start()

    for rs in sub_tiles():
        start = x_ref[rs, :].astype(f32) + t_ref[rs, :] * vec_ref[0:1, :]
        normed_ref[rs, :] = (ln_parts(start)[0] * vec_ref[1:2, :] + vec_ref[2:3, :]).astype(bf16)

    @pl.when(pl.program_id(0) == 0)
    def _():
        for c in qkv_copies(idx_ref, pieces, w_scr, sem):
            c.wait()

    normed = normed_ref[...]
    q_ref[...] = ((dot(normed, w_scr[:, :width]) + vec_ref[3:4, :]) * scale).astype(bf16)
    k_ref[...] = dot(normed, w_scr[:, width : 2 * width]).astype(bf16)
    v_ref[...] = (dot(normed, w_scr[:, 2 * width :]) + vec_ref[4:5, :]).astype(bf16)


def qkv_forward(idx, x, t, vecs, pieces, scale):
    rows, width = x.shape
    n = len(pieces)
    out = jax.ShapeDtypeStruct((rows, width), bf16)
    return pl.pallas_call(
        functools.partial(qkv_kernel, n, scale),
        grid_spec=pltpu.PrefetchScalarGridSpec(
            num_scalar_prefetch=1,
            grid=(rows // BLOCK,),
            in_specs=[row_spec(width, BLOCK), row_spec(1, BLOCK), whole_spec(vecs.shape)] + [any_spec()] * n,
            out_specs=[row_spec(width, BLOCK)] * 4,
            scratch_shapes=[pltpu.VMEM((width, 3 * width), bf16), pltpu.SemaphoreType.DMA((n,))],
        ),
        out_shape=[out] * 4,
        compiler_params=params(),
        cost_estimate=cost(10),
        name="qkv_forward",
    )(idx, x, t, vecs, *pieces)


def gelu_parts(x):
    a = jnp.abs(x)
    t = 1.0 / (1.0 + (0.3275911 * math.sqrt(0.5)) * a)
    e = jnp.exp(-0.5 * x * x)
    poly = t * (0.254829592 + t * (-0.284496736 + t * (1.421413741 + t * (-1.453152027 + t * 1.061405429))))
    tail = 0.5 * poly * e
    cdf = jnp.where(x >= 0, 1.0 - tail, tail)
    return x * cdf, cdf + x * e * (1.0 / math.sqrt(2.0 * math.pi))


def split_cores(value, core, owners):
    rows, c = value.shape
    pairs = value.reshape(owners // 2, 2, rows // owners, c)
    even, odd = pairs[:, 0], pairs[:, 1]
    return jnp.where(core == 0, even, odd), jnp.where(core == 0, odd, even)


def ffn_kernel(n, split, steps, idx_ref, x_ref, t_ref, att_ref, cot_ref, vec_ref, upb_ref, *rest):
    pieces = rest[:n]
    (out_ref, ga_ref, gvec_ref, gm_hbm, keep_hbm, send_hbm,
     wo, up, down, mid, n2, acc, gn2, hid, gp, stage_up, stage_down, sem, out_sem, gm_sem) = rest[n:]
    j = pl.program_id(0)
    rows, width = x_ref.shape
    fc = hid.shape[1]
    tiles = rows // TILE
    core = lax.rem(idx_ref[0], 2)
    r = width // split if split else 0

    def moves(step):
        slot = lax.rem(step, 2)
        if not split:
            return [
                pltpu.make_async_copy(stage_up.at[slot], keep_hbm.at[step], out_sem.at[slot, 0]),
                pltpu.make_async_copy(stage_down.at[slot], send_hbm.at[pl.ds(step * fc, fc), :], out_sem.at[slot, 2]),
            ]
        pairs = fc // (2 * steps * r)
        up_at = pl.ds(pl.multiple_of(step * r, r), r)
        down_at = pl.ds(steps * r, steps * r)
        copies = []
        for s, dest in enumerate((keep_hbm, send_hbm)):
            copies.append(pltpu.make_async_copy(stage_up.at[slot, s], dest.at[:, up_at, :], out_sem.at[slot, s]))
            copies.append(
                pltpu.make_async_copy(
                    stage_down.at[slot, s], dest.at[pl.ds(step * pairs, pairs), down_at, :], out_sem.at[slot, 2 + s]
                )
            )
        return copies

    def out_copies():
        if not split:
            return [pltpu.make_async_copy(stage_up.at[0], keep_hbm.at[steps], out_sem.at[0, 0])]
        at = pl.ds(2 * steps * r, r)
        return [
            pltpu.make_async_copy(stage_up.at[0, s], dest.at[:, at, :], out_sem.at[0, s])
            for s, dest in enumerate((keep_hbm, send_hbm))
        ]

    def put(stage, slot, value, owners):
        if not split:
            stage[slot] = value.astype(bf16)
            return
        keep, send = split_cores(value, core, owners)
        stage[slot, 0] = keep.astype(bf16)
        stage[slot, 1] = send.astype(bf16)

    @pl.when(j == 0)
    def _():
        first, later = ffn_copies(idx_ref, pieces, wo, up, down, sem)
        for c in first + later:
            c.start()
        for c in first:
            c.wait()
        for i in range(tiles):
            rs = pl.ds(i * TILE, TILE)
            start = x_ref[rs, :].astype(f32) + t_ref[rs, :] * vec_ref[0:1, :]
            middle = start + dot(att_ref[rs, :], wo[...]) + vec_ref[1:2, :]
            mid[rs, :] = middle
            acc[rs, :] = middle + vec_ref[4:5, :]
            gn2[rs, :] = jnp.zeros((TILE, width), f32)
            normed = (ln_parts(middle)[0] * vec_ref[2:3, :] + vec_ref[3:4, :]).astype(bf16)
            n2[rs, :] = normed
        for c in later:
            c.wait()

    @pl.when(j > 1)
    def _():
        for c in moves(j - 2):
            c.wait()

    f0 = pl.multiple_of(j * fc, fc)
    up_c = up[:, pl.ds(f0, fc)]
    down_c = down[pl.ds(f0, fc), :]
    upb = upb_ref[...]
    gb = jnp.zeros((1, fc), f32)
    ahead = []

    def enter(i):
        rs = pl.ds(i * TILE, TILE)
        ahead.append((dot(n2[rs, :], up_c), dot(cot_ref[rs, :], down_c, NT)))

    enter(0)
    for i in range(tiles):
        rs = pl.ds(i * TILE, TILE)
        if i + 1 < tiles:
            enter(i + 1)
        pre, gh = ahead[i]
        h, slope = gelu_parts(pre + upb)
        h = h.astype(bf16)
        g = (gh * slope).astype(bf16)
        hid[rs, :] = h
        gp[rs, :] = g
        gb = gb + rows_sum(g.astype(f32))
        acc[rs, :] += dot(h, down_c)
        gn2[rs, :] += dot(g, up_c, NT)
    gvec_ref[pl.ds(4 + j, 1), :] = gb
    slot = lax.rem(j, 2)
    put(stage_down, slot, dot(hid[...], cot_ref[...], TN), 2 * (fc // (2 * steps * r)) if split else 0)
    put(stage_up, slot, dot(n2[...], gp[...], TN), split)
    for c in moves(j):
        c.start()

    @pl.when(j == steps - 1)
    def _():
        sums = [jnp.zeros((1, width), f32)] * 4
        for i in range(tiles):
            rs = pl.ds(i * TILE, TILE)
            out_ref[rs, :] = acc[rs, :].astype(bf16)
            xhat, rstd = ln_parts(mid[rs, :])
            dn = gn2[rs, :]
            cot = cot_ref[rs, :].astype(f32)
            gm = cot + ln_back(xhat, rstd, dn, vec_ref[2:3, :])
            mid[rs, :] = gm
            ga = gm.astype(bf16)
            hid[rs, :] = ga
            ga_ref[rs, :] = dot(ga, wo[...], NT).astype(bf16)
            sums = [s + rows_sum(v) for s, v in zip(sums, (dn * xhat, dn, cot, ga.astype(f32)))]
        gvec_ref[0:4, :] = jnp.concatenate(sums, axis=0)
        mid_copy = pltpu.make_async_copy(mid, gm_hbm, gm_sem)
        mid_copy.start()
        grad_out = dot(att_ref[...], hid[...], TN)
        for c in moves(j - 1) + moves(j):
            c.wait()
        put(stage_up, 0, grad_out, split)
        last = out_copies()
        for c in last:
            c.start()
        for c in last:
            c.wait()
        mid_copy.wait()


def ffn_both(idx, x, t, att, cot, vecs, upb, pieces, ff, split):
    rows, width = x.shape
    n = len(pieces)
    fc = width
    steps = ff // fc
    sd = jax.ShapeDtypeStruct
    V = pltpu.VMEM
    if split:
        half = split // 2
        r = width // split
        grads = [sd((half, (2 * steps + 1) * r, width), bf16)] * 2
        stages = [V((2, 2, half, r, width), bf16), V((2, 2, fc // (2 * steps * r), steps * r, width), bf16)]
    else:
        grads = [sd((steps + 1, width, width), bf16), sd((ff, width), bf16)]
        stages = [V((2, width, width), bf16)] * 2
    return pl.pallas_call(
        functools.partial(ffn_kernel, n, split, steps),
        grid_spec=pltpu.PrefetchScalarGridSpec(
            num_scalar_prefetch=1,
            grid=(steps,),
            in_specs=[whole_spec((rows, width)), whole_spec((rows, 1)), whole_spec((rows, width)), whole_spec((rows, width)),
                      whole_spec(vecs.shape), pl.BlockSpec((1, fc), lambda j, *_: (0, j))] + [any_spec()] * n,
            out_specs=[whole_spec((rows, width)), whole_spec((rows, width)), whole_spec((4 + steps, width)),
                       any_spec(), any_spec(), any_spec()],
            scratch_shapes=[V((width, width), bf16), V((width, ff), bf16), V((ff, width), bf16),
                            V((rows, width), f32), V((rows, width), bf16),
                            V((rows, width), f32), V((rows, width), f32),
                            V((rows, fc), bf16), V((rows, fc), bf16), *stages,
                            pltpu.SemaphoreType.DMA((6 * n,)), pltpu.SemaphoreType.DMA((2, 4)), pltpu.SemaphoreType.DMA],
        ),
        out_shape=[sd((rows, width), bf16), sd((rows, width), bf16), sd((4 + steps, width), f32),
                   sd((rows, width), f32), *grads],
        compiler_params=params(),
        cost_estimate=cost(60),
        name="ffn_both",
    )(idx, x, t, att, cot, vecs, upb, *pieces)


def gqkv_kernel(split, idx_ref, normed_ref, gp_ref, *rest):
    outs, nt = rest[:-1], rest[-1]

    @pl.when(pl.program_id(0) == 0)
    def _():
        nt[...] = normed_ref[...].T

    grad = dot(nt[...], gp_ref[...])
    if split:
        keep, send = split_cores(grad, lax.rem(idx_ref[0], 2), split)
        outs[0][...] = keep.astype(bf16)
        outs[1][...] = send.astype(bf16)
    else:
        outs[0][0] = grad.astype(bf16)


def qkv_weight_grad(idx, normed, gp, split):
    rows, width = normed.shape
    sd = jax.ShapeDtypeStruct
    if split:
        half, r = split // 2, width // split
        out_specs = [pl.BlockSpec((half, r, width), lambda j, *_: (0, j, 0))] * 2
        out_shape = [sd((half, 3 * r, width), bf16)] * 2
    else:
        out_specs = [pl.BlockSpec((1, width, width), lambda j, *_: (j, 0, 0))]
        out_shape = [sd((3, width, width), bf16)]
    return pl.pallas_call(
        functools.partial(gqkv_kernel, split),
        grid_spec=pltpu.PrefetchScalarGridSpec(
            num_scalar_prefetch=1,
            grid=(3,),
            in_specs=[whole_spec((rows, width)), pl.BlockSpec((rows, width), lambda j, *_: (0, j))],
            out_specs=out_specs,
            scratch_shapes=[pltpu.VMEM((width, rows), bf16)],
        ),
        out_shape=out_shape,
        compiler_params=params(),
        cost_estimate=cost(2),
        name="qkv_weight_grad",
    )(idx, normed, gp)


def first_kernel(n, idx_ref, x_ref, t_ref, gm_ref, gp_ref, vec_ref, *rest):
    pieces, (gi_ref, gvec_ref, w_scr, sem) = rest[:n], rest[n:]
    i = pl.program_id(0)
    width = x_ref.shape[1]

    @pl.when(i == 0)
    def _():
        copies = qkv_copies(idx_ref, pieces, w_scr, sem)
        for c in copies:
            c.start()
        gvec_ref[...] = jnp.zeros_like(gvec_ref)
        for c in copies:
            c.wait()

    sums = None
    dns = [dot(gp_ref[rs, :], w_scr[...], NT) for rs in sub_tiles()]
    for rs, dn in zip(sub_tiles(), dns):
        t = t_ref[rs, :]
        start = x_ref[rs, :].astype(f32) + t * vec_ref[0:1, :]
        xhat, rstd = ln_parts(start)
        gs = gm_ref[rs, :] + ln_back(xhat, rstd, dn, vec_ref[1:2, :])
        gi_ref[rs, :] = gs.astype(bf16)
        parts = [t * gs, dn * xhat, dn, gp_ref[rs, :width].astype(f32), gp_ref[rs, 2 * width :].astype(f32)]
        parts = [rows_sum(v) for v in parts]
        sums = parts if sums is None else [a + b for a, b in zip(sums, parts)]
    gvec_ref[...] += jnp.concatenate(sums + [jnp.zeros((3, width), f32)], axis=0)


def first_backward(idx, x, t, gm, gp, vecs, pieces):
    rows, width = x.shape
    n = len(pieces)
    sd = jax.ShapeDtypeStruct
    return pl.pallas_call(
        functools.partial(first_kernel, n),
        grid_spec=pltpu.PrefetchScalarGridSpec(
            num_scalar_prefetch=1,
            grid=(rows // BLOCK,),
            in_specs=[row_spec(width, BLOCK), row_spec(1, BLOCK), row_spec(width, BLOCK), row_spec(3 * width, BLOCK), whole_spec(vecs.shape)] + [any_spec()] * n,
            out_specs=[row_spec(width, BLOCK), whole_spec((8, width))],
            scratch_shapes=[pltpu.VMEM((width, 3 * width), bf16), pltpu.SemaphoreType.DMA((n,))],
        ),
        out_shape=[sd((rows, width), bf16), sd((8, width), f32)],
        compiler_params=params(),
        cost_estimate=cost(3),
        name="first_backward",
    )(idx, x, t, gm, gp, vecs, *pieces)


SHARDS = 8


def swap(value, axis, size, bit_mask):
    return lax.ppermute(value, axis, [(i, i ^ bit_mask) for i in range(size)])


def near(value):
    return swap(value, "fsdp", SHARDS, 1)


def along_x(value):
    return swap(value, "fsdp", SHARDS, 2)


def along_y(value):
    return swap(value, "fsdp", SHARDS, 4)


def with_near(far):
    pieces = []
    for piece in far:
        pieces += [piece, near(piece)]
    return pieces


def in_order(pieces, order):
    stacked = pieces.astype(f32)
    hit = (jnp.arange(stacked.shape[0])[:, None] == order[None, :]).astype(f32)
    return jnp.sum(hit.reshape(hit.shape + (1,) * (stacked.ndim - 1)) * stacked[None], axis=1)


def blocks_of(weight, width):
    r = weight.shape[0]
    return jnp.transpose(weight.reshape(r, -1, width), (1, 0, 2)).reshape(-1, width)


def add_low(*terms):
    total = terms[0].astype(f32)
    for term in terms[1:]:
        total = total + term.astype(f32)
    return total.astype(terms[0].dtype)


def place_rows(arrays, spot, mask, rows):
    return [lax.dynamic_index_in_dim(v, (spot // 2) ^ mask, 0, keepdims=False)[rows] for v in arrays]


def cut_of(arrays):
    cut = arrays[0].shape[1] // 32 * 16
    return slice(None, cut), slice(cut, None)


def far_first(arrays, spot):
    top, low = cut_of(arrays)
    total = lambda mask, rows: add_low(*place_rows(arrays, spot, mask, rows))
    return jnp.stack([total(1, top), total(3, top)]), jnp.stack([total(2, low), total(3, low)])


def far_second(arrays, from_x, from_y, spot):
    top, low = cut_of(arrays)
    total = lambda mask, rows, more: add_low(*place_rows(arrays, spot, mask, rows), more)
    own = total(0, top, from_x[0]), total(0, low, from_y[0])
    return own, total(2, top, from_x[1]), total(1, low, from_y[1])


def far_third(own, from_y, from_x):
    return add_low(own[0], from_y), add_low(own[1], from_x)


def halves(owned, spot):
    parts = owned.reshape(2, owned.shape[0] // 2, owned.shape[1])
    side = spot % 2
    return (
        lax.dynamic_index_in_dim(parts, side, 0, keepdims=False),
        lax.dynamic_index_in_dim(parts, 1 - side, 0, keepdims=False),
    )


def rows_first(kept, sent, size):
    return add_low(kept, swap(sent, "dp", size, 1))


def rows_middle(half, size):
    step = 2
    while step < size:
        half = add_low(half, swap(half, "dp", size, step))
        step *= 2
    return half


def rows_last(half, size, spot):
    other = swap(half, "dp", size, 1)
    even = spot % 2 == 0
    return jnp.concatenate([jnp.where(even, half, other), jnp.where(even, other, half)]).astype(f32)


def sum_owned(packed, spot, size):
    if size != SHARDS:
        return lax.psum_scatter(packed, "fsdp", scatter_dimension=0)
    total = lax.dynamic_index_in_dim(packed, spot, 0, keepdims=False)
    for m in range(1, size):
        total = total + swap(lax.dynamic_index_in_dim(packed, spot ^ m, 0, keepdims=False), "fsdp", size, m)
    return total


def sum_planes(value, size):
    terms = [value] + [swap(value, "dp", size, m) for m in range(1, size)]
    while len(terms) > 1:
        terms = [a + b for a, b in zip(terms[::2], terms[1::2])]
    return terms[0]


def on_device(
    sizes,
    inputs,
    time_of_row,
    coords,
    segment_ids,
    cotangent,
    time_weight,
    ln1_gain,
    ln1_bias,
    w_qkv,
    q_bias,
    v_bias,
    w_out,
    out_bias,
    kernel_mean,
    kernel_width,
    kernel_map,
    ln2_gain,
    ln2_bias,
    w_up,
    up_bias,
    w_down,
    down_bias,
):
    n, planes = sizes
    direct = n == SHARDS
    split = n if direct else 0
    barrier = lax.optimization_barrier
    spot = lax.axis_index("fsdp")
    level = lax.axis_index("dp")
    order = (spot ^ jnp.arange(n)).astype(jnp.int32)
    width = inputs.shape[1]
    r = w_qkv.shape[0]
    heads = kernel_map.shape[1]
    own_kernels = kernel_map.shape[0]
    kernels = own_kernels * n
    wide = up_bias.shape[0] // r
    ff = n * wide * r
    scale = (width // heads) ** (-0.5)
    times = time_of_row[:, None]

    vectors = (time_weight, ln1_gain, ln1_bias, q_bias, v_bias, out_bias, ln2_gain, ln2_bias, down_bias)
    if direct:
        lanes = 128
        pieces = [v[None] for v in vectors] + [up_bias.reshape(-1, lanes), kernel_mean[None], kernel_width[None], kernel_map]
        small = sum(
            jnp.pad(v, ((at, 32 - at - v.shape[0]), (0, lanes - v.shape[1])))
            for at, v in zip((*range(9), 9, 12, 13, 16), pieces)
        )
        pair = jnp.stack([small, near(small)])
        pair, w_first, w_second, coords, segment_ids, times = barrier(
            (pair, w_qkv, (w_out, w_up, w_down), coords, segment_ids, times)
        )
        small_far = [swap(pair, "fsdp", n, 2 * m) for m in range(1, n // 2)]
        qkv_far = [w_first] + [swap(w_first, "fsdp", n, 2 * m) for m in range(1, n // 2)]
        second = jnp.concatenate([w_second[0], blocks_of(w_second[1], width), w_second[2]])
        small_all = in_order(jnp.concatenate([pair] + small_far), order)
        vectors, up_bias_all = small_all[:, :9, :r], small_all[:, 9:12].reshape(1, ff)
        mean_all, width_all = (small_all[:, at, :own_kernels].reshape(kernels) for at in (12, 13))
        map_all = small_all[:, 16 : 16 + own_kernels, :heads].reshape(kernels, heads)
    else:
        gathered = lambda v: lax.all_gather(v, "fsdp", axis=0, tiled=True).astype(f32)
        vectors = lax.all_gather(jnp.stack(vectors), "fsdp", axis=0).astype(f32)
        up_bias_all, map_all = gathered(up_bias)[None], gathered(kernel_map)
        mean_all, width_all = gathered(kernel_mean), gathered(kernel_width)
        qkv_p = (lax.all_gather(w_qkv, "fsdp", axis=0, tiled=True),)
        ffn_p = tuple(lax.all_gather(w, "fsdp", axis=0, tiled=True) for w in (w_out, w_up, w_down))

    aux_win, aux_col = aux_of(coords, segment_ids)
    gmat, amat, kernel_columns = kernel_consts(mean_all, width_all, map_all.astype(bf16))
    done = attn_bias(0, aux_win, aux_col, gmat, amat, ())
    if direct:
        done, second, qkv_far = barrier((done, second, qkv_far))
        qkv_p = tuple(with_near(qkv_far))
        from_x, from_y = along_x(second), along_y(second)
    bias, feats = attn_bias(1, aux_win, aux_col, gmat, amat, done)
    vecs = jnp.transpose(vectors, (1, 0, 2)).reshape(9, width)

    def rows_of(*picked):
        return jnp.concatenate([vecs[p : p + 1] for p in picked] + [jnp.zeros((8 - len(picked), width), f32)])

    first_rows, ffn_rows, back_rows = rows_of(0, 1, 2, 3, 4), rows_of(0, 5, 6, 7, 8), rows_of(0, 1)
    if direct:
        bias, qkv_p, ready = barrier((bias, qkv_p, (first_rows, ffn_rows, back_rows, up_bias_all, amat, kernel_columns)))
        first_rows, ffn_rows, back_rows, up_bias_all, amat, kernel_columns = ready
    normed, queries, keys, values = qkv_forward(order, inputs, times, first_rows, qkv_p, scale)
    if direct:
        cut = (1 + wide) * r
        queries, from_x, from_y = barrier((queries, from_x, from_y))
        top_d, low_d = along_y(from_x[:cut]), along_x(from_y[cut:])
        ffn_p = with_near((second, from_x, from_y))
    attended, probs = attn_fwd(0, queries, keys, values, bias, ())
    if direct:
        attended, top_d, low_d, ffn_p = barrier((attended, top_d, low_d, ffn_p))
        ffn_p = tuple(ffn_p + with_near((top_d, low_d)))

    output, grad_attended, ffn_vecs, grad_middle, ffn_keep, ffn_send = ffn_both(
        order, inputs, times, attended, cotangent, ffn_rows, up_bias_all, ffn_p, ff, split
    )
    up_rows = wide * r

    def backward(part, before):
        return attn_bwd(part, queries, grad_attended, keys, values, probs, scale, before)

    def feat(part, before):
        return attn_feat(part, grad_scores, feats, aux_win, aux_col, amat, kernel_columns, before)

    def scattered(array, blocks):
        owned = lax.psum_scatter(array.reshape(blocks, n, -1, width), "fsdp", scatter_dimension=1)
        return owned.reshape(-1, width)

    if direct:
        a = (ffn_keep, near(ffn_send))
        done = backward(0, ())
        done, go_x, go_y = barrier((done, *far_first(a, spot)))
        from_x, from_y = along_x(go_x), along_y(go_y)
        grad_projected, grad_scores = backward(3, backward(2, backward(1, done)))
        qkv_keep, qkv_send = qkv_weight_grad(order, normed, grad_projected, split)
        qkv_keep, qkv_send, (own, go_y, go_x) = barrier((qkv_keep, qkv_send, far_second(a, from_x, from_y, spot)))
        from_y, from_x = along_y(go_y), along_x(go_x)
        c = (qkv_keep, near(qkv_send))
        c_go = far_first(c, spot)
    else:
        grad_projected, grad_scores = backward(3, backward(2, backward(1, backward(0, ()))))
        a = scattered(ffn_keep[:wide], wide)
        b = jnp.concatenate([scattered(ffn_send, 1), scattered(ffn_keep[wide:], 1)])
        qkv_owned = scattered(qkv_weight_grad(order, normed, grad_projected, split)[0], 3)
    grad_inputs, first_vecs = first_backward(
        order, inputs, times, grad_middle, grad_projected, back_rows, qkv_p
    )
    if direct:
        top, low = far_third(own, from_y, from_x)
        a, b = top[:up_rows], jnp.concatenate([top[up_rows:], low])
        a, b = halves(a, level), halves(b, level)
        grad_scores, first_vecs, a, b, c_go = barrier((grad_scores, first_vecs, a, b, c_go))
        c_from = along_x(c_go[0]), along_y(c_go[1])
    else:
        a, b = halves(a, level), halves(b, level)
    a, b = rows_first(*a, planes), rows_first(*b, planes)
    sums = feat(0, ())
    if direct:
        sums, a, (own, go_y, go_x) = barrier((sums, a, far_second(c, *c_from, spot)))
        from_y, from_x = along_y(go_y), along_x(go_x)
    a = rows_middle(a, planes)
    sums = feat(1, sums)
    if direct:
        qkv_owned = jnp.concatenate(far_third(own, from_y, from_x))
    sums, a, b, c = barrier((sums, a, b, halves(qkv_owned, level)))
    c = rows_first(*c, planes)
    b = rows_middle(b, planes)
    sums = feat(2, sums)
    sums, c = barrier((sums, c))
    c = rows_middle(c, planes)
    grad_up = rows_last(a, planes, level)
    kernel_part, b, c = barrier((feat(3, sums)[2], b, c))
    kernel_part = kernel_part.reshape(n, own_kernels, -1)
    grad_low, grad_qkv = rows_last(b, planes, level), rows_last(c, planes, level)

    lanes = kernel_part.shape[2]
    grad_rows = jnp.concatenate([first_vecs[:5], ffn_vecs[3:4], ffn_vecs[:3]]).reshape(9, n, r)
    grad_rows = jnp.pad(jnp.transpose(grad_rows, (1, 0, 2)), ((0, 0), (0, 0), (0, lanes - r)))
    up_bias_rows = ffn_vecs[4:].reshape(n, -1)
    up_bias_rows = jnp.pad(up_bias_rows, ((0, 0), (0, -up_bias_rows.shape[1] % lanes))).reshape(n, -1, lanes)
    vector_rows = jnp.concatenate([grad_rows, up_bias_rows], axis=1)
    small = sum_owned(jnp.concatenate([kernel_part, vector_rows], axis=1), spot, n)
    small, grad_up, grad_low, grad_qkv = barrier((small, grad_up, grad_low, grad_qkv))
    small = sum_planes(small, planes)
    gaussians, vectors = small[:own_kernels], small[own_kernels : own_kernels + 9, :r]
    grad_up_bias = small[own_kernels + 9 :].reshape(-1)[:up_rows]
    grad_down, grad_out = grad_low[:up_rows], grad_low[up_rows:]

    def columns(array):
        return jnp.transpose(array.reshape(-1, r, width), (1, 0, 2)).reshape(r, -1)

    return (
        output,
        grad_inputs,
        vectors[0],
        vectors[1],
        vectors[2],
        columns(grad_qkv),
        vectors[3],
        vectors[4],
        grad_out.astype(f32),
        vectors[5],
        gaussians[:, heads],
        gaussians[:, heads + 1],
        gaussians[:, :heads],
        vectors[6],
        vectors[7],
        columns(grad_up).astype(f32),
        grad_up_bias,
        grad_down.astype(f32),
        vectors[8],
    )


def solution(mesh):
    rows, split, whole = P(("fsdp", "dp"), None), P("fsdp"), P("fsdp", None)
    placed = (
        rows,
        P(("fsdp", "dp")),
        P(None, ("fsdp", "dp")),
        P(("fsdp", "dp")),
        rows,
        split,
        split,
        split,
        whole,
        split,
        split,
        whole,
        split,
        split,
        split,
        whole,
        split,
        split,
        whole,
        split,
        whole,
        split,
    )
    out_placed = (
        rows,
        rows,
        split,
        split,
        split,
        whole,
        split,
        split,
        whole,
        split,
        split,
        split,
        whole,
        split,
        split,
        whole,
        split,
        whole,
        split,
    )
    return jax.shard_map(
        functools.partial(on_device, (mesh.shape["fsdp"], mesh.shape["dp"])),
        mesh=mesh,
        in_specs=placed,
        out_specs=out_placed,
        check_vma=False,
    )
```

```python
import functools, math
import jax, jax.numpy as jnp
from jax import lax
from jax.experimental import pallas as pl
from jax.experimental.pallas import tpu as pltpu
from jax.sharding import PartitionSpec as P

SET = 256
CH = 32
STEP = 4
UNROLL = 4
PAIR = 4
FEAT_STEP = 2
WIN = 128
GROUPS = ((0, 0), (128, 8), (384, 16), (512, 24))
HW = 24
VM = 60 * 1024 * 1024
f32, bf16 = jnp.float32, jnp.bfloat16
NT = (((1,), (1,)), ((), ()))
TN = (((0,), (0,)), ((), ()))


def dot(a, b, dims=(((1,), (0,)), ((), ()))):
    return lax.dot_general(a, b, dims, preferred_element_type=f32)


def spread_heads(block, lane0, h0):
    wide = block.astype(f32)
    lanes = lax.broadcasted_iota(jnp.int32, (8, 256), 1) + lane0
    masks = [(lanes >= h * HW) & (lanes < (h + 1) * HW) for h in range(h0, h0 + 8)]
    zero = jnp.zeros((8, 256), f32)
    parts = [jnp.where(m, wide[8 * g : 8 * g + 8], zero) for g in range(4) for m in masks]
    return jnp.concatenate(parts, axis=0).astype(bf16)


def own_rows(full, lane0, h0):
    lanes = lax.broadcasted_iota(jnp.int32, (8, 256), 1) + lane0
    groups = []
    for g in range(4):
        out = jnp.zeros((8, 256), f32)
        for h in range(8):
            m = (lanes >= (h0 + h) * HW) & (lanes < (h0 + h + 1) * HW)
            out = jnp.where(m, full[64 * g + 8 * h : 64 * g + 8 * h + 8], out)
        groups.append(out)
    return jnp.concatenate(groups, axis=0)


def window_start(i):
    per = SET // CH
    base = i // per * SET
    return pl.multiple_of(jnp.clip(i * CH - 48, base, base + SET - WIN), 16)


def radius_of(ac, aw):
    d = ac[:, 0:1] - aw[0:1, :]
    s = d * d
    for j in (1, 2):
        d = ac[:, j : j + 1] - aw[j : j + 1, :]
        s = s + d * d
    return jnp.sqrt(s)


def per_chunk(body, unroll):
    if STEP == unroll:
        for t in range(STEP):
            body(t)
        return

    @pl.loop(0, STEP // unroll)
    def _(s):
        for t in range(unroll):
            body(s * unroll + t)


def chunk_rows(t):
    return pl.ds(pl.multiple_of(t * CH, CH), CH)


def parts3(v):
    high = v.astype(bf16).astype(f32)
    rest = v - high
    middle = rest.astype(bf16).astype(f32)
    return high, middle, (rest - middle).astype(bf16).astype(f32)


def distance_rows(ac, aw):
    rho = radius_of(ac, aw)
    rho = jnp.concatenate([rho[8 * g : 8 * g + 8] for g in range(4)], axis=1)
    (sh, sm, sl), (h, m, l) = parts3(rho * rho), parts3(rho)
    one = jnp.ones_like(rho)
    slots = [sh, sh, sm, sm, sh, sl, h, h, m, m, h, l, one, one, one, jnp.zeros_like(rho)]
    return jnp.concatenate(slots, axis=0).astype(bf16)


def bias_kernel(aw_ref, ac_ref, gmat_ref, amat_ref, b_ref, f_ref, t_scr):
    @pl.loop(0, STEP // PAIR)
    def _(s):
        chunks = [s * PAIR + u for u in range(PAIR)]
        ac = [ac_ref[chunk_rows(t), :] for t in chunks]
        aw = [aw_ref[t] for t in chunks]
        dist = [distance_rows(a, w) for a, w in zip(ac, aw)]
        e = [dot(gmat_ref[...], d) for d in dist]
        f = [jnp.exp2(v).astype(bf16) for v in e]
        bias = [dot(amat_ref[...], v, TN) for v in f]
        for u, t in enumerate(chunks):
            f_ref[t] = f[u]
            joined = ac[u][:, 3:4] == aw[u][3:4, :]
            for g in range(4):
                part = bias[u][:, 128 * g : 128 * g + 128].reshape(32, 8, WIN)
                part = jnp.where(joined[8 * g : 8 * g + 8][None], part, -1e30)
                for q in range(4):
                    t_scr[u, 256 * q + 64 * g : 256 * q + 64 * g + 64, :] = part[8 * q : 8 * q + 8].reshape(64, WIN)
        for u, t in enumerate(chunks):
            for n in range(8):
                b_ref[t, :, 128 * n : 128 * n + 128] = t_scr[u, 128 * n : 128 * n + 128, :].T


def fwd_kernel(q_ref, k_ref, v_ref, b_ref, o_ref, p_ref):
    def chunk(t):
        w = window_start(pl.program_id(0) * STEP + t)
        rt = chunk_rows(t)
        kwin = k_ref[pl.ds(w, WIN), :]
        vwin = v_ref[pl.ds(w, WIN), :]
        spans = [slice(lane0, lane0 + 256) for lane0, _ in GROUPS]
        wide = [spread_heads(q_ref[rt, sl], lane0, h0) for sl, (lane0, h0) in zip(spans, GROUPS)]
        s = [dot(kwin[:, sl], qm, NT) + b_ref[t, :, 256 * j : 256 * j + 256] for j, (sl, qm) in enumerate(zip(spans, wide))]
        e = [jnp.exp(v - jnp.max(v, axis=0, keepdims=True)) for v in s]
        pr = [(v * (1.0 / jnp.sum(v, axis=0, keepdims=True))).astype(bf16) for v in e]
        full = [dot(v, vwin[:, sl], TN) for sl, v in zip(spans, pr)]
        acc = [own_rows(v, *GROUPS[j]) for j, v in enumerate(full)]
        for j, v in enumerate(pr):
            p_ref[t, :, 256 * j : 256 * j + 256] = v
        store_lanes(o_ref, rt, acc)

    per_chunk(chunk, UNROLL)


def store_lanes(ref, rows, acc):
    for half in range(2):
        a, b = acc[2 * half], acc[2 * half + 1]
        full = jnp.concatenate([a[:, :128], a[:, 128:] + b[:, :128], b[:, 128:]], axis=1)
        ref[rows, 384 * half : 384 * half + 384] = full.astype(bf16)


def bwd_kernel(q_ref, do_ref, k_ref, v_ref, p_ref, gp_ref, ds_ref, dk_scr, dv_scr, *, scale):
    i = pl.program_id(0)
    width = 32 * HW

    @pl.when(i == 0)
    def _():
        dk_scr[...] = jnp.zeros_like(dk_scr)
        dv_scr[...] = jnp.zeros_like(dv_scr)

    def chunk(t):
        w = window_start(i * STEP + t)
        rt = chunk_rows(t)
        kwin = k_ref[pl.ds(w, WIN), :]
        vwin = v_ref[pl.ds(w, WIN), :]
        left = lax.broadcasted_iota(jnp.int32, (WIN, 128), 1) < 64
        spans = [slice(lane0, lane0 + 256) for lane0, _ in GROUPS]
        qm = [spread_heads(q_ref[rt, sl], lane0, h0) for sl, (lane0, h0) in zip(spans, GROUPS)]
        dom = [spread_heads(do_ref[rt, sl], lane0, h0) for sl, (lane0, h0) in zip(spans, GROUPS)]
        p_low = [p_ref[t, :, 256 * j : 256 * j + 256] for j in range(4)]
        dp = [dot(vwin[:, sl], v, NT) for sl, v in zip(spans, dom)]
        dv = [dot(a, b) for a, b in zip(p_low, dom)]
        pf = [v.astype(f32) for v in p_low]
        pd = [a * b for a, b in zip(pf, dp)]
        ds = [a - b * jnp.sum(a, axis=0, keepdims=True) for a, b in zip(pd, pf)]
        ds_low = [v.astype(bf16) for v in ds]
        full = [dot(v, kwin[:, sl], TN) for sl, v in zip(spans, ds_low)]
        dk = [dot(a, b) for a, b in zip(ds_low, qm)]
        acc = [own_rows(v, *GROUPS[j]) * scale for j, v in enumerate(full)]
        for j in (0, 2):
            for p in range(2):
                a, b = (ds[j + t][:, 128 * p : 128 * p + 128] for t in range(2))
                at = slice(64 * j, 64 * j + 128)
                ds_ref[t, 256 * p : 256 * p + WIN, at] = jnp.where(left, a, pltpu.roll(b, 64, 1)).astype(bf16)
                ds_ref[t, 256 * p + WIN : 256 * p + 256, at] = jnp.where(left, pltpu.roll(a, 64, 1), b).astype(bf16)
        for scr, parts in ((dk_scr, dk), (dv_scr, dv)):
            for half in range(2):
                a, b = parts[2 * half : 2 * half + 2]
                both = jnp.concatenate([a[:, :128], a[:, 128:] + b[:, :128], b[:, 128:]], axis=1)
                scr[pl.ds(w, WIN), 384 * half : 384 * half + 384] += both
        store_lanes(gp_ref, pl.ds(pl.multiple_of((i * STEP + t) * CH, CH), CH), acc)

    per_chunk(chunk, UNROLL)

    @pl.when(i == pl.num_programs(0) - 1)
    def _():
        gp_ref[:, width : 2 * width] = dk_scr[...].astype(bf16)
        gp_ref[:, 2 * width :] = dv_scr[...].astype(bf16)


def feat_kernel(n_before, last, ds_ref, f_ref, aw_ref, ac_ref, amat_ref, kcol_ref, *rest):
    before, (m_ref, s_ref, *out_ref, rho_scr, gf_scr, m0_ref) = rest[:n_before], rest[n_before:]

    @pl.when(pl.program_id(0) == 0)
    def _():
        m0_ref[...] = jnp.zeros_like(m0_ref)
        s_ref[...] = before[1][...] if before else jnp.zeros_like(s_ref)

    for u in range(FEAT_STEP):
        t = u
        rho = radius_of(ac_ref[chunk_rows(t), :], aw_ref[t])
        rho_scr[u] = jnp.concatenate([rho[8 * g : 8 * g + 8] for g in range(4)], axis=1)
    for u in range(FEAT_STEP):
        t = u
        for rb in range(4):
            span = slice(256 * rb, 256 * rb + 256)
            gf_scr[u, span, :] = dot(amat_ref[span, :], ds_ref[t], NT)
            m0_ref[span, :] += dot(f_ref[t, span, :], ds_ref[t])
            for kt in range(8):
                ks = slice(16 * kt, 16 * kt + 16)
                s1, s2 = s_ref[0, ks, :], s_ref[1, ks, :]
                for r in (2 * rb, 2 * rb + 1):
                    for g in range(4):
                        at = (u, slice(128 * r + 16 * kt, 128 * r + 16 * kt + 16), slice(128 * g, 128 * g + 128))
                        rr = rho_scr[u, r : r + 1, 128 * g : 128 * g + 128]
                        w = gf_scr[at] * f_ref[t, at[1], at[2]].astype(f32) * rr
                        s1 = s1 + w
                        s2 = s2 + w * rr
                s_ref[0, ks, :] = s1
                s_ref[1, ks, :] = s2

    @pl.when(pl.program_id(0) == pl.num_programs(0) - 1)
    def _():
        n = kcol_ref.shape[0]
        lanes = lax.broadcasted_iota(jnp.int32, (n, 256), 1)
        m = jnp.zeros((n, 256), f32)
        for r in range(8):
            m = jnp.where(lanes % 8 == r, m0_ref[n * r : n * r + n, :], m)
        if before:
            m = m + before[0][...]
        m_ref[...] = m
        if last:
            out_ref[0][...] = kernel_grads(m, s_ref, kcol_ref[...])


def kernel_grads(m, s_ref, kcol):
    n = kcol.shape[0]
    heads = lax.broadcasted_iota(jnp.int32, (256, 128), 0) // 8 == lax.broadcasted_iota(jnp.int32, (256, 128), 1)
    heads = heads.astype(f32).astype(bf16)
    g_map = sum(dot(v.astype(bf16), heads) for v in parts3(m))
    lanes = lax.broadcasted_iota(jnp.int32, (n, 128), 1)
    s0 = jnp.sum(jnp.where(lanes < 32, g_map * kcol, 0.0), axis=-1, keepdims=True)
    s1 = jnp.sum(s_ref[0], axis=-1, keepdims=True)
    s2 = jnp.sum(s_ref[1], axis=-1, keepdims=True)
    mean, width = kcol[:, 32:33], kcol[:, 33:34]
    square = width * width
    g_mean = (s1 - mean * s0) / square
    g_width = ((s2 - 2.0 * mean * s1 + mean * mean * s0) / square - s0) / width
    return jnp.where(lanes == 32, g_mean, jnp.where(lanes == 33, g_width, g_map))


def cost(micros):
    return pl.CostEstimate(flops=int(micros * 1.1535e9), bytes_accessed=0, transcendentals=0)


def full_spec(shape):
    return pl.BlockSpec(shape, lambda i: (0,) * len(shape))


def params(limit=VM):
    return pltpu.CompilerParams(vmem_limit_bytes=limit, dimension_semantics=("arbitrary",))


BIAS_PARTS = 2
FWD_PARTS = 1
BWD_PARTS = 4
FEAT_PARTS = 4


def shifted(spec_shape, base):
    return pl.BlockSpec(spec_shape, lambda i: (i + base,) + (0,) * (len(spec_shape) - 1))


def half_spec(shape, part):
    return pl.BlockSpec(shape, lambda i: (part,) + (0,) * (len(shape) - 1))


def attn_bias(part, aw, ac, gmat, amat, before):
    c = aw.shape[0]
    per = c // BIAS_PARTS // STEP
    base = part * per
    n_in = 4
    return pl.pallas_call(
        functools.partial(skip_refs, bias_kernel, n_in, len(before)),
        grid=(per,),
        in_specs=[
            shifted((STEP, 8, WIN), base), shifted((STEP * CH, 4), base), full_spec(gmat.shape), full_spec(amat.shape),
        ] + [pl.BlockSpec(memory_space=pl.ANY)] * len(before),
        out_specs=[shifted((STEP, WIN, 1024), base), shifted((STEP, 1024, 4 * WIN), base)],
        out_shape=[jax.ShapeDtypeStruct((c, WIN, 1024), f32), jax.ShapeDtypeStruct((c, 1024, 4 * WIN), bf16)],
        scratch_shapes=[pltpu.VMEM((PAIR, 1024, WIN), f32)],
        input_output_aliases={n_in + t: t for t in range(len(before))},
        compiler_params=params(),
        cost_estimate=cost(4 // BIAS_PARTS),
        name="attn_bias",
    )(aw, ac, gmat, amat, *before)


def attn_fwd(part, q, k, v, bias, before):
    rows, width = q.shape
    c = rows // CH
    per = c // FWD_PARTS // STEP
    base = part * per
    kv = half_spec((rows // FWD_PARTS, width), part)
    n_in = 4
    return pl.pallas_call(
        functools.partial(skip_refs, fwd_kernel, n_in, len(before)),
        grid=(per,),
        in_specs=[shifted((STEP * CH, width), base), kv, kv, shifted((STEP, WIN, 1024), base)]
        + [pl.BlockSpec(memory_space=pl.ANY)] * len(before),
        out_specs=[shifted((STEP * CH, width), base), shifted((STEP, WIN, 1024), base)],
        out_shape=[jax.ShapeDtypeStruct((rows, width), bf16), jax.ShapeDtypeStruct((c, WIN, 1024), bf16)],
        input_output_aliases={n_in + t: t for t in range(len(before))},
        compiler_params=params(),
        cost_estimate=cost(16 // FWD_PARTS),
        name="attn_fwd",
    )(q, k, v, bias, *before)


def skip_refs(kernel, n_in, n_before, *refs):
    kernel(*refs[:n_in], *refs[n_in + n_before :])


def attn_bwd(part, q, do, k, v, p, scale, before):
    rows, width = q.shape
    c = rows // CH
    per = c // BWD_PARTS // STEP
    base = part * per
    kv = half_spec((rows // BWD_PARTS, width), part)
    n_in = 5
    return pl.pallas_call(
        functools.partial(skip_refs, functools.partial(bwd_kernel, scale=scale), n_in, len(before)),
        grid=(per,),
        in_specs=[
            shifted((STEP * CH, width), base), shifted((STEP * CH, width), base), kv, kv,
            shifted((STEP, WIN, 1024), base),
        ] + [pl.BlockSpec(memory_space=pl.ANY)] * len(before),
        out_specs=[half_spec((rows // BWD_PARTS, 3 * width), part), shifted((STEP, 4 * WIN, 256), base)],
        out_shape=[jax.ShapeDtypeStruct((rows, 3 * width), bf16), jax.ShapeDtypeStruct((c, 4 * WIN, 256), bf16)],
        scratch_shapes=[pltpu.VMEM((rows // BWD_PARTS, width), f32)] * 2,
        input_output_aliases={n_in + t: t for t in range(len(before))},
        compiler_params=params(),
        cost_estimate=cost(2),
        name="attn_bwd",
    )(q, do, k, v, p, *before)


def attn_feat(part, ds, feats, aw, ac, amat, kcol, before):
    per = ds.shape[0] // FEAT_PARTS // FEAT_STEP
    base = part * per
    last = part == FEAT_PARTS - 1
    n = kcol.shape[0]
    shapes = [(n, 256), (2, n, WIN)] + [(n, 128)] * last
    return pl.pallas_call(
        functools.partial(feat_kernel, len(before), last),
        grid=(per,),
        in_specs=[
            shifted((FEAT_STEP, 4 * WIN, 256), base), shifted((FEAT_STEP, 1024, 4 * WIN), base),
            shifted((FEAT_STEP, 8, WIN), base), shifted((FEAT_STEP * CH, 4), base),
            full_spec(amat.shape), full_spec(kcol.shape),
        ] + [full_spec(b.shape) for b in before],
        out_specs=[full_spec(s) for s in shapes],
        out_shape=[jax.ShapeDtypeStruct(s, f32) for s in shapes],
        scratch_shapes=[
            pltpu.VMEM((FEAT_STEP, 8, 4 * WIN), f32), pltpu.VMEM((FEAT_STEP, 1024, 4 * WIN), f32), pltpu.VMEM((1024, 256), f32),
        ],
        compiler_params=params(),
        cost_estimate=cost(1),
        name="attn_feat",
    )(ds, feats, aw, ac, amat, kcol, *before)


def aux_of(coords, segment_ids):
    rows = coords.shape[1]
    place = jnp.arange(rows, dtype=jnp.int32) // SET
    key = (segment_ids * (rows // SET) + place).astype(f32)
    packed = jnp.concatenate([coords, key[None], jnp.zeros((4, rows), f32)], axis=0)
    half = SET
    starts = [b + min(max(i - 48, 0), half - WIN) for b in range(0, rows, half) for i in range(0, half, CH)]
    aw = jnp.stack([packed[:, s : s + WIN] for s in starts])
    ac = packed[:4].T
    return aw, ac


def split3(v):
    high = lax.reduce_precision(v, 8, 7)
    middle = lax.reduce_precision(v - high, 8, 7)
    return high, middle, lax.reduce_precision(v - high - middle, 8, 7)


def kernel_consts(mean, width, kmap):
    mean, width = mean.astype(f32), width.astype(f32)
    half = 0.5 * math.log2(math.e) / (width * width)
    ah, am, al = split3(-half)
    bh, bm, bl = split3(2.0 * half * mean)
    ch, cm, cl = split3(-half * mean * mean - jnp.log2(math.sqrt(2.0 * math.pi) * width))
    slots = jnp.stack([ah, am, ah, am, al, ah, bh, bm, bh, bm, bl, bh, ch, cm, cl, jnp.zeros_like(ah)], axis=1)
    eye = jnp.eye(8, dtype=f32)
    n, heads = kmap.shape
    gmat = (eye[:, None, None, :] * slots[None, :, :, None]).reshape(8 * n, 128).astype(bf16)
    amat = (eye[:, None, None, :] * kmap.astype(f32)[None, :, :, None]).reshape(8 * n, heads * 8).astype(bf16)
    kcol = jnp.concatenate([kmap.astype(f32), mean[:, None], width[:, None], jnp.zeros((n, 94), f32)], axis=1)
    return gmat, amat, kcol


TILE = 256
BLOCK = 512
epsilon = 1e-05


def ln_parts(v):
    mean = jnp.mean(v, axis=-1, keepdims=True)
    centred = v - mean
    rstd = lax.rsqrt(jnp.mean(centred * centred, axis=-1, keepdims=True) + epsilon)
    return centred * rstd, rstd


def ln_back(xhat, rstd, dn, gain):
    dg = dn * gain
    m1 = jnp.mean(dg, axis=-1, keepdims=True)
    m2 = jnp.mean(dg * xhat, axis=-1, keepdims=True)
    return rstd * (dg - m1 - xhat * m2)


def rows_sum(v):
    return jnp.sum(v, axis=0, keepdims=True)


def fetch(idx_ref, pieces, moves, sem, base=0):
    copies = []
    for m, (piece, top) in enumerate(pieces):
        for dest, first, column, rows, columns in moves:
            at = pl.multiple_of(idx_ref[m] * rows, 16)
            copies.append(
                pltpu.make_async_copy(
                    piece.at[pl.ds(top + first, rows), :],
                    dest.at[pl.ds(at, rows), pl.ds(column, columns)],
                    sem.at[base + len(copies)],
                )
            )
    return copies


def fetch_whole(arrays, dests, sem):
    return [pltpu.make_async_copy(a, d, sem.at[i]) for i, (a, d) in enumerate(zip(arrays, dests))]


def qkv_copies(idx_ref, pieces, w_scr, sem):
    if len(pieces) == 1:
        return fetch_whole(pieces, [w_scr], sem)
    r, columns = pieces[0].shape
    return fetch(idx_ref, [(p, 0) for p in pieces], [(w_scr, 0, 0, r, columns)], sem)


def ffn_copies(idx_ref, pieces, wo, up, down, sem):
    if len(pieces) == 3:
        copies = fetch_whole(pieces, [wo, up, down], sem)
        return copies[:1], copies[1:]
    width = wo.shape[0]
    n = len(pieces) - 2
    r = width // n
    wide = up.shape[1] // width
    cut = (1 + wide) * r
    tops = [(p, 0) for p in pieces[:n]]
    lows = [(p, cut) for p in pieces[: n - 2]] + [(p, 0) for p in pieces[n:]]
    first = fetch(idx_ref, tops, [(wo, 0, 0, r, width)], sem)
    moves = [(up, r + b * r, b * width, r, width) for b in range(wide)]
    later = fetch(idx_ref, tops, moves, sem, len(first))
    return first, later + fetch(idx_ref, lows, [(down, 0, 0, wide * r, width)], sem, len(first) + len(later))


def any_spec():
    return pl.BlockSpec(memory_space=pl.ANY)


def row_spec(width, tile=TILE):
    return pl.BlockSpec((tile, width), lambda i, *_: (i, 0))


def whole_spec(shape):
    return pl.BlockSpec(shape, lambda i, *_: (0,) * len(shape))


def sub_tiles():
    return [pl.ds(i * TILE, TILE) for i in range(BLOCK // TILE)]


def qkv_kernel(n, scale, idx_ref, x_ref, t_ref, vec_ref, *rest):
    pieces, (normed_ref, q_ref, k_ref, v_ref, w_scr, sem) = rest[:n], rest[n:]
    width = x_ref.shape[1]

    @pl.when(pl.program_id(0) == 0)
    def _():
        for c in qkv_copies(idx_ref, pieces, w_scr, sem):
            c.start()

    for rs in sub_tiles():
        start = x_ref[rs, :].astype(f32) + t_ref[rs, :] * vec_ref[0:1, :]
        normed_ref[rs, :] = (ln_parts(start)[0] * vec_ref[1:2, :] + vec_ref[2:3, :]).astype(bf16)

    @pl.when(pl.program_id(0) == 0)
    def _():
        for c in qkv_copies(idx_ref, pieces, w_scr, sem):
            c.wait()

    normed = normed_ref[...]
    q_ref[...] = ((dot(normed, w_scr[:, :width]) + vec_ref[3:4, :]) * scale).astype(bf16)
    k_ref[...] = dot(normed, w_scr[:, width : 2 * width]).astype(bf16)
    v_ref[...] = (dot(normed, w_scr[:, 2 * width :]) + vec_ref[4:5, :]).astype(bf16)


def qkv_forward(idx, x, t, vecs, pieces, scale):
    rows, width = x.shape
    n = len(pieces)
    out = jax.ShapeDtypeStruct((rows, width), bf16)
    return pl.pallas_call(
        functools.partial(qkv_kernel, n, scale),
        grid_spec=pltpu.PrefetchScalarGridSpec(
            num_scalar_prefetch=1,
            grid=(rows // BLOCK,),
            in_specs=[row_spec(width, BLOCK), row_spec(1, BLOCK), whole_spec(vecs.shape)] + [any_spec()] * n,
            out_specs=[row_spec(width, BLOCK)] * 4,
            scratch_shapes=[pltpu.VMEM((width, 3 * width), bf16), pltpu.SemaphoreType.DMA((n,))],
        ),
        out_shape=[out] * 4,
        compiler_params=params(),
        cost_estimate=cost(10),
        name="qkv_forward",
    )(idx, x, t, vecs, *pieces)


def gelu_parts(x):
    t = 1.0 / (1.0 + (0.3275911 * math.sqrt(0.5)) * jnp.abs(x))
    e = jnp.exp2((-0.5 * math.log2(math.e)) * (x * x))
    poly = t * (0.127414796 + t * (-0.142248368 + t * (0.7107068705 + t * (-0.7265760135 + t * 0.5307027145))))
    tail = poly * e
    cdf = jnp.where(x >= 0, 1.0 - tail, tail)
    return x * cdf, cdf + (x * (1.0 / math.sqrt(2.0 * math.pi))) * e


def split_cores(value, core, owners):
    rows, c = value.shape
    pairs = value.reshape(owners // 2, 2, rows // owners, c)
    even, odd = pairs[:, 0], pairs[:, 1]
    return jnp.where(core == 0, even, odd), jnp.where(core == 0, odd, even)


def ffn_kernel(n, split, steps, idx_ref, x_ref, t_ref, att_ref, cot_ref, vec_ref, upb_ref, *rest):
    pieces = rest[:n]
    (out_ref, ga_ref, gvec_ref, gm_hbm, keep_hbm, send_hbm,
     wo, up, down, mid, n2, acc, gn2, hid, gp, stage_up, stage_down, sem, out_sem, gm_sem) = rest[n:]
    j = pl.program_id(0)
    rows, width = x_ref.shape
    fc = hid.shape[1]
    tiles = rows // TILE
    core = lax.rem(idx_ref[0], 2)
    r = width // split if split else 0

    def moves(step):
        slot = lax.rem(step, 2)
        if not split:
            return [
                pltpu.make_async_copy(stage_up.at[slot], keep_hbm.at[step], out_sem.at[slot, 0]),
                pltpu.make_async_copy(stage_down.at[slot], send_hbm.at[pl.ds(step * fc, fc), :], out_sem.at[slot, 2]),
            ]
        pairs = fc // (2 * steps * r)
        up_at = pl.ds(pl.multiple_of(step * r, r), r)
        down_at = pl.ds(steps * r, steps * r)
        copies = []
        for s, dest in enumerate((keep_hbm, send_hbm)):
            copies.append(pltpu.make_async_copy(stage_up.at[slot, s], dest.at[:, up_at, :], out_sem.at[slot, s]))
            copies.append(
                pltpu.make_async_copy(
                    stage_down.at[slot, s], dest.at[pl.ds(step * pairs, pairs), down_at, :], out_sem.at[slot, 2 + s]
                )
            )
        return copies

    def out_copies():
        if not split:
            return [pltpu.make_async_copy(stage_up.at[0], keep_hbm.at[steps], out_sem.at[0, 0])]
        at = pl.ds(2 * steps * r, r)
        return [
            pltpu.make_async_copy(stage_up.at[0, s], dest.at[:, at, :], out_sem.at[0, s])
            for s, dest in enumerate((keep_hbm, send_hbm))
        ]

    def put(stage, slot, value, owners):
        if not split:
            stage[slot] = value.astype(bf16)
            return
        keep, send = split_cores(value, core, owners)
        stage[slot, 0] = keep.astype(bf16)
        stage[slot, 1] = send.astype(bf16)

    @pl.when(j == 0)
    def _():
        first, later = ffn_copies(idx_ref, pieces, wo, up, down, sem)
        for c in first + later:
            c.start()
        for c in first:
            c.wait()
        for i in range(tiles):
            rs = pl.ds(i * TILE, TILE)
            start = x_ref[rs, :].astype(f32) + t_ref[rs, :] * vec_ref[0:1, :]
            middle = start + dot(att_ref[rs, :], wo[...]) + vec_ref[1:2, :]
            mid[rs, :] = middle
            acc[rs, :] = middle + vec_ref[4:5, :]
            gn2[rs, :] = jnp.zeros((TILE, width), f32)
            normed = (ln_parts(middle)[0] * vec_ref[2:3, :] + vec_ref[3:4, :]).astype(bf16)
            n2[rs, :] = normed
        for c in later:
            c.wait()

    @pl.when(j > 1)
    def _():
        for c in moves(j - 2):
            c.wait()

    f0 = pl.multiple_of(j * fc, fc)
    up_c = up[:, pl.ds(f0, fc)]
    down_c = down[pl.ds(f0, fc), :]
    upb = upb_ref[...]
    gb = jnp.zeros((1, fc), f32)
    ahead = []

    def enter(i):
        rs = pl.ds(i * TILE, TILE)
        ahead.append((dot(n2[rs, :], up_c), dot(cot_ref[rs, :], down_c, NT)))

    enter(0)
    for i in range(tiles):
        rs = pl.ds(i * TILE, TILE)
        if i + 1 < tiles:
            enter(i + 1)
        pre, gh = ahead[i]
        h, slope = gelu_parts(pre + upb)
        h = h.astype(bf16)
        g = (gh * slope).astype(bf16)
        hid[rs, :] = h
        gp[rs, :] = g
        gb = gb + rows_sum(g.astype(f32))
        acc[rs, :] += dot(h, down_c)
        gn2[rs, :] += dot(g, up_c, NT)
    gvec_ref[pl.ds(4 + j, 1), :] = gb
    slot = lax.rem(j, 2)
    put(stage_down, slot, dot(hid[...], cot_ref[...], TN), 2 * (fc // (2 * steps * r)) if split else 0)
    put(stage_up, slot, dot(n2[...], gp[...], TN), split)
    for c in moves(j):
        c.start()

    @pl.when(j == steps - 1)
    def _():
        sums = [jnp.zeros((1, width), f32)] * 4
        for i in range(tiles):
            rs = pl.ds(i * TILE, TILE)
            out_ref[rs, :] = acc[rs, :].astype(bf16)
            xhat, rstd = ln_parts(mid[rs, :])
            dn = gn2[rs, :]
            cot = cot_ref[rs, :].astype(f32)
            gm = cot + ln_back(xhat, rstd, dn, vec_ref[2:3, :])
            mid[rs, :] = gm
            ga = gm.astype(bf16)
            hid[rs, :] = ga
            ga_ref[rs, :] = dot(ga, wo[...], NT).astype(bf16)
            sums = [s + rows_sum(v) for s, v in zip(sums, (dn * xhat, dn, cot, ga.astype(f32)))]
        gvec_ref[0:4, :] = jnp.concatenate(sums, axis=0)
        mid_copy = pltpu.make_async_copy(mid, gm_hbm, gm_sem)
        mid_copy.start()
        grad_out = dot(att_ref[...], hid[...], TN)
        for c in moves(j - 1) + moves(j):
            c.wait()
        put(stage_up, 0, grad_out, split)
        last = out_copies()
        for c in last:
            c.start()
        for c in last:
            c.wait()
        mid_copy.wait()


def ffn_both(idx, x, t, att, cot, vecs, upb, pieces, ff, split):
    rows, width = x.shape
    n = len(pieces)
    fc = width
    steps = ff // fc
    sd = jax.ShapeDtypeStruct
    V = pltpu.VMEM
    if split:
        half = split // 2
        r = width // split
        grads = [sd((half, (2 * steps + 1) * r, width), bf16)] * 2
        stages = [V((2, 2, half, r, width), bf16), V((2, 2, fc // (2 * steps * r), steps * r, width), bf16)]
    else:
        grads = [sd((steps + 1, width, width), bf16), sd((ff, width), bf16)]
        stages = [V((2, width, width), bf16)] * 2
    return pl.pallas_call(
        functools.partial(ffn_kernel, n, split, steps),
        grid_spec=pltpu.PrefetchScalarGridSpec(
            num_scalar_prefetch=1,
            grid=(steps,),
            in_specs=[whole_spec((rows, width)), whole_spec((rows, 1)), whole_spec((rows, width)), whole_spec((rows, width)),
                      whole_spec(vecs.shape), pl.BlockSpec((1, fc), lambda j, *_: (0, j))] + [any_spec()] * n,
            out_specs=[whole_spec((rows, width)), whole_spec((rows, width)), whole_spec((4 + steps, width)),
                       any_spec(), any_spec(), any_spec()],
            scratch_shapes=[V((width, width), bf16), V((width, ff), bf16), V((ff, width), bf16),
                            V((rows, width), f32), V((rows, width), bf16),
                            V((rows, width), f32), V((rows, width), f32),
                            V((rows, fc), bf16), V((rows, fc), bf16), *stages,
                            pltpu.SemaphoreType.DMA((6 * n,)), pltpu.SemaphoreType.DMA((2, 4)), pltpu.SemaphoreType.DMA],
        ),
        out_shape=[sd((rows, width), bf16), sd((rows, width), bf16), sd((4 + steps, width), f32),
                   sd((rows, width), f32), *grads],
        compiler_params=params(),
        cost_estimate=cost(60),
        name="ffn_both",
    )(idx, x, t, att, cot, vecs, upb, *pieces)


def gqkv_kernel(split, idx_ref, normed_ref, gp_ref, *rest):
    outs, nt = rest[:-1], rest[-1]

    @pl.when(pl.program_id(0) == 0)
    def _():
        nt[...] = normed_ref[...].T

    grad = dot(nt[...], gp_ref[...])
    if split:
        keep, send = split_cores(grad, lax.rem(idx_ref[0], 2), split)
        outs[0][...] = keep.astype(bf16)
        outs[1][...] = send.astype(bf16)
    else:
        outs[0][0] = grad.astype(bf16)


def qkv_weight_grad(idx, normed, gp, split):
    rows, width = normed.shape
    sd = jax.ShapeDtypeStruct
    if split:
        half, r = split // 2, width // split
        out_specs = [pl.BlockSpec((half, r, width), lambda j, *_: (0, j, 0))] * 2
        out_shape = [sd((half, 3 * r, width), bf16)] * 2
    else:
        out_specs = [pl.BlockSpec((1, width, width), lambda j, *_: (j, 0, 0))]
        out_shape = [sd((3, width, width), bf16)]
    return pl.pallas_call(
        functools.partial(gqkv_kernel, split),
        grid_spec=pltpu.PrefetchScalarGridSpec(
            num_scalar_prefetch=1,
            grid=(3,),
            in_specs=[whole_spec((rows, width)), pl.BlockSpec((rows, width), lambda j, *_: (0, j))],
            out_specs=out_specs,
            scratch_shapes=[pltpu.VMEM((width, rows), bf16)],
        ),
        out_shape=out_shape,
        compiler_params=params(),
        cost_estimate=cost(2),
        name="qkv_weight_grad",
    )(idx, normed, gp)


def first_kernel(n, idx_ref, x_ref, t_ref, gm_ref, gp_ref, vec_ref, *rest):
    pieces, (gi_ref, gvec_ref, w_scr, sem) = rest[:n], rest[n:]
    i = pl.program_id(0)
    width = x_ref.shape[1]

    @pl.when(i == 0)
    def _():
        copies = qkv_copies(idx_ref, pieces, w_scr, sem)
        for c in copies:
            c.start()
        gvec_ref[...] = jnp.zeros_like(gvec_ref)
        for c in copies:
            c.wait()

    sums = None
    dns = [dot(gp_ref[rs, :], w_scr[...], NT) for rs in sub_tiles()]
    for rs, dn in zip(sub_tiles(), dns):
        t = t_ref[rs, :]
        start = x_ref[rs, :].astype(f32) + t * vec_ref[0:1, :]
        xhat, rstd = ln_parts(start)
        gs = gm_ref[rs, :] + ln_back(xhat, rstd, dn, vec_ref[1:2, :])
        gi_ref[rs, :] = gs.astype(bf16)
        parts = [t * gs, dn * xhat, dn, gp_ref[rs, :width].astype(f32), gp_ref[rs, 2 * width :].astype(f32)]
        parts = [rows_sum(v) for v in parts]
        sums = parts if sums is None else [a + b for a, b in zip(sums, parts)]
    gvec_ref[...] += jnp.concatenate(sums + [jnp.zeros((3, width), f32)], axis=0)


def first_backward(idx, x, t, gm, gp, vecs, pieces):
    rows, width = x.shape
    n = len(pieces)
    sd = jax.ShapeDtypeStruct
    return pl.pallas_call(
        functools.partial(first_kernel, n),
        grid_spec=pltpu.PrefetchScalarGridSpec(
            num_scalar_prefetch=1,
            grid=(rows // BLOCK,),
            in_specs=[row_spec(width, BLOCK), row_spec(1, BLOCK), row_spec(width, BLOCK), row_spec(3 * width, BLOCK), whole_spec(vecs.shape)] + [any_spec()] * n,
            out_specs=[row_spec(width, BLOCK), whole_spec((8, width))],
            scratch_shapes=[pltpu.VMEM((width, 3 * width), bf16), pltpu.SemaphoreType.DMA((n,))],
        ),
        out_shape=[sd((rows, width), bf16), sd((8, width), f32)],
        compiler_params=params(),
        cost_estimate=cost(3),
        name="first_backward",
    )(idx, x, t, gm, gp, vecs, *pieces)


SHARDS = 8


def swap(value, axis, size, bit_mask):
    return lax.ppermute(value, axis, [(i, i ^ bit_mask) for i in range(size)])


def near(value):
    return swap(value, "fsdp", SHARDS, 1)


def along_x(value):
    return swap(value, "fsdp", SHARDS, 2)


def along_y(value):
    return swap(value, "fsdp", SHARDS, 4)


def with_near(far):
    pieces = []
    for piece in far:
        pieces += [piece, near(piece)]
    return pieces


def in_order(pieces, order):
    stacked = pieces.astype(f32)
    hit = (jnp.arange(stacked.shape[0])[:, None] == order[None, :]).astype(f32)
    return jnp.sum(hit.reshape(hit.shape + (1,) * (stacked.ndim - 1)) * stacked[None], axis=1)


def blocks_of(weight, width):
    r = weight.shape[0]
    return jnp.transpose(weight.reshape(r, -1, width), (1, 0, 2)).reshape(-1, width)


def add_low(*terms):
    total = terms[0].astype(f32)
    for term in terms[1:]:
        total = total + term.astype(f32)
    return total.astype(terms[0].dtype)


def place_rows(arrays, spot, mask, rows):
    return [lax.dynamic_index_in_dim(v, (spot // 2) ^ mask, 0, keepdims=False)[rows] for v in arrays]


def cut_of(arrays):
    cut = arrays[0].shape[1] // 32 * 16
    return slice(None, cut), slice(cut, None)


def far_first(arrays, spot):
    top, low = cut_of(arrays)
    total = lambda mask, rows: add_low(*place_rows(arrays, spot, mask, rows))
    return jnp.stack([total(1, top), total(3, top)]), jnp.stack([total(2, low), total(3, low)])


def far_second(arrays, from_x, from_y, spot):
    top, low = cut_of(arrays)
    total = lambda mask, rows, more: add_low(*place_rows(arrays, spot, mask, rows), more)
    return total(2, top, from_x[1]), total(1, low, from_y[1])


def far_third(arrays, from_x, from_y, last_y, last_x, spot):
    top, low = cut_of(arrays)
    total = lambda rows, *more: add_low(*place_rows(arrays, spot, 0, rows), *more)
    return total(top, from_x[0], last_y), total(low, from_y[0], last_x)


def halves(owned, spot):
    parts = owned.reshape(2, owned.shape[0] // 2, owned.shape[1])
    side = spot % 2
    return (
        lax.dynamic_index_in_dim(parts, side, 0, keepdims=False),
        lax.dynamic_index_in_dim(parts, 1 - side, 0, keepdims=False),
    )


def rows_first(kept, sent, size):
    return add_low(kept, swap(sent, "dp", size, 1))


def rows_middle(half, size):
    step = 2
    while step < size:
        half = add_low(half, swap(half, "dp", size, step))
        step *= 2
    return half


def rows_last(half, size, spot):
    other = swap(half, "dp", size, 1)
    even = spot % 2 == 0
    return jnp.concatenate([jnp.where(even, half, other), jnp.where(even, other, half)]).astype(f32)


def sum_owned(packed, tied, spot, size):
    if size != SHARDS:
        return lax.psum_scatter(packed, "fsdp", scatter_dimension=0)
    total = lax.dynamic_index_in_dim(packed, spot, 0, keepdims=False)
    for m in range(1, size):
        source = packed if m <= size // 2 else tied
        total = total + swap(lax.dynamic_index_in_dim(source, spot ^ m, 0, keepdims=False), "fsdp", size, m)
    return total


def sum_planes(value, size):
    terms = [value] + [swap(value, "dp", size, m) for m in range(1, size)]
    while len(terms) > 1:
        terms = [a + b for a, b in zip(terms[::2], terms[1::2])]
    return terms[0]


def on_device(
    sizes,
    inputs,
    time_of_row,
    coords,
    segment_ids,
    cotangent,
    time_weight,
    ln1_gain,
    ln1_bias,
    w_qkv,
    q_bias,
    v_bias,
    w_out,
    out_bias,
    kernel_mean,
    kernel_width,
    kernel_map,
    ln2_gain,
    ln2_bias,
    w_up,
    up_bias,
    w_down,
    down_bias,
):
    n, planes = sizes
    direct = n == SHARDS
    split = n if direct else 0
    barrier = lax.optimization_barrier
    spot = lax.axis_index("fsdp")
    level = lax.axis_index("dp")
    order = (spot ^ jnp.arange(n)).astype(jnp.int32)
    width = inputs.shape[1]
    r = w_qkv.shape[0]
    heads = kernel_map.shape[1]
    own_kernels = kernel_map.shape[0]
    kernels = own_kernels * n
    wide = up_bias.shape[0] // r
    ff = n * wide * r
    scale = (width // heads) ** (-0.5)
    times = time_of_row[:, None]

    vectors = (time_weight, ln1_gain, ln1_bias, q_bias, v_bias, out_bias, ln2_gain, ln2_bias, down_bias)
    if direct:
        lanes = 128
        pieces = [v[None] for v in vectors] + [up_bias.reshape(-1, lanes), kernel_mean[None], kernel_width[None], kernel_map]
        small = sum(
            jnp.pad(v, ((at, 32 - at - v.shape[0]), (0, lanes - v.shape[1])))
            for at, v in zip((*range(9), 9, 12, 13, 16), pieces)
        )
        pair = jnp.stack([small, near(small)])
        pair, w_first, w_second, coords, segment_ids, times = barrier(
            (pair, w_qkv, (w_out, w_up, w_down), coords, segment_ids, times)
        )
        small_far = [swap(pair, "fsdp", n, 2 * m) for m in range(1, n // 2)]
        qkv_far = [w_first] + [swap(w_first, "fsdp", n, 2 * m) for m in range(1, n // 2)]
        second = jnp.concatenate([w_second[0], blocks_of(w_second[1], width), w_second[2]])
        small_all = in_order(jnp.concatenate([pair] + small_far), order)
        vectors, up_bias_all = small_all[:, :9, :r], small_all[:, 9:12].reshape(1, ff)
        mean_all, width_all = (small_all[:, at, :own_kernels].reshape(kernels) for at in (12, 13))
        map_all = small_all[:, 16 : 16 + own_kernels, :heads].reshape(kernels, heads)
    else:
        gathered = lambda v: lax.all_gather(v, "fsdp", axis=0, tiled=True).astype(f32)
        vectors = lax.all_gather(jnp.stack(vectors), "fsdp", axis=0).astype(f32)
        up_bias_all, map_all = gathered(up_bias)[None], gathered(kernel_map)
        mean_all, width_all = gathered(kernel_mean), gathered(kernel_width)
        qkv_p = (lax.all_gather(w_qkv, "fsdp", axis=0, tiled=True),)
        ffn_p = tuple(lax.all_gather(w, "fsdp", axis=0, tiled=True) for w in (w_out, w_up, w_down))

    aux_win, aux_col = aux_of(coords, segment_ids)
    gmat, amat, kernel_columns = kernel_consts(mean_all, width_all, map_all.astype(bf16))
    done = attn_bias(0, aux_win, aux_col, gmat, amat, ())
    if direct:
        done, second, qkv_far = barrier((done, second, qkv_far))
        qkv_p = tuple(with_near(qkv_far))
        from_x, from_y = along_x(second), along_y(second)
    bias, feats = attn_bias(1, aux_win, aux_col, gmat, amat, done)
    vecs = jnp.transpose(vectors, (1, 0, 2)).reshape(9, width)

    def rows_of(*picked):
        return jnp.concatenate([vecs[p : p + 1] for p in picked] + [jnp.zeros((8 - len(picked), width), f32)])

    first_rows, ffn_rows, back_rows = rows_of(0, 1, 2, 3, 4), rows_of(0, 5, 6, 7, 8), rows_of(0, 1)
    if direct:
        bias, qkv_p, ready = barrier((bias, qkv_p, (first_rows, ffn_rows, back_rows, up_bias_all, amat, kernel_columns)))
        first_rows, ffn_rows, back_rows, up_bias_all, amat, kernel_columns = ready
    normed, queries, keys, values = qkv_forward(order, inputs, times, first_rows, qkv_p, scale)
    if direct:
        cut = (1 + wide) * r
        queries, from_x, from_y = barrier((queries, from_x, from_y))
        top_d, low_d = along_y(from_x[:cut]), along_x(from_y[cut:])
        ffn_p = with_near((second, from_x, from_y))
    attended, probs = attn_fwd(0, queries, keys, values, bias, ())
    if direct:
        attended, top_d, low_d, ffn_p = barrier((attended, top_d, low_d, ffn_p))
        ffn_p = tuple(ffn_p + with_near((top_d, low_d)))

    output, grad_attended, ffn_vecs, grad_middle, ffn_keep, ffn_send = ffn_both(
        order, inputs, times, attended, cotangent, ffn_rows, up_bias_all, ffn_p, ff, split
    )
    up_rows = wide * r

    def backward(part, before):
        return attn_bwd(part, queries, grad_attended, keys, values, probs, scale, before)

    def feat(part, before):
        return attn_feat(part, grad_scores, feats, aux_win, aux_col, amat, kernel_columns, before)

    def scattered(array, blocks):
        owned = lax.psum_scatter(array.reshape(blocks, n, -1, width), "fsdp", scatter_dimension=1)
        return owned.reshape(-1, width)

    if direct:
        a = (ffn_keep, near(ffn_send))
        done = backward(0, ())
        done, go_x, go_y = barrier((done, *far_first(a, spot)))
        from_x, from_y = along_x(go_x), along_y(go_y)
        grad_projected, grad_scores = backward(3, backward(2, backward(1, done)))
        qkv_keep, qkv_send = qkv_weight_grad(order, normed, grad_projected, split)
        a_from = from_x, from_y
        qkv_keep, qkv_send, (go_y, go_x) = barrier((qkv_keep, qkv_send, far_second(a, *a_from, spot)))
        a_last = along_y(go_y), along_x(go_x)
        c = (qkv_keep, near(qkv_send))
        c_go = far_first(c, spot)
    else:
        grad_projected, grad_scores = backward(3, backward(2, backward(1, backward(0, ()))))
        a = scattered(ffn_keep[:wide], wide)
        b = jnp.concatenate([scattered(ffn_send, 1), scattered(ffn_keep[wide:], 1)])
        qkv_owned = scattered(qkv_weight_grad(order, normed, grad_projected, split)[0], 3)
    grad_inputs, first_vecs = first_backward(
        order, inputs, times, grad_middle, grad_projected, back_rows, qkv_p
    )
    if direct:
        top, low = far_third(a, *a_from, *a_last, spot)
        a, b = top[:up_rows], jnp.concatenate([top[up_rows:], low])
        a, b = halves(a, level), halves(b, level)
        grad_scores, first_vecs, a, b, c_go = barrier((grad_scores, first_vecs, a, b, c_go))
        c_from = along_x(c_go[0]), along_y(c_go[1])
    else:
        a, b = halves(a, level), halves(b, level)
    a, b = rows_first(*a, planes), rows_first(*b, planes)
    sums = feat(0, ())
    if direct:
        sums, a, (go_y, go_x) = barrier((sums, a, far_second(c, *c_from, spot)))
        c_last = along_y(go_y), along_x(go_x)
    a = rows_middle(a, planes)
    sums = feat(1, sums)
    if direct:
        qkv_owned = jnp.concatenate(far_third(c, *c_from, *c_last, spot))
    sums, a, b, c = barrier((sums, a, b, halves(qkv_owned, level)))
    c = rows_first(*c, planes)
    b = rows_middle(b, planes)
    sums = feat(2, sums)
    sums, c = barrier((sums, c))
    c = rows_middle(c, planes)
    grad_up = rows_last(a, planes, level)
    kernel_part = feat(3, sums)[2].reshape(n, own_kernels, -1)

    lanes = kernel_part.shape[2]
    grad_rows = jnp.concatenate([first_vecs[:5], ffn_vecs[3:4], ffn_vecs[:3]]).reshape(9, n, r)
    grad_rows = jnp.pad(jnp.transpose(grad_rows, (1, 0, 2)), ((0, 0), (0, 0), (0, lanes - r)))
    up_bias_rows = ffn_vecs[4:].reshape(n, -1)
    up_bias_rows = jnp.pad(up_bias_rows, ((0, 0), (0, -up_bias_rows.shape[1] % lanes))).reshape(n, -1, lanes)
    vector_rows = jnp.concatenate([grad_rows, up_bias_rows], axis=1)
    packed = jnp.concatenate([kernel_part, vector_rows], axis=1)
    tied, b, c = barrier((packed, b, c))
    grad_low, grad_qkv = rows_last(b, planes, level), rows_last(c, planes, level)
    small = sum_owned(packed, tied, spot, n)
    small, grad_up, grad_low, grad_qkv = barrier((small, grad_up, grad_low, grad_qkv))
    small = sum_planes(small, planes)
    gaussians, vectors = small[:own_kernels], small[own_kernels : own_kernels + 9, :r]
    grad_up_bias = small[own_kernels + 9 :].reshape(-1)[:up_rows]
    grad_down, grad_out = grad_low[:up_rows], grad_low[up_rows:]

    def columns(array):
        return jnp.transpose(array.reshape(-1, r, width), (1, 0, 2)).reshape(r, -1)

    return (
        output,
        grad_inputs,
        vectors[0],
        vectors[1],
        vectors[2],
        columns(grad_qkv),
        vectors[3],
        vectors[4],
        grad_out.astype(f32),
        vectors[5],
        gaussians[:, heads],
        gaussians[:, heads + 1],
        gaussians[:, :heads],
        vectors[6],
        vectors[7],
        columns(grad_up).astype(f32),
        grad_up_bias,
        grad_down.astype(f32),
        vectors[8],
    )


def solution(mesh):
    rows, split, whole = P(("fsdp", "dp"), None), P("fsdp"), P("fsdp", None)
    placed = (
        rows,
        P(("fsdp", "dp")),
        P(None, ("fsdp", "dp")),
        P(("fsdp", "dp")),
        rows,
        split,
        split,
        split,
        whole,
        split,
        split,
        whole,
        split,
        split,
        split,
        whole,
        split,
        split,
        whole,
        split,
        whole,
        split,
    )
    out_placed = (
        rows,
        rows,
        split,
        split,
        split,
        whole,
        split,
        split,
        whole,
        split,
        split,
        split,
        whole,
        split,
        split,
        whole,
        split,
        whole,
        split,
    )
    return jax.shard_map(
        functools.partial(on_device, (mesh.shape["fsdp"], mesh.shape["dp"])),
        mesh=mesh,
        in_specs=placed,
        out_specs=out_placed,
        check_vma=False,
    )
```

```python
import functools, math
import jax, jax.numpy as jnp
from jax import lax
from jax.experimental import pallas as pl
from jax.experimental.pallas import tpu as pltpu
from jax.sharding import PartitionSpec as P

SET = 256
CH = 32
STEP = 4
UNROLL = 4
PAIR = 4
FEAT_STEP = 2
WIN = 128
GROUPS = ((0, 0), (128, 8), (384, 16), (512, 24))
HW = 24
VM = 60 * 1024 * 1024
f32, bf16 = jnp.float32, jnp.bfloat16
NT = (((1,), (1,)), ((), ()))
TN = (((0,), (0,)), ((), ()))


def dot(a, b, dims=(((1,), (0,)), ((), ()))):
    return lax.dot_general(a, b, dims, preferred_element_type=f32)


def spread_heads(block, lane0, h0):
    wide = block.astype(f32)
    lanes = lax.broadcasted_iota(jnp.int32, (8, 256), 1) + lane0
    masks = [(lanes >= h * HW) & (lanes < (h + 1) * HW) for h in range(h0, h0 + 8)]
    zero = jnp.zeros((8, 256), f32)
    parts = [jnp.where(m, wide[8 * g : 8 * g + 8], zero) for g in range(4) for m in masks]
    return jnp.concatenate(parts, axis=0).astype(bf16)


def own_rows(full, lane0, h0):
    lanes = lax.broadcasted_iota(jnp.int32, (8, 256), 1) + lane0
    groups = []
    for g in range(4):
        out = jnp.zeros((8, 256), f32)
        for h in range(8):
            m = (lanes >= (h0 + h) * HW) & (lanes < (h0 + h + 1) * HW)
            out = jnp.where(m, full[64 * g + 8 * h : 64 * g + 8 * h + 8], out)
        groups.append(out)
    return jnp.concatenate(groups, axis=0)


def window_start(i):
    per = SET // CH
    base = i // per * SET
    return pl.multiple_of(jnp.clip(i * CH - 48, base, base + SET - WIN), 16)


def radius_of(ac, aw):
    d = ac[:, 0:1] - aw[0:1, :]
    s = d * d
    for j in (1, 2):
        d = ac[:, j : j + 1] - aw[j : j + 1, :]
        s = s + d * d
    return jnp.sqrt(s)


def per_chunk(body, unroll):
    if STEP == unroll:
        for t in range(STEP):
            body(t)
        return

    @pl.loop(0, STEP // unroll)
    def _(s):
        for t in range(unroll):
            body(s * unroll + t)


def chunk_rows(t):
    return pl.ds(pl.multiple_of(t * CH, CH), CH)


def parts3(v):
    high = v.astype(bf16).astype(f32)
    rest = v - high
    middle = rest.astype(bf16).astype(f32)
    return high, middle, (rest - middle).astype(bf16).astype(f32)


def distance_rows(ac, aw):
    rho = radius_of(ac, aw)
    rho = jnp.concatenate([rho[8 * g : 8 * g + 8] for g in range(4)], axis=1)
    (sh, sm, sl), (h, m, l) = parts3(rho * rho), parts3(rho)
    one = jnp.ones_like(rho)
    slots = [sh, sh, sm, sm, sh, sl, h, h, m, m, h, l, one, one, one, jnp.zeros_like(rho)]
    return jnp.concatenate(slots, axis=0).astype(bf16)


def bias_kernel(aw_ref, ac_ref, gmat_ref, amat_ref, b_ref, f_ref, t_scr):
    @pl.loop(0, STEP // PAIR)
    def _(s):
        chunks = [s * PAIR + u for u in range(PAIR)]
        ac = [ac_ref[chunk_rows(t), :] for t in chunks]
        aw = [aw_ref[t] for t in chunks]
        dist = [distance_rows(a, w) for a, w in zip(ac, aw)]
        e = [dot(gmat_ref[...], d) for d in dist]
        f = [jnp.exp2(v).astype(bf16) for v in e]
        bias = [dot(amat_ref[...], v, TN) for v in f]
        for u, t in enumerate(chunks):
            f_ref[t] = f[u]
            joined = ac[u][:, 3:4] == aw[u][3:4, :]
            for g in range(4):
                part = bias[u][:, 128 * g : 128 * g + 128].reshape(32, 8, WIN)
                part = jnp.where(joined[8 * g : 8 * g + 8][None], part, -1e30)
                for q in range(4):
                    t_scr[u, 256 * q + 64 * g : 256 * q + 64 * g + 64, :] = part[8 * q : 8 * q + 8].reshape(64, WIN)
        for u, t in enumerate(chunks):
            for n in range(8):
                b_ref[t, :, 128 * n : 128 * n + 128] = t_scr[u, 128 * n : 128 * n + 128, :].T


def fwd_kernel(q_ref, k_ref, v_ref, b_ref, o_ref, p_ref):
    def chunk(t):
        w = window_start(pl.program_id(0) * STEP + t)
        rt = chunk_rows(t)
        kwin = k_ref[pl.ds(w, WIN), :]
        vwin = v_ref[pl.ds(w, WIN), :]
        spans = [slice(lane0, lane0 + 256) for lane0, _ in GROUPS]
        wide = [spread_heads(q_ref[rt, sl], lane0, h0) for sl, (lane0, h0) in zip(spans, GROUPS)]
        s = [dot(kwin[:, sl], qm, NT) + b_ref[t, :, 256 * j : 256 * j + 256] for j, (sl, qm) in enumerate(zip(spans, wide))]
        e = [jnp.exp(v - jnp.max(v, axis=0, keepdims=True)) for v in s]
        pr = [(v * (1.0 / jnp.sum(v, axis=0, keepdims=True))).astype(bf16) for v in e]
        full = [dot(v, vwin[:, sl], TN) for sl, v in zip(spans, pr)]
        acc = [own_rows(v, *GROUPS[j]) for j, v in enumerate(full)]
        for j, v in enumerate(pr):
            p_ref[t, :, 256 * j : 256 * j + 256] = v
        store_lanes(o_ref, rt, acc)

    per_chunk(chunk, UNROLL)


def store_lanes(ref, rows, acc):
    for half in range(2):
        a, b = acc[2 * half], acc[2 * half + 1]
        full = jnp.concatenate([a[:, :128], a[:, 128:] + b[:, :128], b[:, 128:]], axis=1)
        ref[rows, 384 * half : 384 * half + 384] = full.astype(bf16)


def bwd_kernel(q_ref, do_ref, k_ref, v_ref, p_ref, gp_ref, ds_ref, dk_scr, dv_scr, *, scale):
    i = pl.program_id(0)
    width = 32 * HW

    @pl.when(i == 0)
    def _():
        dk_scr[...] = jnp.zeros_like(dk_scr)
        dv_scr[...] = jnp.zeros_like(dv_scr)

    def chunk(t):
        w = window_start(i * STEP + t)
        rt = chunk_rows(t)
        kwin = k_ref[pl.ds(w, WIN), :]
        vwin = v_ref[pl.ds(w, WIN), :]
        left = lax.broadcasted_iota(jnp.int32, (WIN, 128), 1) < 64
        spans = [slice(lane0, lane0 + 256) for lane0, _ in GROUPS]
        qm = [spread_heads(q_ref[rt, sl], lane0, h0) for sl, (lane0, h0) in zip(spans, GROUPS)]
        dom = [spread_heads(do_ref[rt, sl], lane0, h0) for sl, (lane0, h0) in zip(spans, GROUPS)]
        p_low = [p_ref[t, :, 256 * j : 256 * j + 256] for j in range(4)]
        dp = [dot(vwin[:, sl], v, NT) for sl, v in zip(spans, dom)]
        dv = [dot(a, b) for a, b in zip(p_low, dom)]
        pf = [v.astype(f32) for v in p_low]
        pd = [a * b for a, b in zip(pf, dp)]
        ds = [a - b * jnp.sum(a, axis=0, keepdims=True) for a, b in zip(pd, pf)]
        ds_low = [v.astype(bf16) for v in ds]
        full = [dot(v, kwin[:, sl], TN) for sl, v in zip(spans, ds_low)]
        dk = [dot(a, b) for a, b in zip(ds_low, qm)]
        acc = [own_rows(v, *GROUPS[j]) * scale for j, v in enumerate(full)]
        for j in (0, 2):
            for p in range(2):
                a, b = (ds[j + t][:, 128 * p : 128 * p + 128] for t in range(2))
                at = slice(64 * j, 64 * j + 128)
                ds_ref[t, 256 * p : 256 * p + WIN, at] = jnp.where(left, a, pltpu.roll(b, 64, 1)).astype(bf16)
                ds_ref[t, 256 * p + WIN : 256 * p + 256, at] = jnp.where(left, pltpu.roll(a, 64, 1), b).astype(bf16)
        for scr, parts in ((dk_scr, dk), (dv_scr, dv)):
            for half in range(2):
                a, b = parts[2 * half : 2 * half + 2]
                both = jnp.concatenate([a[:, :128], a[:, 128:] + b[:, :128], b[:, 128:]], axis=1)
                scr[pl.ds(w, WIN), 384 * half : 384 * half + 384] += both
        store_lanes(gp_ref, pl.ds(pl.multiple_of((i * STEP + t) * CH, CH), CH), acc)

    per_chunk(chunk, UNROLL)

    @pl.when(i == pl.num_programs(0) - 1)
    def _():
        gp_ref[:, width : 2 * width] = dk_scr[...].astype(bf16)
        gp_ref[:, 2 * width :] = dv_scr[...].astype(bf16)


def feat_kernel(n_before, last, ds_ref, f_ref, aw_ref, ac_ref, amat_ref, kcol_ref, *rest):
    before, (m_ref, s_ref, *out_ref, rho_scr, gf_scr, m0_ref) = rest[:n_before], rest[n_before:]

    @pl.when(pl.program_id(0) == 0)
    def _():
        m0_ref[...] = jnp.zeros_like(m0_ref)
        s_ref[...] = before[1][...] if before else jnp.zeros_like(s_ref)

    for u in range(FEAT_STEP):
        t = u
        rho = radius_of(ac_ref[chunk_rows(t), :], aw_ref[t])
        rho_scr[u] = jnp.concatenate([rho[8 * g : 8 * g + 8] for g in range(4)], axis=1)
    for u in range(FEAT_STEP):
        t = u
        for rb in range(4):
            span = slice(256 * rb, 256 * rb + 256)
            gf_scr[u, span, :] = dot(amat_ref[span, :], ds_ref[t], NT)
            m0_ref[span, :] += dot(f_ref[t, span, :], ds_ref[t])
            for kt in range(8):
                ks = slice(16 * kt, 16 * kt + 16)
                s1, s2 = s_ref[0, ks, :], s_ref[1, ks, :]
                for r in (2 * rb, 2 * rb + 1):
                    for g in range(4):
                        at = (u, slice(128 * r + 16 * kt, 128 * r + 16 * kt + 16), slice(128 * g, 128 * g + 128))
                        rr = rho_scr[u, r : r + 1, 128 * g : 128 * g + 128]
                        w = gf_scr[at] * f_ref[t, at[1], at[2]].astype(f32) * rr
                        s1 = s1 + w
                        s2 = s2 + w * rr
                s_ref[0, ks, :] = s1
                s_ref[1, ks, :] = s2

    @pl.when(pl.program_id(0) == pl.num_programs(0) - 1)
    def _():
        n = kcol_ref.shape[0]
        lanes = lax.broadcasted_iota(jnp.int32, (n, 256), 1)
        m = jnp.zeros((n, 256), f32)
        for r in range(8):
            m = jnp.where(lanes % 8 == r, m0_ref[n * r : n * r + n, :], m)
        if before:
            m = m + before[0][...]
        m_ref[...] = m
        if last:
            out_ref[0][...] = kernel_grads(m, s_ref, kcol_ref[...])


def kernel_grads(m, s_ref, kcol):
    n = kcol.shape[0]
    heads = lax.broadcasted_iota(jnp.int32, (256, 128), 0) // 8 == lax.broadcasted_iota(jnp.int32, (256, 128), 1)
    heads = heads.astype(f32).astype(bf16)
    g_map = sum(dot(v.astype(bf16), heads) for v in parts3(m))
    lanes = lax.broadcasted_iota(jnp.int32, (n, 128), 1)
    s0 = jnp.sum(jnp.where(lanes < 32, g_map * kcol, 0.0), axis=-1, keepdims=True)
    s1 = jnp.sum(s_ref[0], axis=-1, keepdims=True)
    s2 = jnp.sum(s_ref[1], axis=-1, keepdims=True)
    mean, width = kcol[:, 32:33], kcol[:, 33:34]
    square = width * width
    g_mean = (s1 - mean * s0) / square
    g_width = ((s2 - 2.0 * mean * s1 + mean * mean * s0) / square - s0) / width
    return jnp.where(lanes == 32, g_mean, jnp.where(lanes == 33, g_width, g_map))


def cost(micros):
    return pl.CostEstimate(flops=int(micros * 1.1535e9), bytes_accessed=0, transcendentals=0)


def full_spec(shape):
    return pl.BlockSpec(shape, lambda i: (0,) * len(shape))


def params(limit=VM):
    return pltpu.CompilerParams(vmem_limit_bytes=limit, dimension_semantics=("arbitrary",))


BIAS_PARTS = 2
FWD_PARTS = 1
BWD_PARTS = 4
FEAT_PARTS = 4


def shifted(spec_shape, base):
    return pl.BlockSpec(spec_shape, lambda i: (i + base,) + (0,) * (len(spec_shape) - 1))


def half_spec(shape, part):
    return pl.BlockSpec(shape, lambda i: (part,) + (0,) * (len(shape) - 1))


def attn_bias(part, aw, ac, gmat, amat, before):
    c = aw.shape[0]
    per = c // BIAS_PARTS // STEP
    base = part * per
    n_in = 4
    return pl.pallas_call(
        functools.partial(skip_refs, bias_kernel, n_in, len(before)),
        grid=(per,),
        in_specs=[
            shifted((STEP, 8, WIN), base), shifted((STEP * CH, 4), base), full_spec(gmat.shape), full_spec(amat.shape),
        ] + [pl.BlockSpec(memory_space=pl.ANY)] * len(before),
        out_specs=[shifted((STEP, WIN, 1024), base), shifted((STEP, 1024, 4 * WIN), base)],
        out_shape=[jax.ShapeDtypeStruct((c, WIN, 1024), f32), jax.ShapeDtypeStruct((c, 1024, 4 * WIN), bf16)],
        scratch_shapes=[pltpu.VMEM((PAIR, 1024, WIN), f32)],
        input_output_aliases={n_in + t: t for t in range(len(before))},
        compiler_params=params(),
        cost_estimate=cost(4 // BIAS_PARTS),
        name="attn_bias",
    )(aw, ac, gmat, amat, *before)


def attn_fwd(part, q, k, v, bias, before):
    rows, width = q.shape
    c = rows // CH
    per = c // FWD_PARTS // STEP
    base = part * per
    kv = half_spec((rows // FWD_PARTS, width), part)
    n_in = 4
    return pl.pallas_call(
        functools.partial(skip_refs, fwd_kernel, n_in, len(before)),
        grid=(per,),
        in_specs=[shifted((STEP * CH, width), base), kv, kv, shifted((STEP, WIN, 1024), base)]
        + [pl.BlockSpec(memory_space=pl.ANY)] * len(before),
        out_specs=[shifted((STEP * CH, width), base), shifted((STEP, WIN, 1024), base)],
        out_shape=[jax.ShapeDtypeStruct((rows, width), bf16), jax.ShapeDtypeStruct((c, WIN, 1024), bf16)],
        input_output_aliases={n_in + t: t for t in range(len(before))},
        compiler_params=params(),
        cost_estimate=cost(16 // FWD_PARTS),
        name="attn_fwd",
    )(q, k, v, bias, *before)


def skip_refs(kernel, n_in, n_before, *refs):
    kernel(*refs[:n_in], *refs[n_in + n_before :])


def attn_bwd(part, q, do, k, v, p, scale, before):
    rows, width = q.shape
    c = rows // CH
    per = c // BWD_PARTS // STEP
    base = part * per
    kv = half_spec((rows // BWD_PARTS, width), part)
    n_in = 5
    return pl.pallas_call(
        functools.partial(skip_refs, functools.partial(bwd_kernel, scale=scale), n_in, len(before)),
        grid=(per,),
        in_specs=[
            shifted((STEP * CH, width), base), shifted((STEP * CH, width), base), kv, kv,
            shifted((STEP, WIN, 1024), base),
        ] + [pl.BlockSpec(memory_space=pl.ANY)] * len(before),
        out_specs=[half_spec((rows // BWD_PARTS, 3 * width), part), shifted((STEP, 4 * WIN, 256), base)],
        out_shape=[jax.ShapeDtypeStruct((rows, 3 * width), bf16), jax.ShapeDtypeStruct((c, 4 * WIN, 256), bf16)],
        scratch_shapes=[pltpu.VMEM((rows // BWD_PARTS, width), f32)] * 2,
        input_output_aliases={n_in + t: t for t in range(len(before))},
        compiler_params=params(),
        cost_estimate=cost(2),
        name="attn_bwd",
    )(q, do, k, v, p, *before)


def attn_feat(part, ds, feats, aw, ac, amat, kcol, before):
    per = ds.shape[0] // FEAT_PARTS // FEAT_STEP
    base = part * per
    last = part == FEAT_PARTS - 1
    n = kcol.shape[0]
    shapes = [(n, 256), (2, n, WIN)] + [(n, 128)] * last
    return pl.pallas_call(
        functools.partial(feat_kernel, len(before), last),
        grid=(per,),
        in_specs=[
            shifted((FEAT_STEP, 4 * WIN, 256), base), shifted((FEAT_STEP, 1024, 4 * WIN), base),
            shifted((FEAT_STEP, 8, WIN), base), shifted((FEAT_STEP * CH, 4), base),
            full_spec(amat.shape), full_spec(kcol.shape),
        ] + [full_spec(b.shape) for b in before],
        out_specs=[full_spec(s) for s in shapes],
        out_shape=[jax.ShapeDtypeStruct(s, f32) for s in shapes],
        scratch_shapes=[
            pltpu.VMEM((FEAT_STEP, 8, 4 * WIN), f32), pltpu.VMEM((FEAT_STEP, 1024, 4 * WIN), f32), pltpu.VMEM((1024, 256), f32),
        ],
        compiler_params=params(),
        cost_estimate=cost(1),
        name="attn_feat",
    )(ds, feats, aw, ac, amat, kcol, *before)


def aux_of(coords, segment_ids):
    rows = coords.shape[1]
    place = jnp.arange(rows, dtype=jnp.int32) // SET
    key = (segment_ids * (rows // SET) + place).astype(f32)
    packed = jnp.concatenate([coords, key[None], jnp.zeros((4, rows), f32)], axis=0)
    half = SET
    starts = [b + min(max(i - 48, 0), half - WIN) for b in range(0, rows, half) for i in range(0, half, CH)]
    aw = jnp.stack([packed[:, s : s + WIN] for s in starts])
    ac = packed[:4].T
    return aw, ac


def split3(v):
    high = lax.reduce_precision(v, 8, 7)
    middle = lax.reduce_precision(v - high, 8, 7)
    return high, middle, lax.reduce_precision(v - high - middle, 8, 7)


def kernel_consts(mean, width, kmap):
    mean, width = mean.astype(f32), width.astype(f32)
    half = 0.5 * math.log2(math.e) / (width * width)
    ah, am, al = split3(-half)
    bh, bm, bl = split3(2.0 * half * mean)
    ch, cm, cl = split3(-half * mean * mean - jnp.log2(math.sqrt(2.0 * math.pi) * width))
    slots = jnp.stack([ah, am, ah, am, al, ah, bh, bm, bh, bm, bl, bh, ch, cm, cl, jnp.zeros_like(ah)], axis=1)
    eye = jnp.eye(8, dtype=f32)
    n, heads = kmap.shape
    gmat = (eye[:, None, None, :] * slots[None, :, :, None]).reshape(8 * n, 128).astype(bf16)
    amat = (eye[:, None, None, :] * kmap.astype(f32)[None, :, :, None]).reshape(8 * n, heads * 8).astype(bf16)
    kcol = jnp.concatenate([kmap.astype(f32), mean[:, None], width[:, None], jnp.zeros((n, 94), f32)], axis=1)
    return gmat, amat, kcol


TILE = 256
BLOCK = 512
epsilon = 1e-05


def ln_parts(v):
    mean = jnp.mean(v, axis=-1, keepdims=True)
    centred = v - mean
    rstd = lax.rsqrt(jnp.mean(centred * centred, axis=-1, keepdims=True) + epsilon)
    return centred * rstd, rstd


def ln_back(xhat, rstd, dn, gain):
    dg = dn * gain
    m1 = jnp.mean(dg, axis=-1, keepdims=True)
    m2 = jnp.mean(dg * xhat, axis=-1, keepdims=True)
    return rstd * (dg - m1 - xhat * m2)


def rows_sum(v):
    return jnp.sum(v, axis=0, keepdims=True)


def fetch(idx_ref, pieces, moves, sem, base=0):
    copies = []
    for m, (piece, top) in enumerate(pieces):
        for dest, first, column, rows, columns in moves:
            at = pl.multiple_of(idx_ref[m] * rows, 16)
            copies.append(
                pltpu.make_async_copy(
                    piece.at[pl.ds(top + first, rows), :],
                    dest.at[pl.ds(at, rows), pl.ds(column, columns)],
                    sem.at[base + len(copies)],
                )
            )
    return copies


def fetch_whole(arrays, dests, sem):
    return [pltpu.make_async_copy(a, d, sem.at[i]) for i, (a, d) in enumerate(zip(arrays, dests))]


def qkv_copies(idx_ref, pieces, w_scr, sem):
    if len(pieces) == 1:
        return fetch_whole(pieces, [w_scr], sem)
    r, columns = pieces[0].shape
    return fetch(idx_ref, [(p, 0) for p in pieces], [(w_scr, 0, 0, r, columns)], sem)


def ffn_copies(idx_ref, pieces, wo, up, down, sem):
    if len(pieces) == 3:
        copies = fetch_whole(pieces, [wo, up, down], sem)
        return copies[:1], copies[1:]
    width = wo.shape[0]
    n = len(pieces) - 2
    r = width // n
    wide = up.shape[1] // width
    cut = (1 + wide) * r
    tops = [(p, 0) for p in pieces[:n]]
    lows = [(p, cut) for p in pieces[: n - 2]] + [(p, 0) for p in pieces[n:]]
    first = fetch(idx_ref, tops, [(wo, 0, 0, r, width)], sem)
    moves = [(up, r + b * r, b * width, r, width) for b in range(wide)]
    later = fetch(idx_ref, tops, moves, sem, len(first))
    return first, later + fetch(idx_ref, lows, [(down, 0, 0, wide * r, width)], sem, len(first) + len(later))


def any_spec():
    return pl.BlockSpec(memory_space=pl.ANY)


def row_spec(width, tile=TILE):
    return pl.BlockSpec((tile, width), lambda i, *_: (i, 0))


def whole_spec(shape):
    return pl.BlockSpec(shape, lambda i, *_: (0,) * len(shape))


def sub_tiles():
    return [pl.ds(i * TILE, TILE) for i in range(BLOCK // TILE)]


def qkv_kernel(n, scale, idx_ref, x_ref, t_ref, vec_ref, *rest):
    pieces, (normed_ref, q_ref, k_ref, v_ref, w_scr, sem) = rest[:n], rest[n:]
    width = x_ref.shape[1]

    @pl.when(pl.program_id(0) == 0)
    def _():
        for c in qkv_copies(idx_ref, pieces, w_scr, sem):
            c.start()

    for rs in sub_tiles():
        start = x_ref[rs, :].astype(f32) + t_ref[rs, :] * vec_ref[0:1, :]
        normed_ref[rs, :] = (ln_parts(start)[0] * vec_ref[1:2, :] + vec_ref[2:3, :]).astype(bf16)

    @pl.when(pl.program_id(0) == 0)
    def _():
        for c in qkv_copies(idx_ref, pieces, w_scr, sem):
            c.wait()

    normed = normed_ref[...]
    q_ref[...] = ((dot(normed, w_scr[:, :width]) + vec_ref[3:4, :]) * scale).astype(bf16)
    k_ref[...] = dot(normed, w_scr[:, width : 2 * width]).astype(bf16)
    v_ref[...] = (dot(normed, w_scr[:, 2 * width :]) + vec_ref[4:5, :]).astype(bf16)


def qkv_forward(idx, x, t, vecs, pieces, scale):
    rows, width = x.shape
    n = len(pieces)
    out = jax.ShapeDtypeStruct((rows, width), bf16)
    return pl.pallas_call(
        functools.partial(qkv_kernel, n, scale),
        grid_spec=pltpu.PrefetchScalarGridSpec(
            num_scalar_prefetch=1,
            grid=(rows // BLOCK,),
            in_specs=[row_spec(width, BLOCK), row_spec(1, BLOCK), whole_spec(vecs.shape)] + [any_spec()] * n,
            out_specs=[row_spec(width, BLOCK)] * 4,
            scratch_shapes=[pltpu.VMEM((width, 3 * width), bf16), pltpu.SemaphoreType.DMA((n,))],
        ),
        out_shape=[out] * 4,
        compiler_params=params(),
        cost_estimate=cost(10),
        name="qkv_forward",
    )(idx, x, t, vecs, *pieces)


def gelu_parts(x):
    t = 1.0 / (1.0 + (0.3275911 * math.sqrt(0.5)) * jnp.abs(x))
    e = jnp.exp2((-0.5 * math.log2(math.e)) * (x * x))
    poly = t * (0.127414796 + t * (-0.142248368 + t * (0.7107068705 + t * (-0.7265760135 + t * 0.5307027145))))
    tail = poly * e
    cdf = jnp.where(x >= 0, 1.0 - tail, tail)
    return x * cdf, cdf + (x * (1.0 / math.sqrt(2.0 * math.pi))) * e


def split_cores(value, core, owners):
    rows, c = value.shape
    pairs = value.reshape(owners // 2, 2, rows // owners, c)
    even, odd = pairs[:, 0], pairs[:, 1]
    return jnp.where(core == 0, even, odd), jnp.where(core == 0, odd, even)


def ffn_kernel(n, split, steps, idx_ref, x_ref, t_ref, att_ref, cot_ref, vec_ref, upb_ref, *rest):
    pieces = rest[:n]
    (out_ref, ga_ref, gvec_ref, gm_hbm, keep_hbm, send_hbm,
     wo, up, down, mid, n2, acc, gn2, hid, gp, stage_up, stage_down, sem, out_sem, gm_sem) = rest[n:]
    j = pl.program_id(0)
    rows, width = x_ref.shape
    fc = hid.shape[1]
    tiles = rows // TILE
    core = lax.rem(idx_ref[0], 2)
    r = width // split if split else 0

    def moves(step):
        slot = lax.rem(step, 2)
        if not split:
            return [
                pltpu.make_async_copy(stage_up.at[slot], keep_hbm.at[step], out_sem.at[slot, 0]),
                pltpu.make_async_copy(stage_down.at[slot], send_hbm.at[pl.ds(step * fc, fc), :], out_sem.at[slot, 2]),
            ]
        pairs = fc // (2 * steps * r)
        up_at = pl.ds(pl.multiple_of(step * r, r), r)
        down_at = pl.ds(steps * r, steps * r)
        copies = []
        for s, dest in enumerate((keep_hbm, send_hbm)):
            copies.append(pltpu.make_async_copy(stage_up.at[slot, s], dest.at[:, up_at, :], out_sem.at[slot, s]))
            copies.append(
                pltpu.make_async_copy(
                    stage_down.at[slot, s], dest.at[pl.ds(step * pairs, pairs), down_at, :], out_sem.at[slot, 2 + s]
                )
            )
        return copies

    def out_copies():
        if not split:
            return [pltpu.make_async_copy(stage_up.at[0], keep_hbm.at[steps], out_sem.at[0, 0])]
        at = pl.ds(2 * steps * r, r)
        return [
            pltpu.make_async_copy(stage_up.at[0, s], dest.at[:, at, :], out_sem.at[0, s])
            for s, dest in enumerate((keep_hbm, send_hbm))
        ]

    def put(stage, slot, value, owners):
        if not split:
            stage[slot] = value.astype(bf16)
            return
        keep, send = split_cores(value, core, owners)
        stage[slot, 0] = keep.astype(bf16)
        stage[slot, 1] = send.astype(bf16)

    @pl.when(j == 0)
    def _():
        first, later = ffn_copies(idx_ref, pieces, wo, up, down, sem)
        for c in first + later:
            c.start()
        for c in first:
            c.wait()
        for i in range(tiles):
            rs = pl.ds(i * TILE, TILE)
            start = x_ref[rs, :].astype(f32) + t_ref[rs, :] * vec_ref[0:1, :]
            middle = start + dot(att_ref[rs, :], wo[...]) + vec_ref[1:2, :]
            mid[rs, :] = middle
            acc[rs, :] = middle + vec_ref[4:5, :]
            gn2[rs, :] = jnp.zeros((TILE, width), f32)
            normed = (ln_parts(middle)[0] * vec_ref[2:3, :] + vec_ref[3:4, :]).astype(bf16)
            n2[rs, :] = normed
        for c in later:
            c.wait()

    @pl.when(j > 1)
    def _():
        for c in moves(j - 2):
            c.wait()

    f0 = pl.multiple_of(j * fc, fc)
    up_c = up[:, pl.ds(f0, fc)]
    down_c = down[pl.ds(f0, fc), :]
    upb = upb_ref[...]
    gb = jnp.zeros((1, fc), f32)
    ahead = []

    def enter(i):
        rs = pl.ds(i * TILE, TILE)
        ahead.append((dot(n2[rs, :], up_c), dot(cot_ref[rs, :], down_c, NT)))

    enter(0)
    for i in range(tiles):
        rs = pl.ds(i * TILE, TILE)
        if i + 1 < tiles:
            enter(i + 1)
        pre, gh = ahead[i]
        h, slope = gelu_parts(pre + upb)
        h = h.astype(bf16)
        g = (gh * slope).astype(bf16)
        hid[rs, :] = h
        gp[rs, :] = g
        gb = gb + rows_sum(g.astype(f32))
        acc[rs, :] += dot(h, down_c)
        gn2[rs, :] += dot(g, up_c, NT)
    gvec_ref[pl.ds(4 + j, 1), :] = gb
    slot = lax.rem(j, 2)
    put(stage_down, slot, dot(hid[...], cot_ref[...], TN), 2 * (fc // (2 * steps * r)) if split else 0)
    put(stage_up, slot, dot(n2[...], gp[...], TN), split)
    for c in moves(j):
        c.start()

    @pl.when(j == steps - 1)
    def _():
        sums = [jnp.zeros((1, width), f32)] * 4
        for i in range(tiles):
            rs = pl.ds(i * TILE, TILE)
            out_ref[rs, :] = acc[rs, :].astype(bf16)
            xhat, rstd = ln_parts(mid[rs, :])
            dn = gn2[rs, :]
            cot = cot_ref[rs, :].astype(f32)
            gm = cot + ln_back(xhat, rstd, dn, vec_ref[2:3, :])
            mid[rs, :] = gm
            ga = gm.astype(bf16)
            hid[rs, :] = ga
            ga_ref[rs, :] = dot(ga, wo[...], NT).astype(bf16)
            sums = [s + rows_sum(v) for s, v in zip(sums, (dn * xhat, dn, cot, ga.astype(f32)))]
        gvec_ref[0:4, :] = jnp.concatenate(sums, axis=0)
        mid_copy = pltpu.make_async_copy(mid, gm_hbm, gm_sem)
        mid_copy.start()
        grad_out = dot(att_ref[...], hid[...], TN)
        for c in moves(j - 1) + moves(j):
            c.wait()
        put(stage_up, 0, grad_out, split)
        last = out_copies()
        for c in last:
            c.start()
        for c in last:
            c.wait()
        mid_copy.wait()


def ffn_both(idx, x, t, att, cot, vecs, upb, pieces, ff, split):
    rows, width = x.shape
    n = len(pieces)
    fc = width
    steps = ff // fc
    sd = jax.ShapeDtypeStruct
    V = pltpu.VMEM
    if split:
        half = split // 2
        r = width // split
        grads = [sd((half, (2 * steps + 1) * r, width), bf16)] * 2
        stages = [V((2, 2, half, r, width), bf16), V((2, 2, fc // (2 * steps * r), steps * r, width), bf16)]
    else:
        grads = [sd((steps + 1, width, width), bf16), sd((ff, width), bf16)]
        stages = [V((2, width, width), bf16)] * 2
    return pl.pallas_call(
        functools.partial(ffn_kernel, n, split, steps),
        grid_spec=pltpu.PrefetchScalarGridSpec(
            num_scalar_prefetch=1,
            grid=(steps,),
            in_specs=[whole_spec((rows, width)), whole_spec((rows, 1)), whole_spec((rows, width)), whole_spec((rows, width)),
                      whole_spec(vecs.shape), pl.BlockSpec((1, fc), lambda j, *_: (0, j))] + [any_spec()] * n,
            out_specs=[whole_spec((rows, width)), whole_spec((rows, width)), whole_spec((4 + steps, width)),
                       any_spec(), any_spec(), any_spec()],
            scratch_shapes=[V((width, width), bf16), V((width, ff), bf16), V((ff, width), bf16),
                            V((rows, width), f32), V((rows, width), bf16),
                            V((rows, width), f32), V((rows, width), f32),
                            V((rows, fc), bf16), V((rows, fc), bf16), *stages,
                            pltpu.SemaphoreType.DMA((6 * n,)), pltpu.SemaphoreType.DMA((2, 4)), pltpu.SemaphoreType.DMA],
        ),
        out_shape=[sd((rows, width), bf16), sd((rows, width), bf16), sd((4 + steps, width), f32),
                   sd((rows, width), f32), *grads],
        compiler_params=params(),
        cost_estimate=cost(60),
        name="ffn_both",
    )(idx, x, t, att, cot, vecs, upb, *pieces)


def gqkv_kernel(split, idx_ref, normed_ref, gp_ref, *rest):
    outs, nt = rest[:-1], rest[-1]

    @pl.when(pl.program_id(0) == 0)
    def _():
        nt[...] = normed_ref[...].T

    grad = dot(nt[...], gp_ref[...])
    if split:
        keep, send = split_cores(grad, lax.rem(idx_ref[0], 2), split)
        outs[0][...] = keep.astype(bf16)
        outs[1][...] = send.astype(bf16)
    else:
        outs[0][0] = grad.astype(bf16)


def qkv_weight_grad(idx, normed, gp, split):
    rows, width = normed.shape
    sd = jax.ShapeDtypeStruct
    if split:
        half, r = split // 2, width // split
        out_specs = [pl.BlockSpec((half, r, width), lambda j, *_: (0, j, 0))] * 2
        out_shape = [sd((half, 3 * r, width), bf16)] * 2
    else:
        out_specs = [pl.BlockSpec((1, width, width), lambda j, *_: (j, 0, 0))]
        out_shape = [sd((3, width, width), bf16)]
    return pl.pallas_call(
        functools.partial(gqkv_kernel, split),
        grid_spec=pltpu.PrefetchScalarGridSpec(
            num_scalar_prefetch=1,
            grid=(3,),
            in_specs=[whole_spec((rows, width)), pl.BlockSpec((rows, width), lambda j, *_: (0, j))],
            out_specs=out_specs,
            scratch_shapes=[pltpu.VMEM((width, rows), bf16)],
        ),
        out_shape=out_shape,
        compiler_params=params(),
        cost_estimate=cost(2),
        name="qkv_weight_grad",
    )(idx, normed, gp)


def first_kernel(n, idx_ref, x_ref, t_ref, gm_ref, gp_ref, vec_ref, *rest):
    pieces, (gi_ref, gvec_ref, w_scr, sem) = rest[:n], rest[n:]
    i = pl.program_id(0)
    width = x_ref.shape[1]

    @pl.when(i == 0)
    def _():
        copies = qkv_copies(idx_ref, pieces, w_scr, sem)
        for c in copies:
            c.start()
        gvec_ref[...] = jnp.zeros_like(gvec_ref)
        for c in copies:
            c.wait()

    sums = None
    dns = [dot(gp_ref[rs, :], w_scr[...], NT) for rs in sub_tiles()]
    for rs, dn in zip(sub_tiles(), dns):
        t = t_ref[rs, :]
        start = x_ref[rs, :].astype(f32) + t * vec_ref[0:1, :]
        xhat, rstd = ln_parts(start)
        gs = gm_ref[rs, :] + ln_back(xhat, rstd, dn, vec_ref[1:2, :])
        gi_ref[rs, :] = gs.astype(bf16)
        parts = [t * gs, dn * xhat, dn, gp_ref[rs, :width].astype(f32), gp_ref[rs, 2 * width :].astype(f32)]
        parts = [rows_sum(v) for v in parts]
        sums = parts if sums is None else [a + b for a, b in zip(sums, parts)]
    gvec_ref[...] += jnp.concatenate(sums + [jnp.zeros((3, width), f32)], axis=0)


def first_backward(idx, x, t, gm, gp, vecs, pieces):
    rows, width = x.shape
    n = len(pieces)
    sd = jax.ShapeDtypeStruct
    return pl.pallas_call(
        functools.partial(first_kernel, n),
        grid_spec=pltpu.PrefetchScalarGridSpec(
            num_scalar_prefetch=1,
            grid=(rows // BLOCK,),
            in_specs=[row_spec(width, BLOCK), row_spec(1, BLOCK), row_spec(width, BLOCK), row_spec(3 * width, BLOCK), whole_spec(vecs.shape)] + [any_spec()] * n,
            out_specs=[row_spec(width, BLOCK), whole_spec((8, width))],
            scratch_shapes=[pltpu.VMEM((width, 3 * width), bf16), pltpu.SemaphoreType.DMA((n,))],
        ),
        out_shape=[sd((rows, width), bf16), sd((8, width), f32)],
        compiler_params=params(),
        cost_estimate=cost(3),
        name="first_backward",
    )(idx, x, t, gm, gp, vecs, *pieces)


SHARDS = 8


def swap(value, axis, size, bit_mask):
    return lax.ppermute(value, axis, [(i, i ^ bit_mask) for i in range(size)])


def near(value):
    return swap(value, "fsdp", SHARDS, 1)


def along_x(value):
    return swap(value, "fsdp", SHARDS, 2)


def along_y(value):
    return swap(value, "fsdp", SHARDS, 4)


def with_near(far):
    pieces = []
    for piece in far:
        pieces += [piece, near(piece)]
    return pieces


def in_order(pieces, order):
    stacked = pieces.astype(f32)
    hit = (jnp.arange(stacked.shape[0])[:, None] == order[None, :]).astype(f32)
    return jnp.sum(hit.reshape(hit.shape + (1,) * (stacked.ndim - 1)) * stacked[None], axis=1)


def blocks_of(weight, width):
    r = weight.shape[0]
    return jnp.transpose(weight.reshape(r, -1, width), (1, 0, 2)).reshape(-1, width)


def add_low(*terms):
    total = terms[0].astype(f32)
    for term in terms[1:]:
        total = total + term.astype(f32)
    return total.astype(terms[0].dtype)


def place_rows(arrays, spot, mask, rows):
    return [lax.dynamic_index_in_dim(v, (spot // 2) ^ mask, 0, keepdims=False)[rows] for v in arrays]


def cut_of(arrays):
    cut = arrays[0].shape[1] // 32 * 16
    return slice(None, cut), slice(cut, None)


def far_first(arrays, spot):
    top, low = cut_of(arrays)
    total = lambda mask, rows: add_low(*place_rows(arrays, spot, mask, rows))
    return jnp.stack([total(1, top), total(3, top)]), jnp.stack([total(2, low), total(3, low)])


def far_second(arrays, from_x, from_y, spot):
    top, low = cut_of(arrays)
    total = lambda mask, rows, more: add_low(*place_rows(arrays, spot, mask, rows), more)
    return total(2, top, from_x[1]), total(1, low, from_y[1])


def far_third(arrays, from_x, from_y, last_y, last_x, spot):
    top, low = cut_of(arrays)
    total = lambda rows, *more: add_low(*place_rows(arrays, spot, 0, rows), *more)
    return total(top, from_x[0], last_y), total(low, from_y[0], last_x)


def halves(owned, spot):
    parts = owned.reshape(2, owned.shape[0] // 2, owned.shape[1])
    side = spot % 2
    return (
        lax.dynamic_index_in_dim(parts, side, 0, keepdims=False),
        lax.dynamic_index_in_dim(parts, 1 - side, 0, keepdims=False),
    )


def rows_first(kept, sent, size):
    return add_low(kept, swap(sent, "dp", size, 1))


def rows_middle(half, size):
    step = 2
    while step < size:
        half = add_low(half, swap(half, "dp", size, step))
        step *= 2
    return half


def rows_last(half, size, spot):
    other = swap(half, "dp", size, 1)
    even = spot % 2 == 0
    return jnp.concatenate([jnp.where(even, half, other), jnp.where(even, other, half)]).astype(f32)


def sum_owned(packed, tied, spot, size):
    if size != SHARDS:
        return lax.psum_scatter(packed, "fsdp", scatter_dimension=0)
    total = lax.dynamic_index_in_dim(packed, spot, 0, keepdims=False)
    for m in range(1, size):
        source = packed if m <= size // 2 else tied
        total = total + swap(lax.dynamic_index_in_dim(source, spot ^ m, 0, keepdims=False), "fsdp", size, m)
    return total


def sum_planes(value, size):
    terms = [value] + [swap(value, "dp", size, m) for m in range(1, size)]
    while len(terms) > 1:
        terms = [a + b for a, b in zip(terms[::2], terms[1::2])]
    return terms[0]


def on_device(
    sizes,
    inputs,
    time_of_row,
    coords,
    segment_ids,
    cotangent,
    time_weight,
    ln1_gain,
    ln1_bias,
    w_qkv,
    q_bias,
    v_bias,
    w_out,
    out_bias,
    kernel_mean,
    kernel_width,
    kernel_map,
    ln2_gain,
    ln2_bias,
    w_up,
    up_bias,
    w_down,
    down_bias,
):
    n, planes = sizes
    direct = n == SHARDS
    split = n if direct else 0
    barrier = lax.optimization_barrier
    spot = lax.axis_index("fsdp")
    level = lax.axis_index("dp")
    order = (spot ^ jnp.arange(n)).astype(jnp.int32)
    width = inputs.shape[1]
    r = w_qkv.shape[0]
    heads = kernel_map.shape[1]
    own_kernels = kernel_map.shape[0]
    kernels = own_kernels * n
    wide = up_bias.shape[0] // r
    ff = n * wide * r
    scale = (width // heads) ** (-0.5)
    times = time_of_row[:, None]

    vectors = (time_weight, ln1_gain, ln1_bias, q_bias, v_bias, out_bias, ln2_gain, ln2_bias, down_bias)
    if direct:
        lanes = 128
        pieces = [v[None] for v in vectors] + [up_bias.reshape(-1, lanes), kernel_mean[None], kernel_width[None], kernel_map]
        small = sum(
            jnp.pad(v, ((at, 32 - at - v.shape[0]), (0, lanes - v.shape[1])))
            for at, v in zip((*range(9), 9, 12, 13, 16), pieces)
        )
        pair = jnp.stack([small, near(small)])
        pair, w_first, w_second, coords, segment_ids, times = barrier(
            (pair, w_qkv, (w_out, w_up, w_down), coords, segment_ids, times)
        )
        small_far = [swap(pair, "fsdp", n, 2 * m) for m in range(1, n // 2)]
        qkv_far = [w_first] + [swap(w_first, "fsdp", n, 2 * m) for m in range(1, n // 2)]
        second = jnp.concatenate([w_second[0], blocks_of(w_second[1], width), w_second[2]])
        small_all = in_order(jnp.concatenate([pair] + small_far), order)
        vectors, up_bias_all = small_all[:, :9, :r], small_all[:, 9:12].reshape(1, ff)
        mean_all, width_all = (small_all[:, at, :own_kernels].reshape(kernels) for at in (12, 13))
        map_all = small_all[:, 16 : 16 + own_kernels, :heads].reshape(kernels, heads)
    else:
        gathered = lambda v: lax.all_gather(v, "fsdp", axis=0, tiled=True).astype(f32)
        vectors = lax.all_gather(jnp.stack(vectors), "fsdp", axis=0).astype(f32)
        up_bias_all, map_all = gathered(up_bias)[None], gathered(kernel_map)
        mean_all, width_all = gathered(kernel_mean), gathered(kernel_width)
        qkv_p = (lax.all_gather(w_qkv, "fsdp", axis=0, tiled=True),)
        ffn_p = tuple(lax.all_gather(w, "fsdp", axis=0, tiled=True) for w in (w_out, w_up, w_down))

    aux_win, aux_col = aux_of(coords, segment_ids)
    gmat, amat, kernel_columns = kernel_consts(mean_all, width_all, map_all.astype(bf16))
    done = attn_bias(0, aux_win, aux_col, gmat, amat, ())
    if direct:
        done, second, qkv_far = barrier((done, second, qkv_far))
        qkv_p = tuple(with_near(qkv_far))
        from_x, from_y = along_x(second), along_y(second)
    bias, feats = attn_bias(1, aux_win, aux_col, gmat, amat, done)
    vecs = jnp.transpose(vectors, (1, 0, 2)).reshape(9, width)

    def rows_of(*picked):
        return jnp.concatenate([vecs[p : p + 1] for p in picked] + [jnp.zeros((8 - len(picked), width), f32)])

    first_rows, ffn_rows, back_rows = rows_of(0, 1, 2, 3, 4), rows_of(0, 5, 6, 7, 8), rows_of(0, 1)
    if direct:
        bias, qkv_p, ready = barrier((bias, qkv_p, (first_rows, ffn_rows, back_rows, up_bias_all, amat, kernel_columns)))
        first_rows, ffn_rows, back_rows, up_bias_all, amat, kernel_columns = ready
    normed, queries, keys, values = qkv_forward(order, inputs, times, first_rows, qkv_p, scale)
    if direct:
        cut = (1 + wide) * r
        queries, from_x, from_y = barrier((queries, from_x, from_y))
        top_d, low_d = along_y(from_x[:cut]), along_x(from_y[cut:])
        ffn_p = with_near((second, from_x, from_y))
    attended, probs = attn_fwd(0, queries, keys, values, bias, ())
    if direct:
        attended, top_d, low_d, ffn_p = barrier((attended, top_d, low_d, ffn_p))
        ffn_p = tuple(ffn_p + with_near((top_d, low_d)))

    output, grad_attended, ffn_vecs, grad_middle, ffn_keep, ffn_send = ffn_both(
        order, inputs, times, attended, cotangent, ffn_rows, up_bias_all, ffn_p, ff, split
    )
    up_rows = wide * r

    def backward(part, before):
        return attn_bwd(part, queries, grad_attended, keys, values, probs, scale, before)

    def feat(part, before):
        return attn_feat(part, grad_scores, feats, aux_win, aux_col, amat, kernel_columns, before)

    def scattered(array, blocks):
        owned = lax.psum_scatter(array.reshape(blocks, n, -1, width), "fsdp", scatter_dimension=1)
        return owned.reshape(-1, width)

    if direct:
        a = (ffn_keep, near(ffn_send))
        done = backward(0, ())
        done, go_x, go_y = barrier((done, *far_first(a, spot)))
        from_x, from_y = along_x(go_x), along_y(go_y)
        grad_projected, grad_scores = backward(3, backward(2, backward(1, done)))
        qkv_keep, qkv_send = qkv_weight_grad(order, normed, grad_projected, split)
        a_from = from_x, from_y
        qkv_keep, qkv_send, (go_y, go_x) = barrier((qkv_keep, qkv_send, far_second(a, *a_from, spot)))
        a_last = along_y(go_y), along_x(go_x)
        c = (qkv_keep, near(qkv_send))
    else:
        grad_projected, grad_scores = backward(3, backward(2, backward(1, backward(0, ()))))
        a = scattered(ffn_keep[:wide], wide)
        b = jnp.concatenate([scattered(ffn_send, 1), scattered(ffn_keep[wide:], 1)])
        qkv_owned = scattered(qkv_weight_grad(order, normed, grad_projected, split)[0], 3)
    grad_inputs, first_vecs = first_backward(
        order, inputs, times, grad_middle, grad_projected, back_rows, qkv_p
    )
    if direct:
        top, low = far_third(a, *a_from, *a_last, spot)
        a, b = top[:up_rows], jnp.concatenate([top[up_rows:], low])
        a, b = halves(a, level), halves(b, level)
        a, b, c = barrier((a, b, c))
        c_go = far_first(c, spot)
        grad_scores, first_vecs, c_go = barrier((grad_scores, first_vecs, c_go))
        c_from = along_x(c_go[0]), along_y(c_go[1])
    else:
        a, b = halves(a, level), halves(b, level)
    a, b = rows_first(*a, planes), rows_first(*b, planes)
    sums = feat(0, ())
    if direct:
        sums, a, (go_y, go_x) = barrier((sums, a, far_second(c, *c_from, spot)))
        c_last = along_y(go_y), along_x(go_x)
    a = rows_middle(a, planes)
    sums = feat(1, sums)
    if direct:
        qkv_owned = jnp.concatenate(far_third(c, *c_from, *c_last, spot))
    sums, a, b, c = barrier((sums, a, b, halves(qkv_owned, level)))
    c = rows_first(*c, planes)
    b = rows_middle(b, planes)
    sums = feat(2, sums)
    sums, c = barrier((sums, c))
    c = rows_middle(c, planes)
    grad_up = rows_last(a, planes, level)
    kernel_part = feat(3, sums)[2].reshape(n, own_kernels, -1)

    lanes = kernel_part.shape[2]
    grad_rows = jnp.concatenate([first_vecs[:5], ffn_vecs[3:4], ffn_vecs[:3]]).reshape(9, n, r)
    grad_rows = jnp.pad(jnp.transpose(grad_rows, (1, 0, 2)), ((0, 0), (0, 0), (0, lanes - r)))
    up_bias_rows = ffn_vecs[4:].reshape(n, -1)
    up_bias_rows = jnp.pad(up_bias_rows, ((0, 0), (0, -up_bias_rows.shape[1] % lanes))).reshape(n, -1, lanes)
    vector_rows = jnp.concatenate([grad_rows, up_bias_rows], axis=1)
    packed = jnp.concatenate([kernel_part, vector_rows], axis=1)
    tied, b, c = barrier((packed, b, c))
    grad_low, grad_qkv = rows_last(b, planes, level), rows_last(c, planes, level)
    small = sum_owned(packed, tied, spot, n)
    small, grad_up, grad_low, grad_qkv = barrier((small, grad_up, grad_low, grad_qkv))
    small = sum_planes(small, planes)
    gaussians, vectors = small[:own_kernels], small[own_kernels : own_kernels + 9, :r]
    grad_up_bias = small[own_kernels + 9 :].reshape(-1)[:up_rows]
    grad_down, grad_out = grad_low[:up_rows], grad_low[up_rows:]

    def columns(array):
        return jnp.transpose(array.reshape(-1, r, width), (1, 0, 2)).reshape(r, -1)

    return (
        output,
        grad_inputs,
        vectors[0],
        vectors[1],
        vectors[2],
        columns(grad_qkv),
        vectors[3],
        vectors[4],
        grad_out.astype(f32),
        vectors[5],
        gaussians[:, heads],
        gaussians[:, heads + 1],
        gaussians[:, :heads],
        vectors[6],
        vectors[7],
        columns(grad_up).astype(f32),
        grad_up_bias,
        grad_down.astype(f32),
        vectors[8],
    )


def solution(mesh):
    rows, split, whole = P(("fsdp", "dp"), None), P("fsdp"), P("fsdp", None)
    placed = (
        rows,
        P(("fsdp", "dp")),
        P(None, ("fsdp", "dp")),
        P(("fsdp", "dp")),
        rows,
        split,
        split,
        split,
        whole,
        split,
        split,
        whole,
        split,
        split,
        split,
        whole,
        split,
        split,
        whole,
        split,
        whole,
        split,
    )
    out_placed = (
        rows,
        rows,
        split,
        split,
        split,
        whole,
        split,
        split,
        whole,
        split,
        split,
        split,
        whole,
        split,
        split,
        whole,
        split,
        whole,
        split,
    )
    return jax.shard_map(
        functools.partial(on_device, (mesh.shape["fsdp"], mesh.shape["dp"])),
        mesh=mesh,
        in_specs=placed,
        out_specs=out_placed,
        check_vma=False,
    )
```
